128 devices in a mesh: blk: 32 (over z, y, x_lo), val: 4 (over x_hi, core).
Axes of the slice: x: 4 (x_hi: 2, x_lo: 2; x = x_hi * 2 + x_lo), y: 4, z: 4, core: 2. Of those that a mesh axis runs over, the one named last changes fastest.
Arguments:
- data_rows: bfloat16 [8192, 4096], P('blk', 'val')
- noise_rows: bfloat16 [8192, 4096], P('blk', 'val')
Outputs:
- targets: bfloat16 [8192, 4096], P('blk', 'val')
All inputs are finite; a program needn't handle non-finite values.
Results may differ from the reference program's by a relative error of at most 0.0048.
Values may be sent and summed in bfloat16 or wider, within the bound.
No kernel may reach another device: no remote copies, remote signals or barrier semaphores. Data moves between devices by JAX's collectives and lax.ppermute only.
A program may use at most 128 MiB of HBM per device.

```python
import math
import jax
import jax.numpy as jnp
from jax import lax

D = 4096
ITERS = 2
TOKENS = 8192


def latent_rows(key):
    values = jax.random.normal(key, (TOKENS, D), jnp.float32)
    return jnp.clip(values, -6.0, 6.0).astype(jnp.bfloat16)


def draw_data_rows(key, part):
    key = jax.random.fold_in(key, 1)
    return latent_rows(key)


def draw_noise_rows(key, part):
    key = jax.random.fold_in(key, 2)
    return latent_rows(key)


def setup_inputs(seed: int = 0) -> dict:
    keys = jax.random.split(jax.random.key(seed), 3)
    data_rows = draw_data_rows(jax.random.fold_in(keys[2], 71), 0)
    noise_rows = draw_noise_rows(jax.random.fold_in(keys[2], 71), 0)
    return dict(data_rows=data_rows, noise_rows=noise_rows)


def reference(data_rows, noise_rows):
    width = data_rows.shape[1]
    count = noise_rows.shape[0]
    eps = 0.64 / math.sqrt(width)
    data_f = data_rows.astype(jnp.float32)
    noise_f = noise_rows.astype(jnp.float32)
    data_sq = lax.optimization_barrier(jnp.sum(data_f * data_f, axis=1))
    noise_sq = lax.optimization_barrier(jnp.sum(noise_f * noise_f, axis=1))
    cross = jnp.dot(data_rows, noise_rows.T, preferred_element_type=jnp.float32)
    cost = (data_sq[:, None] + noise_sq[None, :] - 2.0 * cross) / width
    log_count = math.log(count)
    col_pot = jnp.zeros((count,), jnp.float32)
    for step in range(ITERS):
        row_pot = -eps * log_count - eps * jax.nn.logsumexp((col_pot[None, :] - cost) / eps, axis=1)
        col_pot = -eps * log_count - eps * jax.nn.logsumexp((row_pot[:, None] - cost) / eps, axis=0)
    weights = jax.nn.softmax((col_pot[None, :] - cost) / eps, axis=1).astype(jnp.bfloat16)
    return jnp.dot(weights, noise_rows, preferred_element_type=jnp.float32).astype(jnp.bfloat16)
```

```python
import functools
import itertools
import math

import jax
import jax.numpy as jnp
from jax import lax
from jax.experimental import pallas as pl
from jax.experimental.pallas import tpu as pltpu
from jax.sharding import Mesh, PartitionSpec as P

AXES = ("z", "y", "l", "h", "c")
SIZES = (4, 4, 2, 2, 2)


def index_of(*place):
    index = 0
    for n, a in zip(SIZES, place):
        index = index * n + a % n
    return index


def move(value, dest):
    places = itertools.product(*(range(n) for n in SIZES))
    pairs = [(index_of(*place), index_of(*dest(*place))) for place in places]
    return lax.ppermute(value, AXES, pairs)


def from_y(value, k):
    return move(value, lambda z, y, l, h, c: (z, y - k, l, h, c))


def from_z(value, k):
    return move(value, lambda z, y, l, h, c: (z - k, y, l, h, c))


def flip(value, names):
    return move(
        value,
        lambda *place: [1 - a if name in names else a for name, a in zip(AXES, place)],
    )


def cross(a, b):
    return lax.dot_general(a, b, (((1,), (1,)), ((), ())), preferred_element_type=jnp.float32)


def dot(a, b):
    return jnp.dot(a, b, preferred_element_type=jnp.float32)


def exact_terms(total):
    terms = []
    for _ in range(3):
        terms.append(total.astype(jnp.bfloat16))
        total = total - terms[-1].astype(jnp.float32)
    return terms


def flat(blocks):
    return blocks.reshape(-1, blocks.shape[-1])


def half_squares(rows):
    sums = 0.0
    for at in range(0, rows.shape[1], 128):
        wide = rows[:, at : at + 128].astype(jnp.float32)
        sums = sums + wide * wide
    ones = jnp.full((16, 128), 0.5, jnp.bfloat16)
    return sum(cross(ones, term) for term in exact_terms(sums))[:1]


def call(kernel, outs, flops, *args, anywhere=0, spaces=None, scratch=()):
    moved = sum(a.size * a.dtype.itemsize for a in (*args, *outs))
    inner = len(args) - 1 - anywhere
    return pl.pallas_call(
        kernel,
        out_shape=outs,
        in_specs=[pl.BlockSpec(memory_space=pltpu.SMEM)]
        + [pl.BlockSpec(memory_space=pltpu.VMEM)] * inner
        + [pl.BlockSpec(memory_space=pl.ANY)] * anywhere,
        out_specs=[pl.BlockSpec(memory_space=spaces or pltpu.VMEM)] * len(outs),
        scratch_shapes=scratch,
        compiler_params=pltpu.CompilerParams(vmem_limit_bytes=20 * 2**20),
        cost_estimate=pl.CostEstimate(flops=flops, bytes_accessed=moved, transcendentals=0),
    )(*args)


def started(sems, *pairs):
    copies = [pltpu.make_async_copy(a, b, sems.at[n]) for n, (a, b) in enumerate(pairs)]
    for copy in copies:
        copy.start()
    return copies


def terms_in_rows(vec):
    row = lax.broadcasted_iota(jnp.int32, (16, vec.shape[1]), 0)
    terms = jnp.zeros(row.shape, jnp.float32)
    for n, term in enumerate(exact_terms(vec)):
        terms = jnp.where(row == n, term.astype(jnp.float32), terms)
    return terms.astype(jnp.bfloat16)


def to_rows(terms):
    ones = jnp.ones((terms.shape[0], 128), jnp.bfloat16)
    return lax.dot_general(
        terms, ones, (((0,), (0,)), ((), ())), preferred_element_type=jnp.float32
    )


def lane_sums(values):
    ones = jnp.ones((16, 128), jnp.bfloat16)
    return sum(cross(ones, term) for term in exact_terms(values))[:1]


def first_lanes(values):
    lane = lax.broadcasted_iota(jnp.int32, (16, 128), 1)
    pick = jnp.where(lane == 0, 1.0, 0.0).astype(jnp.bfloat16)
    return sum(cross(pick, term) for term in exact_terms(values))[:1]


def log_sum_exp(values):
    top = functools.reduce(jnp.maximum, values)
    return top + jnp.log(sum(jnp.exp(v - top) for v in values))


def stack_kernel(at, *refs):
    *blocks, out, sems = refs
    copies = started(sems, *((block, out.at[n]) for n, block in enumerate(blocks)))
    for copy in copies:
        copy.wait()


def halves_kernel(at, next_, last, low, high, sems):
    for copy in started(sems, (next_.at[:2], low), (last.at[2:], high)):
        copy.wait()


def near_place(at, k, r):
    return lax.rem(at[0] + k - 2 * at[4] + 4, 4), lax.rem(at[1] + r, 4)


def far_place(at, k, r):
    return lax.rem(at[0] + r - 2 * at[4] + 4, 4), lax.rem(at[1] + k, 4)


def first_kernel(at, *refs):
    data, noises, (out, x, held, sems) = refs[:4], refs[4:10], refs[10:]
    rows = data[0].shape[0]
    own, other = (pl.ds(pl.multiple_of(r * rows, rows), rows) for r in (at[2], 1 - at[2]))
    places = x.at[0, own], x.at[0, other], x.at[1, own], x.at[1, other]
    copies = started(
        sems, *zip(data, places), *((noise, held.at[n]) for n, noise in enumerate(noises))
    )
    for copy in copies[:4]:
        copy.wait()
    x_sq = 0.0
    for side in range(2):
        for span in range(0, x.shape[2], 128):
            wide = x[side, :, span : span + 128].astype(jnp.float32)
            x_sq = x_sq + wide * wide
    x_sq = jnp.broadcast_to(0.5 * jnp.sum(x_sq, axis=1, keepdims=True), x_sq.shape)
    for n, k in enumerate((0, 1, 3)):
        copies[4 + n].wait()
        for r in (0, 2):
            noise = flat(held[n, r : r + 2])
            value = cross(x[0], noise) - half_squares(noise)
            out[near_place(at, k, r)] = value[:, :128] - x_sq
            out[near_place(at, k, r + 1)] = value[:, 128:] - x_sq
    for r in range(4):
        out[near_place(at, 2, r)] = -x_sq
    for n, k in enumerate((0, 1, 3)):
        copies[7 + n].wait()
        for r in (0, 2):
            noise = flat(held[3 + n, r : r + 2])
            value = cross(x[1], noise) - half_squares(noise)
            out[far_place(at, k, r)] += value[:, :128]
            out[far_place(at, k, r + 1)] += value[:, 128:]


def second_kernel(half, at, x, acc, n_a, n_b, f_a, f_b, out, held, sems):
    copies = started(sems, *((p, held.at[n]) for n, p in enumerate((n_a, n_b, f_a, f_b))))
    for block in range(2):
        for j in range(4):
            out[block, j] = acc[2 * half + block, j]
    for copy in copies:
        copy.wait()
    block, _ = near_place(at, 2, 0)

    @pl.when((block >= 2) == bool(half))
    def _():
        for n, r in ((0, 0), (1, 2)):
            noise = flat(held[n])
            value = cross(x[0], noise) - half_squares(noise)
            out[block - 2 * half, near_place(at, 2, r)[1]] += value[:, :128]
            out[block - 2 * half, near_place(at, 2, r + 1)[1]] += value[:, 128:]

    for block in range(2):
        r = lax.rem(2 * at[4] + 2 * half + block - at[0] + 4, 4)
        j = far_place(at, 2, 0)[1]
        noise = held[2 + r // 2, lax.rem(r, 2)]
        out[block, j] += cross(x[1], noise) - half_squares(noise)


def weights_of(at, weights, place, own_rows):
    rows = weights.shape[2] // 2
    to_l = at[2] if own_rows else 1 - at[2]
    here = pl.ds(pl.multiple_of(to_l * rows, rows), rows)
    parts = []
    for k, rs in ((0, range(4)), (1, range(4)), (3, range(4)), (2, (0, 1)), (2, (2, 3))):
        blocks = [place(at, k, r) for r in rs]
        parts.append(
            jnp.concatenate([weights[block[0], block[1], here] for block in blocks], axis=1)
        )
    total = 0.0
    for value in parts:
        total = total + cross(jnp.ones((16, value.shape[1]), jnp.bfloat16), value)
    return parts, total[:1]


STEP = 256


def product(parts, noise, first):
    span = slice(first, first + STEP)
    return sum(dot(w, flat(p[:, :, span])) for w, p in zip(parts, noise))


def target_1_kernel(at, weights, p0, p1, p3, p2_a, p2_b, low, high):
    parts, total = weights_of(at, weights, far_place, True)
    mid = low.shape[0] - 16
    for first in range(0, p0.shape[-1], STEP):
        value = product(parts, (p0, p1, p3, p2_a, p2_b), first)
        low[:mid, first : first + STEP] = value[:mid].astype(low.dtype)
        high[:mid, first : first + STEP] = value[mid:].astype(high.dtype)
    for n, out in enumerate((low, high)):
        out[mid:, :] = jnp.zeros((16, out.shape[1]), out.dtype)
        out[mid:, :mid] = terms_in_rows(total[:, n * mid : n * mid + mid])


def target_2_kernel(place, own_rows, at, weights, p0, p1, p3, p2_a, p2_b, out, row_total):
    parts, total = weights_of(at, weights, place, own_rows)
    for first in range(0, p0.shape[-1], STEP):
        out[:, first : first + STEP] = product(parts, (p0, p1, p3, p2_a, p2_b), first)
    row_total[...] = jnp.broadcast_to(total, row_total.shape)


def add_kernel(part, at, values, row_total, came, out):
    mid = came.shape[0] - 16
    here = slice(part * mid, part * mid + mid)
    there = slice(mid - part * mid, 2 * mid - part * mid)
    out[here] = (values[here] + came[:mid].astype(jnp.float32)).astype(out.dtype)
    out[there] = values[there].astype(out.dtype)
    terms = came[mid:, :mid].astype(jnp.float32)
    total = [row_total[:1, :mid], row_total[:1, mid:]]
    total[part] = total[part] + terms[0:1] + terms[1:2] + terms[2:3]
    out[2 * mid :, :] = jnp.zeros((16, out.shape[1]), out.dtype)
    out[2 * mid :, : 2 * mid] = terms_in_rows(jnp.concatenate(total, axis=1))


def last_kernel(at, own, own_total, a, b, out):
    rows = own.shape[0]
    terms = [terms_in_rows(own_total[:1])] + [m[rows:, :rows] for m in (a, b)]
    total = to_rows(jnp.concatenate(terms, axis=0))
    for column in range(0, own.shape[1], 128):
        span = slice(column, column + 128)
        value = own[:, span]
        for m in (a, b):
            value = value + m[:rows, span].astype(jnp.float32)
        out[:, span] = (value / total).astype(out.dtype)


TILE = 64


def rows_1_kernel(scale, at, keep, got, score, sent, tops, sums):
    blocks = keep.shape[0]

    @pl.loop(0, keep.shape[1] // TILE)
    def _(t):
        here = pl.ds(pl.multiple_of(t * TILE, TILE), TILE)
        top = None
        for b in range(blocks):
            value = (keep[b, here] + got[b, here]) * scale
            score[b, here] = value
            top = value if top is None else jnp.maximum(top, value)
        top = jnp.broadcast_to(jnp.max(top, axis=1, keepdims=True), top.shape)
        tops[here] = top
        sums[here] = sum(jnp.exp(score[b, here] - top) for b in range(blocks))

    log_row = first_lanes(tops[...]) + jnp.log(lane_sums(sums[...]))
    for n in range(sent.shape[0]):
        sent[n] = log_row


def columns_1_kernel(log_count, at, came, score, row_pot, sent):
    pot = -log_count - log_sum_exp([came[n] for n in range(came.shape[0])])
    row_pot[...] = to_rows(terms_in_rows(pot))
    logs = []
    for b in range(score.shape[0]):
        value = score[b] + row_pot[...]
        top = jnp.max(value, axis=0, keepdims=True)
        total = jnp.sum(jnp.exp(value - top), axis=0, keepdims=True)
        logs.append(top + jnp.log(total))
    logs = jnp.concatenate(logs)
    for n in range(sent.shape[0]):
        sent[n] = logs


def rows_2_kernel(at, came, score, row_pot, plan, sent, sums):
    pot = -log_sum_exp([came[n] for n in range(came.shape[0])])

    @pl.loop(0, score.shape[1] // TILE)
    def _(t):
        here = pl.ds(pl.multiple_of(t * TILE, TILE), TILE)
        total = 0.0
        for b in range(score.shape[0]):
            value = score[b, here] + row_pot[here] + pot[b : b + 1]
            value = jnp.exp(jnp.minimum(value, 0.0))
            plan[b, here] = value
            total = total + value
        sums[here] = total

    row_sum = lane_sums(sums[...])
    for n in range(sent.shape[0]):
        sent[n] = row_sum


def columns_2_kernel(least, at, came, plan, row_scale, sent):
    total = sum(came[n] for n in range(came.shape[0]))
    row_scale[...] = to_rows(terms_in_rows(1.0 / jnp.maximum(total, least)))
    sums = []
    for b in range(plan.shape[0]):
        sums.append(jnp.sum(plan[b] * row_scale[...], axis=0, keepdims=True))
    sums = jnp.concatenate(sums)
    for n in range(sent.shape[0]):
        sent[n] = sums


def weights_kernel(least, at, came, plan, other, row_scale, weights):
    c = at[4]
    mine = sum(came[2 * n + c] for n in range(came.shape[0] // 2))
    theirs = sum(came[2 * n + 1 - c] for n in range(came.shape[0] // 2))
    for half, (values, total) in enumerate(((plan, mine), (other, theirs))):
        scale = 1.0 / jnp.maximum(total, least)
        for b in range(values.shape[0]):
            value = values[b] * row_scale[...] * scale[b : b + 1]
            weights[values.shape[0] * half + b] = value.astype(weights.dtype)


def per_device(data_rows, noise_rows):
    z, y, l, h, c = (lax.axis_index(name) for name in AXES)
    rows, part = data_rows.shape
    width = part * 4
    count = rows * 32
    eps = 0.64 / math.sqrt(width)
    log_count = math.log(count)
    piece = rows // 4

    def float32(*shape):
        return jax.ShapeDtypeStruct(shape, jnp.float32)

    def bfloat16(*shape):
        return jax.ShapeDtypeStruct(shape, jnp.bfloat16)

    at = jnp.stack([z, y, l, h, c])

    def quarter(to_l, to_h):
        return lax.dynamic_slice_in_dim(noise_rows, (2 * to_h + to_l) * piece, piece)

    wave = lax.optimization_barrier
    near_other, far_own, far_other = wave(
        (
            flip(quarter(1 - l, h), "l"),
            flip(quarter(l, 1 - h), "h"),
            flip(quarter(1 - l, 1 - h), "lh"),
        )
    )
    near = jnp.concatenate([quarter(l, h), near_other])
    far = jnp.concatenate([far_own, far_other])

    data_l = flip(data_rows, "l")
    near_1, near_3, far_1, far_3, data_rows = wave(
        (from_y(near, 1), from_y(near, 3), from_z(far, 1), from_z(far, 3), data_rows)
    )
    data_lh = flip(data_rows, "lh")
    near_2, far_2, data_l, data_rows = wave(
        (from_y(near_1, 1), from_z(far_1, 1), data_l, data_rows)
    )
    sems = pltpu.SemaphoreType.DMA((4,))

    def stacked(*blocks):
        out = [bfloat16(4, *blocks[0].shape)]
        return call(
            stack_kernel, out, 0, at, *blocks, anywhere=4, spaces=pl.ANY, scratch=[sems]
        )[0]

    def halves(next_, last):
        out = [bfloat16(2, *next_.shape[1:])] * 2
        return call(
            halves_kernel, out, 0, at, next_, last, anywhere=2, spaces=pl.ANY, scratch=[sems]
        )

    near, far = stacked(near, near_1, near_2, near_3), stacked(far, far_1, far_2, far_3)
    near_next, near_last = from_z(near, 1), from_z(near, 3)
    far_next, far_last = from_y(far, 1), from_y(far, 3)
    data_h = flip(data_rows, "h")
    near_next, near_last, far_next, far_last, data_lh, data_h = wave(
        (near_next, near_last, far_next, far_last, data_lh, data_h)
    )
    nears, fars = (near, near_next, near_last), (far, far_next, far_last)
    low, high = halves(near_next, near_last)
    near_two = from_z(low, 1), from_z(high, 3)
    low, high = halves(far_next, far_last)
    far_two = from_y(low, 1), from_y(high, 3)

    one = 2 * 2 * rows * part * 2 * 2 * piece
    noise_shape = 4, 2 * piece, part
    scores, x_all = call(
        first_kernel,
        [float32(4, 4, 2 * rows, 2 * piece), bfloat16(2, 2 * rows, part)],
        12 * one,
        *(at, data_rows, data_l, data_h, data_lh, *nears, *fars),
        anywhere=10,
        scratch=[pltpu.VMEM((6, *noise_shape), jnp.bfloat16), pltpu.SemaphoreType.DMA((10,))],
    )
    give, keep = (
        call(
            functools.partial(second_kernel, half),
            [float32(2, 4, 2 * rows, 2 * piece)],
            2 * one,
            *(at, x_all, scores, *near_two, *far_two),
            anywhere=4,
            scratch=[pltpu.VMEM((4, 2, *noise_shape[1:]), jnp.bfloat16), sems],
        )[0]
        for half in (1, 0)
    )

    blocks = (8, 2 * rows, 2 * piece)
    tall = 2 * rows, 2 * piece
    least = 0.5 / count
    row_axes, col_axes = ("l", "h", "c"), ("z", "y")
    row_sent, col_sent = float32(8, 1, 2 * rows), float32(16, 8, 2 * piece)

    def exchange(sent, axes):
        return lax.all_to_all(sent, axes, 0, 0, tiled=True)

    keep, give = keep.reshape(blocks), give.reshape(blocks)
    kernel = functools.partial(rows_1_kernel, 2.0 / (width * eps))
    score, sent = call(
        kernel, [float32(*blocks), row_sent], 0, at, keep, flip(give, "c"), scratch=[pltpu.VMEM(tall, jnp.float32)] * 2
    )
    kernel = functools.partial(columns_1_kernel, log_count)
    row_pot, sent = call(
        kernel, [float32(*tall), col_sent], 0, at, exchange(sent, row_axes), score
    )
    plan, sent = call(
        rows_2_kernel,
        [float32(*blocks), row_sent],
        0,
        *(at, exchange(sent, col_axes), score, row_pot),
        scratch=[pltpu.VMEM(tall, jnp.float32)],
    )
    plan_other = flip(plan, "c")
    kernel = functools.partial(columns_2_kernel, least)
    col_sent = float32(32, 8, 2 * piece)
    row_scale, sent = call(
        kernel, [float32(*tall), col_sent], 0, at, exchange(sent, row_axes), plan
    )
    kernel = functools.partial(weights_kernel, least)
    (weights,) = call(
        kernel,
        [bfloat16(16, *blocks[1:])],
        0,
        *(at, exchange(sent, ("z", "y", "c")), plan, plan_other, row_scale),
    )
    weights = weights.reshape(4, 4, *blocks[1:])

    near_noise, far_noise = (*nears, *near_two), (*fars, *far_two)
    low, high = call(
        target_1_kernel, [bfloat16(rows // 2 + 16, part)] * 2, 8 * one, at, weights, *far_noise
    )
    low, high = flip(low, "l"), flip(high, "lh")

    def target(place, own_rows):
        kernel = functools.partial(target_2_kernel, place, own_rows)
        noise = near_noise if place is near_place else far_noise
        return call(kernel, [float32(rows, part), float32(8, rows)], 8 * one, at, weights, *noise)

    def message(half, came, values, row_total):
        kernel = functools.partial(add_kernel, half)
        return call(kernel, [bfloat16(rows + 16, part)], 0, at, values, row_total, came)[0]

    to_lh = flip(message(0, low, *target(far_place, False)), "lh")
    to_l = flip(message(1, high, *target(near_place, False)), "l")
    own, own_total = target(near_place, True)
    return call(last_kernel, [bfloat16(rows, part)], 0, at, own, own_total, to_l, to_lh)[0]


def solution(mesh):
    fine = Mesh(mesh.devices.reshape(SIZES), AXES)
    spec = P(("z", "y", "l"), ("h", "c"))
    return jax.shard_map(
        per_device, mesh=fine, in_specs=(spec, spec), out_specs=spec, check_vma=False
    )
```

```python
import functools
import itertools
import math

import jax
import jax.numpy as jnp
from jax import lax
from jax.experimental import pallas as pl
from jax.experimental.pallas import tpu as pltpu
from jax.sharding import Mesh, PartitionSpec as P

AXES = ("z", "y", "l", "h", "c")
SIZES = (4, 4, 2, 2, 2)


def index_of(*place):
    index = 0
    for n, a in zip(SIZES, place):
        index = index * n + a % n
    return index


def move(value, dest):
    places = itertools.product(*(range(n) for n in SIZES))
    pairs = [(index_of(*place), index_of(*dest(*place))) for place in places]
    return lax.ppermute(value, AXES, pairs)


def from_y(value, k):
    return move(value, lambda z, y, l, h, c: (z, y - k, l, h, c))


def from_z(value, k):
    return move(value, lambda z, y, l, h, c: (z - k, y, l, h, c))


def flip(value, names):
    return move(
        value,
        lambda *place: [1 - a if name in names else a for name, a in zip(AXES, place)],
    )


def cross(a, b):
    return lax.dot_general(a, b, (((1,), (1,)), ((), ())), preferred_element_type=jnp.float32)


def dot(a, b):
    return jnp.dot(a, b, preferred_element_type=jnp.float32)


def exact_terms(total):
    terms = []
    for _ in range(3):
        terms.append(total.astype(jnp.bfloat16))
        total = total - terms[-1].astype(jnp.float32)
    return terms


def flat(blocks):
    return blocks.reshape(-1, blocks.shape[-1])


def half_squares(rows):
    sums = 0.0
    for at in range(0, rows.shape[1], 128):
        wide = rows[:, at : at + 128].astype(jnp.float32)
        sums = sums + wide * wide
    ones = jnp.full((16, 128), 0.5, jnp.bfloat16)
    return sum(cross(ones, term) for term in exact_terms(sums))[:1]


def call(kernel, outs, flops, *args, anywhere=0, spaces=None, scratch=()):
    moved = sum(a.size * a.dtype.itemsize for a in (*args, *outs))
    inner = len(args) - 1 - anywhere
    return pl.pallas_call(
        kernel,
        out_shape=outs,
        in_specs=[pl.BlockSpec(memory_space=pltpu.SMEM)]
        + [pl.BlockSpec(memory_space=pltpu.VMEM)] * inner
        + [pl.BlockSpec(memory_space=pl.ANY)] * anywhere,
        out_specs=[pl.BlockSpec(memory_space=spaces or pltpu.VMEM)] * len(outs),
        scratch_shapes=scratch,
        compiler_params=pltpu.CompilerParams(vmem_limit_bytes=20 * 2**20),
        cost_estimate=pl.CostEstimate(flops=flops, bytes_accessed=moved, transcendentals=0),
    )(*args)


def started(sems, *pairs):
    copies = [pltpu.make_async_copy(a, b, sems.at[n]) for n, (a, b) in enumerate(pairs)]
    for copy in copies:
        copy.start()
    return copies


def terms_in_rows(vec):
    row = lax.broadcasted_iota(jnp.int32, (16, vec.shape[1]), 0)
    terms = jnp.zeros(row.shape, jnp.float32)
    for n, term in enumerate(exact_terms(vec)):
        terms = jnp.where(row == n, term.astype(jnp.float32), terms)
    return terms.astype(jnp.bfloat16)


def to_rows(terms):
    ones = jnp.ones((terms.shape[0], 128), jnp.bfloat16)
    return lax.dot_general(
        terms, ones, (((0,), (0,)), ((), ())), preferred_element_type=jnp.float32
    )


def lane_sums(values):
    ones = jnp.ones((16, 128), jnp.bfloat16)
    return sum(cross(ones, term) for term in exact_terms(values))[:1]


def first_lanes(values):
    lane = lax.broadcasted_iota(jnp.int32, (16, 128), 1)
    pick = jnp.where(lane == 0, 1.0, 0.0).astype(jnp.bfloat16)
    return sum(cross(pick, term) for term in exact_terms(values))[:1]


def log_sum_exp(values):
    top = functools.reduce(jnp.maximum, values)
    return top + jnp.log(sum(jnp.exp(v - top) for v in values))


def stack_kernel(at, *refs):
    *blocks, out, sems = refs
    copies = started(sems, *((block, out.at[n]) for n, block in enumerate(blocks)))
    for copy in copies:
        copy.wait()


def halves_kernel(at, next_, last, low, high, sems):
    for copy in started(sems, (next_.at[:2], low), (last.at[2:], high)):
        copy.wait()


def split_kernel(at, noise, near, far, sems):
    mid = near.shape[0]
    spans = [pl.ds(pl.multiple_of(n * mid, mid), mid) for n in (at[3], 1 - at[3])]
    copies = started(sems, (noise.at[spans[0]], near), (noise.at[spans[1]], far))
    for copy in copies:
        copy.wait()


def near_place(at, k, r):
    return lax.rem(at[0] + k - 2 * at[4] + 4, 4), lax.rem(at[1] + r, 4)


def far_place(at, k, r):
    return lax.rem(at[0] + r - 2 * at[4] + 4, 4), lax.rem(at[1] + k, 4)


def first_kernel(at, *refs):
    data, noises, (out, x, held, sems) = refs[:4], refs[4:10], refs[10:]
    rows = data[0].shape[0]
    own, other = (pl.ds(pl.multiple_of(r * rows, rows), rows) for r in (at[2], 1 - at[2]))
    places = x.at[0, own], x.at[0, other], x.at[1, own], x.at[1, other]
    copies = started(
        sems, *zip(data, places), *((noise, held.at[n]) for n, noise in enumerate(noises))
    )
    for copy in copies[:4]:
        copy.wait()
    x_sq = 0.0
    for side in range(2):
        for span in range(0, x.shape[2], 128):
            wide = x[side, :, span : span + 128].astype(jnp.float32)
            x_sq = x_sq + wide * wide
    x_sq = jnp.broadcast_to(0.5 * jnp.sum(x_sq, axis=1, keepdims=True), x_sq.shape)
    for n, k in enumerate((0, 1, 3)):
        copies[4 + n].wait()
        for r in (0, 2):
            noise = flat(held[n, r : r + 2])
            value = cross(x[0], noise) - half_squares(noise)
            out[near_place(at, k, r)] = value[:, :128] - x_sq
            out[near_place(at, k, r + 1)] = value[:, 128:] - x_sq
    for r in range(4):
        out[near_place(at, 2, r)] = -x_sq
    for n, k in enumerate((0, 1, 3)):
        copies[7 + n].wait()
        for r in (0, 2):
            noise = flat(held[3 + n, r : r + 2])
            value = cross(x[1], noise) - half_squares(noise)
            out[far_place(at, k, r)] += value[:, :128]
            out[far_place(at, k, r + 1)] += value[:, 128:]


def second_kernel(half, at, x, acc, n_a, n_b, f_a, f_b, out, held, sems):
    copies = started(sems, *((p, held.at[n]) for n, p in enumerate((n_a, n_b, f_a, f_b))))
    for block in range(2):
        for j in range(4):
            out[block, j] = acc[2 * half + block, j]
    for copy in copies:
        copy.wait()
    block, _ = near_place(at, 2, 0)

    @pl.when((block >= 2) == bool(half))
    def _():
        for n, r in ((0, 0), (1, 2)):
            noise = flat(held[n])
            value = cross(x[0], noise) - half_squares(noise)
            out[block - 2 * half, near_place(at, 2, r)[1]] += value[:, :128]
            out[block - 2 * half, near_place(at, 2, r + 1)[1]] += value[:, 128:]

    for block in range(2):
        r = lax.rem(2 * at[4] + 2 * half + block - at[0] + 4, 4)
        j = far_place(at, 2, 0)[1]
        noise = held[2 + r // 2, lax.rem(r, 2)]
        out[block, j] += cross(x[1], noise) - half_squares(noise)


def weights_of(at, weights, place, own_rows):
    rows = weights.shape[2] // 2
    to_l = at[2] if own_rows else 1 - at[2]
    here = pl.ds(pl.multiple_of(to_l * rows, rows), rows)
    parts = []
    for k, rs in ((0, range(4)), (1, range(4)), (3, range(4)), (2, (0, 1)), (2, (2, 3))):
        blocks = [place(at, k, r) for r in rs]
        parts.append(
            jnp.concatenate([weights[block[0], block[1], here] for block in blocks], axis=1)
        )
    total = 0.0
    for value in parts:
        total = total + cross(jnp.ones((16, value.shape[1]), jnp.bfloat16), value)
    return parts, total[:1]


STEP = 256


def product(parts, noise, first):
    span = slice(first, first + STEP)
    return sum(dot(w, flat(p[:, :, span])) for w, p in zip(parts, noise))


def target_1_kernel(at, weights, p0, p1, p3, p2_a, p2_b, low, high):
    parts, total = weights_of(at, weights, far_place, True)
    mid = low.shape[0] - 16
    for first in range(0, p0.shape[-1], STEP):
        value = product(parts, (p0, p1, p3, p2_a, p2_b), first)
        low[:mid, first : first + STEP] = value[:mid].astype(low.dtype)
        high[:mid, first : first + STEP] = value[mid:].astype(high.dtype)
    for n, out in enumerate((low, high)):
        out[mid:, :] = jnp.zeros((16, out.shape[1]), out.dtype)
        out[mid:, :mid] = terms_in_rows(total[:, n * mid : n * mid + mid])


def target_2_kernel(
    place, half, at, weights, p0, p1, p3, p2_a, p2_b, message, values, row_total
):
    parts, total = weights_of(at, weights, place, False)
    mid = values.shape[0]
    kept, sent = (slice(n * mid, n * mid + mid) for n in (half, 1 - half))
    for first in range(0, p0.shape[-1], STEP):
        value = product(parts, (p0, p1, p3, p2_a, p2_b), first)
        message[:mid, first : first + STEP] = value[sent].astype(message.dtype)
        values[:, first : first + STEP] = value[kept]
    message[mid:, :] = jnp.zeros((16, message.shape[1]), message.dtype)
    message[mid:, :mid] = terms_in_rows(total[:, sent])
    row_total[...] = jnp.broadcast_to(total[:, kept], row_total.shape)


def target_3_kernel(at, weights, p0, p1, p3, p2_a, p2_b, values, row_total):
    parts, total = weights_of(at, weights, near_place, True)
    for first in range(0, p0.shape[-1], STEP):
        values[:, first : first + STEP] = product(parts, (p0, p1, p3, p2_a, p2_b), first)
    row_total[...] = jnp.broadcast_to(total, row_total.shape)


def add_kernel(at, values, row_total, came, out):
    mid = values.shape[0]
    out[:mid, :] = (values[...] + came[:mid].astype(jnp.float32)).astype(out.dtype)
    terms = came[mid:, :mid].astype(jnp.float32)
    total = row_total[:1] + terms[0:1] + terms[1:2] + terms[2:3]
    out[mid:, :] = jnp.zeros((16, out.shape[1]), out.dtype)
    out[mid:, :mid] = terms_in_rows(total)


def last_kernel(at, own, own_total, l_low, l_high, lh_low, lh_high, out):
    mid = own.shape[0] // 2
    for n, messages in enumerate(((l_low, lh_low), (l_high, lh_high))):
        here = slice(n * mid, n * mid + mid)
        terms = [terms_in_rows(own_total[:1, here])] + [m[mid:, :mid] for m in messages]
        total = to_rows(jnp.concatenate(terms, axis=0))
        for column in range(0, own.shape[1], 128):
            span = slice(column, column + 128)
            value = own[here, span]
            for m in messages:
                value = value + m[:mid, span].astype(jnp.float32)
            out[here, span] = (value / total).astype(out.dtype)


TILE = 64


def rows_1_kernel(scale, at, keep, got, score, sent, tops, sums):
    blocks = keep.shape[0]

    @pl.loop(0, keep.shape[1] // TILE)
    def _(t):
        here = pl.ds(pl.multiple_of(t * TILE, TILE), TILE)
        top = None
        for b in range(blocks):
            value = (keep[b, here] + got[b, here]) * scale
            score[b, here] = value
            top = value if top is None else jnp.maximum(top, value)
        top = jnp.broadcast_to(jnp.max(top, axis=1, keepdims=True), top.shape)
        tops[here] = top
        sums[here] = sum(jnp.exp(score[b, here] - top) for b in range(blocks))

    log_row = first_lanes(tops[...]) + jnp.log(lane_sums(sums[...]))
    for n in range(sent.shape[0]):
        sent[n] = log_row


def columns_1_kernel(log_count, at, came, score, row_pot, sent):
    pot = -log_count - log_sum_exp([came[n] for n in range(came.shape[0])])
    row_pot[...] = to_rows(terms_in_rows(pot))
    logs = []
    for b in range(score.shape[0]):
        value = score[b] + row_pot[...]
        top = jnp.max(value, axis=0, keepdims=True)
        total = jnp.sum(jnp.exp(value - top), axis=0, keepdims=True)
        logs.append(top + jnp.log(total))
    logs = jnp.concatenate(logs)
    for n in range(sent.shape[0]):
        sent[n] = logs


def rows_2_kernel(at, came, score, row_pot, plan, sent, sums):
    pot = -log_sum_exp([came[n] for n in range(came.shape[0])])

    @pl.loop(0, score.shape[1] // TILE)
    def _(t):
        here = pl.ds(pl.multiple_of(t * TILE, TILE), TILE)
        total = 0.0
        for b in range(score.shape[0]):
            value = score[b, here] + row_pot[here] + pot[b : b + 1]
            value = jnp.exp(jnp.minimum(value, 0.0))
            plan[b, here] = value
            total = total + value
        sums[here] = total

    row_sum = lane_sums(sums[...])
    for n in range(sent.shape[0]):
        sent[n] = row_sum


def columns_2_kernel(least, at, came, plan, row_scale, sent):
    total = sum(came[n] for n in range(came.shape[0]))
    row_scale[...] = to_rows(terms_in_rows(1.0 / jnp.maximum(total, least)))
    sums = []
    for b in range(plan.shape[0]):
        sums.append(jnp.sum(plan[b] * row_scale[...], axis=0, keepdims=True))
    sums = jnp.concatenate(sums)
    for n in range(sent.shape[0]):
        sent[n] = sums


def weights_kernel(least, at, came, plan, other, row_scale, weights):
    c = at[4]
    mine = sum(came[2 * n + c] for n in range(came.shape[0] // 2))
    theirs = sum(came[2 * n + 1 - c] for n in range(came.shape[0] // 2))
    for half, (values, total) in enumerate(((plan, mine), (other, theirs))):
        scale = 1.0 / jnp.maximum(total, least)
        for b in range(values.shape[0]):
            value = values[b] * row_scale[...] * scale[b : b + 1]
            weights[values.shape[0] * half + b] = value.astype(weights.dtype)


def per_device(data_rows, noise_rows):
    z, y, l, h, c = (lax.axis_index(name) for name in AXES)
    rows, part = data_rows.shape
    width = part * 4
    count = rows * 32
    eps = 0.64 / math.sqrt(width)
    log_count = math.log(count)
    piece = rows // 4

    def float32(*shape):
        return jax.ShapeDtypeStruct(shape, jnp.float32)

    def bfloat16(*shape):
        return jax.ShapeDtypeStruct(shape, jnp.bfloat16)

    at = jnp.stack([z, y, l, h, c])

    wave = lax.optimization_barrier
    mid = rows // 2
    sems = pltpu.SemaphoreType.DMA((4,))
    near, far = call(
        split_kernel,
        [bfloat16(mid, part)] * 2,
        0,
        *(at, noise_rows),
        anywhere=1,
        spaces=pl.ANY,
        scratch=[sems],
    )
    far = flip(far, "h")
    near_1, near_2, near_3 = (from_y(near, k) for k in (1, 2, 3))
    near_1, near_2, near_3, far, data_rows = wave((near_1, near_2, near_3, far, data_rows))
    far_1, far_2, far_3 = (from_z(far, k) for k in (1, 2, 3))
    data_l = flip(data_rows, "l")

    def stacked(*blocks):
        out = [bfloat16(4, *blocks[0].shape)]
        return call(
            stack_kernel, out, 0, at, *blocks, anywhere=4, spaces=pl.ANY, scratch=[sems]
        )[0]

    def halves(next_, last):
        out = [bfloat16(2, *next_.shape[1:])] * 2
        return call(
            halves_kernel, out, 0, at, next_, last, anywhere=2, spaces=pl.ANY, scratch=[sems]
        )

    near = stacked(near, near_1, near_2, near_3)
    near, far_1, far_3 = wave((near, far_1, far_3))
    near_next, near_last = from_z(near, 1), from_z(near, 3)
    far_2, data_l, data_rows = wave((far_2, data_l, data_rows))
    far = stacked(far, far_1, far_2, far_3)
    far_next, far_last = from_y(far, 1), from_y(far, 3)
    data_lh = flip(data_rows, "lh")
    data_lh, data_rows = wave((data_lh, data_rows))
    data_h = flip(data_rows, "h")
    nears, fars = (near, near_next, near_last), (far, far_next, far_last)
    low, high = halves(near_next, near_last)
    near_two = from_z(low, 1), from_z(high, 3)
    low, high = halves(far_next, far_last)
    far_two = from_y(low, 1), from_y(high, 3)

    one = 2 * 2 * rows * part * 2 * 2 * piece
    noise_shape = 4, 2 * piece, part
    scores, x_all = call(
        first_kernel,
        [float32(4, 4, 2 * rows, 2 * piece), bfloat16(2, 2 * rows, part)],
        12 * one,
        *(at, data_rows, data_l, data_h, data_lh, *nears, *fars),
        anywhere=10,
        scratch=[pltpu.VMEM((6, *noise_shape), jnp.bfloat16), pltpu.SemaphoreType.DMA((10,))],
    )
    give, keep = (
        call(
            functools.partial(second_kernel, half),
            [float32(2, 4, 2 * rows, 2 * piece)],
            2 * one,
            *(at, x_all, scores, *near_two, *far_two),
            anywhere=4,
            scratch=[pltpu.VMEM((4, 2, *noise_shape[1:]), jnp.bfloat16), sems],
        )[0]
        for half in (1, 0)
    )

    blocks = (8, 2 * rows, 2 * piece)
    tall = 2 * rows, 2 * piece
    least = 0.5 / count
    row_axes, col_axes = ("l", "h", "c"), ("z", "y")
    row_sent, col_sent = float32(8, 1, 2 * rows), float32(16, 8, 2 * piece)

    def exchange(sent, axes):
        return lax.all_to_all(sent, axes, 0, 0, tiled=True)

    keep, give = keep.reshape(blocks), give.reshape(blocks)
    kernel = functools.partial(rows_1_kernel, 2.0 / (width * eps))
    score, sent = call(
        kernel, [float32(*blocks), row_sent], 0, at, keep, flip(give, "c"), scratch=[pltpu.VMEM(tall, jnp.float32)] * 2
    )
    kernel = functools.partial(columns_1_kernel, log_count)
    row_pot, sent = call(
        kernel, [float32(*tall), col_sent], 0, at, exchange(sent, row_axes), score
    )
    plan, sent = call(
        rows_2_kernel,
        [float32(*blocks), row_sent],
        0,
        *(at, exchange(sent, col_axes), score, row_pot),
        scratch=[pltpu.VMEM(tall, jnp.float32)],
    )
    plan_other = flip(plan, "c")
    kernel = functools.partial(columns_2_kernel, least)
    col_sent = float32(32, 8, 2 * piece)
    row_scale, sent = call(
        kernel, [float32(*tall), col_sent], 0, at, exchange(sent, row_axes), plan
    )
    kernel = functools.partial(weights_kernel, least)
    (weights,) = call(
        kernel,
        [bfloat16(16, *blocks[1:])],
        0,
        *(at, exchange(sent, ("z", "y", "c")), plan, plan_other, row_scale),
    )
    weights = weights.reshape(4, 4, *blocks[1:])

    near_noise, far_noise = (*nears, *near_two), (*fars, *far_two)
    message = bfloat16(mid + 16, part)
    low, high = call(target_1_kernel, [message] * 2, 8 * one, at, weights, *far_noise)
    low, high = flip(low, "l"), flip(high, "lh")

    def other_rows(place, half, came, names):
        noise = near_noise if place is near_place else far_noise
        kernel = functools.partial(target_2_kernel, place, half)
        outs = [message, float32(mid, part), float32(8, mid)]
        sent, *kept = call(kernel, outs, 8 * one, at, weights, *noise)
        added = call(add_kernel, [message], 0, at, *kept, came)[0]
        return flip(sent, names), flip(added, names)

    lh_high, lh_low = other_rows(far_place, 0, low, "lh")
    l_low, l_high = other_rows(near_place, 1, high, "l")
    own = call(
        target_3_kernel,
        [float32(rows, part), float32(8, rows)],
        8 * one,
        *(at, weights, *near_noise),
    )
    messages = l_low, l_high, lh_low, lh_high
    return call(last_kernel, [bfloat16(rows, part)], 0, at, *own, *messages)[0]


def solution(mesh):
    fine = Mesh(mesh.devices.reshape(SIZES), AXES)
    spec = P(("z", "y", "l"), ("h", "c"))
    return jax.shard_map(
        per_device, mesh=fine, in_specs=(spec, spec), out_specs=spec, check_vma=False
    )
```

```python
import functools
import itertools
import math

import jax
import jax.numpy as jnp
from jax import lax
from jax.experimental import pallas as pl
from jax.experimental.pallas import tpu as pltpu
from jax.sharding import Mesh, PartitionSpec as P

AXES = ("z", "y", "l", "h", "c")
SIZES = (4, 4, 2, 2, 2)


def index_of(*place):
    index = 0
    for n, a in zip(SIZES, place):
        index = index * n + a % n
    return index


def move(value, dest):
    places = itertools.product(*(range(n) for n in SIZES))
    pairs = [(index_of(*place), index_of(*dest(*place))) for place in places]
    return lax.ppermute(value, AXES, pairs)


def from_y(value, k):
    return move(value, lambda z, y, l, h, c: (z, y - k, l, h, c))


def from_z(value, k):
    return move(value, lambda z, y, l, h, c: (z - k, y, l, h, c))


def flip(value, names):
    return move(
        value,
        lambda *place: [1 - a if name in names else a for name, a in zip(AXES, place)],
    )


def cross(a, b):
    return lax.dot_general(a, b, (((1,), (1,)), ((), ())), preferred_element_type=jnp.float32)


def dot(a, b):
    return jnp.dot(a, b, preferred_element_type=jnp.float32)


def exact_terms(total):
    terms = []
    for _ in range(3):
        terms.append(total.astype(jnp.bfloat16))
        total = total - terms[-1].astype(jnp.float32)
    return terms


def flat(blocks):
    return blocks.reshape(-1, blocks.shape[-1])


def half_squares(rows):
    sums = 0.0
    for at in range(0, rows.shape[1], 128):
        wide = rows[:, at : at + 128].astype(jnp.float32)
        sums = sums + wide * wide
    ones = jnp.full((16, 128), 0.5, jnp.bfloat16)
    return sum(cross(ones, term) for term in exact_terms(sums))[:1]


def call(kernel, outs, flops, *args, anywhere=0, spaces=None, scratch=()):
    moved = sum(a.size * a.dtype.itemsize for a in (*args, *outs))
    inner = len(args) - 1 - anywhere
    return pl.pallas_call(
        kernel,
        out_shape=outs,
        in_specs=[pl.BlockSpec(memory_space=pltpu.SMEM)]
        + [pl.BlockSpec(memory_space=pltpu.VMEM)] * inner
        + [pl.BlockSpec(memory_space=pl.ANY)] * anywhere,
        out_specs=[pl.BlockSpec(memory_space=spaces or pltpu.VMEM)] * len(outs),
        scratch_shapes=scratch,
        compiler_params=pltpu.CompilerParams(vmem_limit_bytes=20 * 2**20),
        cost_estimate=pl.CostEstimate(flops=flops, bytes_accessed=moved, transcendentals=0),
    )(*args)


def started(sems, *pairs):
    copies = [pltpu.make_async_copy(a, b, sems.at[n]) for n, (a, b) in enumerate(pairs)]
    for copy in copies:
        copy.start()
    return copies


def terms_in_rows(vec):
    row = lax.broadcasted_iota(jnp.int32, (16, vec.shape[1]), 0)
    terms = jnp.zeros(row.shape, jnp.float32)
    for n, term in enumerate(exact_terms(vec)):
        terms = jnp.where(row == n, term.astype(jnp.float32), terms)
    return terms.astype(jnp.bfloat16)


def to_rows(terms):
    ones = jnp.ones((terms.shape[0], 128), jnp.bfloat16)
    return lax.dot_general(
        terms, ones, (((0,), (0,)), ((), ())), preferred_element_type=jnp.float32
    )


def lane_sums(values):
    ones = jnp.ones((16, 128), jnp.bfloat16)
    return sum(cross(ones, term) for term in exact_terms(values))[:1]


def first_lanes(values):
    lane = lax.broadcasted_iota(jnp.int32, (16, 128), 1)
    pick = jnp.where(lane == 0, 1.0, 0.0).astype(jnp.bfloat16)
    return sum(cross(pick, term) for term in exact_terms(values))[:1]


def log_sum_exp(values):
    top = functools.reduce(jnp.maximum, values)
    return top + jnp.log(sum(jnp.exp(v - top) for v in values))


def stack_kernel(at, *refs):
    *blocks, out, sems = refs
    copies = started(sems, *((block, out.at[n]) for n, block in enumerate(blocks)))
    for copy in copies:
        copy.wait()


def halves_kernel(at, next_, last, low, high, sems):
    for copy in started(sems, (next_.at[:2], low), (last.at[2:], high)):
        copy.wait()


def near_place(at, k, r):
    return lax.rem(at[0] + k - 2 * at[4] + 4, 4), lax.rem(at[1] + r, 4)


def far_place(at, k, r):
    return lax.rem(at[0] + r - 2 * at[4] + 4, 4), lax.rem(at[1] + k, 4)


def first_kernel(at, *refs):
    data, noises, (out, x, held, sems) = refs[:4], refs[4:10], refs[10:]
    rows = data[0].shape[0]
    own, other = (pl.ds(pl.multiple_of(r * rows, rows), rows) for r in (at[2], 1 - at[2]))
    places = x.at[0, own], x.at[0, other], x.at[1, own], x.at[1, other]
    copies = started(
        sems, *zip(data, places), *((noise, held.at[n]) for n, noise in enumerate(noises))
    )
    for copy in copies[:4]:
        copy.wait()
    x_sq = 0.0
    for side in range(2):
        for span in range(0, x.shape[2], 128):
            wide = x[side, :, span : span + 128].astype(jnp.float32)
            x_sq = x_sq + wide * wide
    x_sq = jnp.broadcast_to(0.5 * jnp.sum(x_sq, axis=1, keepdims=True), x_sq.shape)
    for n, k in enumerate((0, 1, 3)):
        copies[4 + n].wait()
        for r in (0, 2):
            noise = flat(held[n, r : r + 2])
            value = cross(x[0], noise) - half_squares(noise)
            out[near_place(at, k, r)] = value[:, :128] - x_sq
            out[near_place(at, k, r + 1)] = value[:, 128:] - x_sq
    for r in range(4):
        out[near_place(at, 2, r)] = -x_sq
    for n, k in enumerate((0, 1, 3)):
        copies[7 + n].wait()
        for r in (0, 2):
            noise = flat(held[3 + n, r : r + 2])
            value = cross(x[1], noise) - half_squares(noise)
            out[far_place(at, k, r)] += value[:, :128]
            out[far_place(at, k, r + 1)] += value[:, 128:]


def second_kernel(half, at, x, acc, n_a, n_b, out, held, sems):
    copies = started(sems, *((p, held.at[n]) for n, p in enumerate((n_a, n_b))))
    for block in range(2):
        for j in range(4):
            out[block, j] = acc[2 * half + block, j]
    for copy in copies:
        copy.wait()
    block, _ = near_place(at, 2, 0)

    @pl.when((block >= 2) == bool(half))
    def _():
        for n, r in ((0, 0), (1, 2)):
            noise = flat(held[n])
            value = cross(x[0], noise) - half_squares(noise)
            out[block - 2 * half, near_place(at, 2, r)[1]] += value[:, :128]
            out[block - 2 * half, near_place(at, 2, r + 1)[1]] += value[:, 128:]


def third_kernel(at, x, f_a, f_b, keep, give, held, sems):
    copies = started(sems, *((p, held.at[n]) for n, p in enumerate((f_a, f_b))))
    for copy in copies:
        copy.wait()
    for block in range(4):
        r = lax.rem(2 * at[4] + block - at[0] + 4, 4)
        noise = held[r // 2, lax.rem(r, 2)]
        (keep, give)[block // 2][block % 2] = cross(x[1], noise) - half_squares(noise)


def weights_of(at, weights, place, own_rows):
    rows = weights.shape[2] // 2
    to_l = at[2] if own_rows else 1 - at[2]
    here = pl.ds(pl.multiple_of(to_l * rows, rows), rows)
    parts = []
    for k, rs in ((0, range(4)), (1, range(4)), (3, range(4)), (2, (0, 1)), (2, (2, 3))):
        blocks = [place(at, k, r) for r in rs]
        parts.append(
            jnp.concatenate([weights[block[0], block[1], here] for block in blocks], axis=1)
        )
    total = 0.0
    for value in parts:
        total = total + cross(jnp.ones((16, value.shape[1]), jnp.bfloat16), value)
    return parts, total[:1]


STEP = 256


def product(parts, noise, first):
    span = slice(first, first + STEP)
    return sum(dot(w, flat(p[:, :, span])) for w, p in zip(parts, noise))


def target_1_kernel(at, weights, p0, p1, p3, p2_a, p2_b, low, high):
    parts, total = weights_of(at, weights, far_place, True)
    mid = low.shape[0] - 16
    for first in range(0, p0.shape[-1], STEP):
        value = product(parts, (p0, p1, p3, p2_a, p2_b), first)
        low[:mid, first : first + STEP] = value[:mid].astype(low.dtype)
        high[:mid, first : first + STEP] = value[mid:].astype(high.dtype)
    for n, out in enumerate((low, high)):
        out[mid:, :] = jnp.zeros((16, out.shape[1]), out.dtype)
        out[mid:, :mid] = terms_in_rows(total[:, n * mid : n * mid + mid])


def target_2_kernel(
    place, half, at, weights, p0, p1, p3, p2_a, p2_b, message, values, row_total
):
    parts, total = weights_of(at, weights, place, False)
    mid = values.shape[0]
    kept, sent = (slice(n * mid, n * mid + mid) for n in (half, 1 - half))
    for first in range(0, p0.shape[-1], STEP):
        value = product(parts, (p0, p1, p3, p2_a, p2_b), first)
        message[:, first : first + STEP] = value[sent].astype(message.dtype)
        values[:, first : first + STEP] = value[kept]
    row_total[...] = jnp.broadcast_to(total, row_total.shape)


def target_3_kernel(at, weights, p0, p1, p3, p2_a, p2_b, values, row_total):
    parts, total = weights_of(at, weights, near_place, True)
    for first in range(0, p0.shape[-1], STEP):
        values[:, first : first + STEP] = product(parts, (p0, p1, p3, p2_a, p2_b), first)
    row_total[...] = jnp.broadcast_to(total, row_total.shape)


def add_kernel(half, at, values, row_total, came, out):
    mid = values.shape[0]
    out[:mid, :] = (values[...] + came[:mid].astype(jnp.float32)).astype(out.dtype)
    terms = came[mid:, :mid].astype(jnp.float32)
    total = [row_total[:1, :mid], row_total[:1, mid:]]
    total[half] = total[half] + terms[0:1] + terms[1:2] + terms[2:3]
    out[mid:, :] = jnp.zeros((16, out.shape[1]), out.dtype)
    out[mid:, : 2 * mid] = terms_in_rows(jnp.concatenate(total, axis=1))


def last_kernel(at, own, own_total, l_low, l_high, lh_low, lh_high, out):
    mid = own.shape[0] // 2
    terms = [m[mid:, : 2 * mid] for m in (l_high, lh_low)]
    total = to_rows(jnp.concatenate([terms_in_rows(own_total[:1])] + terms, axis=0))
    for n, messages in enumerate(((l_low, lh_low), (l_high, lh_high))):
        here = slice(n * mid, n * mid + mid)
        for column in range(0, own.shape[1], 128):
            span = slice(column, column + 128)
            value = own[here, span]
            for m in messages:
                value = value + m[:mid, span].astype(jnp.float32)
            out[here, span] = (value / total[here]).astype(out.dtype)


TILE = 64


def rows_1_kernel(scale, at, keep, got, far_keep, far_got, score, sent, tops, sums):
    blocks = keep.shape[0]
    late = lax.rem(at[1] + 2, 4)

    @pl.loop(0, keep.shape[1] // TILE)
    def _(t):
        here = pl.ds(pl.multiple_of(t * TILE, TILE), TILE)
        for b in range(blocks):
            score[b, here] = (keep[b, here] + got[b, here]) * scale
        for b in range(2):
            score[4 * b + late, here] += (far_keep[b, here] + far_got[b, here]) * scale
        top = functools.reduce(jnp.maximum, [score[b, here] for b in range(blocks)])
        top = jnp.broadcast_to(jnp.max(top, axis=1, keepdims=True), top.shape)
        tops[here] = top
        sums[here] = sum(jnp.exp(score[b, here] - top) for b in range(blocks))

    log_row = first_lanes(tops[...]) + jnp.log(lane_sums(sums[...]))
    for n in range(sent.shape[0]):
        sent[n] = log_row


def columns_1_kernel(log_count, at, came, score, row_pot, sent):
    pot = -log_count - log_sum_exp([came[n] for n in range(came.shape[0])])
    row_pot[...] = to_rows(terms_in_rows(pot))
    logs = []
    for b in range(score.shape[0]):
        value = score[b] + row_pot[...]
        top = jnp.max(value, axis=0, keepdims=True)
        total = jnp.sum(jnp.exp(value - top), axis=0, keepdims=True)
        logs.append(top + jnp.log(total))
    logs = jnp.concatenate(logs)
    for n in range(sent.shape[0]):
        sent[n] = logs


def rows_2_kernel(at, came, score, row_pot, plan, sent, sums):
    pot = -log_sum_exp([came[n] for n in range(came.shape[0])])

    @pl.loop(0, score.shape[1] // TILE)
    def _(t):
        here = pl.ds(pl.multiple_of(t * TILE, TILE), TILE)
        total = 0.0
        for b in range(score.shape[0]):
            value = score[b, here] + row_pot[here] + pot[b : b + 1]
            value = jnp.exp(jnp.minimum(value, 0.0))
            plan[b, here] = value
            total = total + value
        sums[here] = total

    row_sum = lane_sums(sums[...])
    for n in range(sent.shape[0]):
        sent[n] = row_sum


def columns_2_kernel(least, at, came, plan, row_scale, sent):
    total = sum(came[n] for n in range(came.shape[0]))
    row_scale[...] = to_rows(terms_in_rows(1.0 / jnp.maximum(total, least)))
    sums = []
    for b in range(plan.shape[0]):
        sums.append(jnp.sum(plan[b] * row_scale[...], axis=0, keepdims=True))
    sums = jnp.concatenate(sums)
    for n in range(sent.shape[0]):
        sent[n] = sums


def weights_kernel(least, at, came, plan, other, row_scale, weights):
    c = at[4]
    mine = sum(came[2 * n + c] for n in range(came.shape[0] // 2))
    theirs = sum(came[2 * n + 1 - c] for n in range(came.shape[0] // 2))
    for half, (values, total) in enumerate(((plan, mine), (other, theirs))):
        scale = 1.0 / jnp.maximum(total, least)
        for b in range(values.shape[0]):
            value = values[b] * row_scale[...] * scale[b : b + 1]
            weights[values.shape[0] * half + b] = value.astype(weights.dtype)


def per_device(data_rows, noise_rows):
    z, y, l, h, c = (lax.axis_index(name) for name in AXES)
    rows, part = data_rows.shape
    width = part * 4
    count = rows * 32
    eps = 0.64 / math.sqrt(width)
    log_count = math.log(count)
    piece = rows // 4

    def float32(*shape):
        return jax.ShapeDtypeStruct(shape, jnp.float32)

    def bfloat16(*shape):
        return jax.ShapeDtypeStruct(shape, jnp.bfloat16)

    at = jnp.stack([z, y, l, h, c])

    wave = lax.optimization_barrier
    mid = rows // 2
    near = lax.dynamic_slice_in_dim(noise_rows, h * mid, mid)
    far = flip(lax.dynamic_slice_in_dim(noise_rows, (1 - h) * mid, mid), "h")
    near_1, near_3 = from_y(near, 1), from_y(near, 3)
    far, data_rows = wave((far, data_rows))
    data_l, data_lh = flip(data_rows, "l"), flip(data_rows, "lh")
    near_2 = from_y(near_1, 1)
    near_3, far_1, far_3 = wave((near_3, from_z(far, 1), from_z(far, 3)))
    far_2, data_l, data_lh, data_rows = wave((from_z(far_1, 1), data_l, data_lh, data_rows))
    sems = pltpu.SemaphoreType.DMA((4,))

    def stacked(*blocks):
        out = [bfloat16(4, *blocks[0].shape)]
        return call(
            stack_kernel, out, 0, at, *blocks, anywhere=4, spaces=pl.ANY, scratch=[sems]
        )[0]

    def halves(next_, last):
        out = [bfloat16(2, *next_.shape[1:])] * 2
        return call(
            halves_kernel, out, 0, at, next_, last, anywhere=2, spaces=pl.ANY, scratch=[sems]
        )

    near, far = stacked(near, near_1, near_2, near_3), stacked(far, far_1, far_2, far_3)
    near_next, near_last = from_z(near, 1), from_z(near, 3)
    far_next, far_last = from_y(far, 1), from_y(far, 3)
    data_h = flip(data_rows, "h")
    far_next, far_last, data_h = wave((far_next, far_last, data_h))
    nears, fars = (near, near_next, near_last), (far, far_next, far_last)
    low, high = halves(near_next, near_last)
    near_two = from_z(low, 1), from_z(high, 3)
    low, high = halves(far_next, far_last)
    far_two = from_y(low, 1), from_y(high, 3)

    one = 2 * 2 * rows * part * 2 * 2 * piece
    noise_shape = 4, 2 * piece, part
    scores, x_all = call(
        first_kernel,
        [float32(4, 4, 2 * rows, 2 * piece), bfloat16(2, 2 * rows, part)],
        12 * one,
        *(at, data_rows, data_l, data_h, data_lh, *nears, *fars),
        anywhere=10,
        scratch=[pltpu.VMEM((6, *noise_shape), jnp.bfloat16), pltpu.SemaphoreType.DMA((10,))],
    )
    give, keep = (
        call(
            functools.partial(second_kernel, half),
            [float32(2, 4, 2 * rows, 2 * piece)],
            100 * one,
            *(at, x_all, scores, *near_two),
            anywhere=2,
            scratch=[pltpu.VMEM((2, 2, *noise_shape[1:]), jnp.bfloat16), sems],
        )[0]
        for half in (1, 0)
    )
    far_keep, far_give = call(
        third_kernel,
        [float32(2, 2 * rows, 2 * piece)] * 2,
        2 * one,
        *(at, x_all, *far_two),
        anywhere=2,
        scratch=[pltpu.VMEM((2, 2, *noise_shape[1:]), jnp.bfloat16), sems],
    )

    blocks = (8, 2 * rows, 2 * piece)
    tall = 2 * rows, 2 * piece
    least = 0.5 / count
    row_axes, col_axes = ("l", "h", "c"), ("z", "y")
    row_sent, col_sent = float32(8, 1, 2 * rows), float32(16, 8, 2 * piece)

    def exchange(sent, axes):
        return lax.all_to_all(sent, axes, 0, 0, tiled=True)

    keep, give = keep.reshape(blocks), give.reshape(blocks)
    kernel = functools.partial(rows_1_kernel, 2.0 / (width * eps))
    score, sent = call(
        kernel,
        [float32(*blocks), row_sent],
        0,
        *(at, keep, flip(give, "c"), far_keep, flip(far_give, "c")),
        scratch=[pltpu.VMEM(tall, jnp.float32)] * 2,
    )
    kernel = functools.partial(columns_1_kernel, log_count)
    row_pot, sent = call(
        kernel, [float32(*tall), col_sent], 0, at, exchange(sent, row_axes), score
    )
    plan, sent = call(
        rows_2_kernel,
        [float32(*blocks), row_sent],
        0,
        *(at, exchange(sent, col_axes), score, row_pot),
        scratch=[pltpu.VMEM(tall, jnp.float32)],
    )
    plan_other = flip(plan, "c")
    kernel = functools.partial(columns_2_kernel, least)
    col_sent = float32(32, 8, 2 * piece)
    row_scale, sent = call(
        kernel, [float32(*tall), col_sent], 0, at, exchange(sent, row_axes), plan
    )
    kernel = functools.partial(weights_kernel, least)
    (weights,) = call(
        kernel,
        [bfloat16(16, *blocks[1:])],
        0,
        *(at, exchange(sent, ("z", "y", "c")), plan, plan_other, row_scale),
    )
    weights = weights.reshape(4, 4, *blocks[1:])

    near_noise, far_noise = (*nears, *near_two), (*fars, *far_two)
    message = bfloat16(mid + 16, part)
    low, high = call(target_1_kernel, [message] * 2, 8 * one, at, weights, *far_noise)
    low, high = flip(low, "l"), flip(high, "lh")

    def other_rows(place, half, came, names):
        noise = near_noise if place is near_place else far_noise
        kernel = functools.partial(target_2_kernel, place, half)
        outs = [bfloat16(mid, part), float32(mid, part), float32(8, rows)]
        sent, *kept = call(kernel, outs, 8 * one, at, weights, *noise)
        added = call(functools.partial(add_kernel, half), [message], 0, at, *kept, came)[0]
        return flip(sent, names), flip(added, names)

    lh_high, lh_low = other_rows(far_place, 0, low, "lh")
    l_low, l_high = other_rows(near_place, 1, high, "l")
    own = call(
        target_3_kernel,
        [float32(rows, part), float32(8, rows)],
        64 * one,
        *(at, weights, *near_noise),
    )
    messages = l_low, l_high, lh_low, lh_high
    return call(last_kernel, [bfloat16(rows, part)], 0, at, *own, *messages)[0]


def solution(mesh):
    fine = Mesh(mesh.devices.reshape(SIZES), AXES)
    spec = P(("z", "y", "l"), ("h", "c"))
    return jax.shard_map(
        per_device, mesh=fine, in_specs=(spec, spec), out_specs=spec, check_vma=False
    )
```

```python
import functools
import itertools
import math

import jax
import jax.numpy as jnp
from jax import lax
from jax.experimental import pallas as pl
from jax.experimental.pallas import tpu as pltpu
from jax.sharding import Mesh, PartitionSpec as P

AXES = ("z", "y", "l", "h", "c")
SIZES = (4, 4, 2, 2, 2)


def index_of(*place):
    index = 0
    for n, a in zip(SIZES, place):
        index = index * n + a % n
    return index


def move(value, dest):
    places = itertools.product(*(range(n) for n in SIZES))
    pairs = [(index_of(*place), index_of(*dest(*place))) for place in places]
    return lax.ppermute(value, AXES, pairs)


def from_y(value, k):
    return move(value, lambda z, y, l, h, c: (z, y - k, l, h, c))


def from_z(value, k):
    return move(value, lambda z, y, l, h, c: (z - k, y, l, h, c))


def flip(value, names):
    return move(
        value,
        lambda *place: [1 - a if name in names else a for name, a in zip(AXES, place)],
    )


def cross(a, b):
    return lax.dot_general(a, b, (((1,), (1,)), ((), ())), preferred_element_type=jnp.float32)


def dot(a, b):
    return jnp.dot(a, b, preferred_element_type=jnp.float32)


def exact_terms(total):
    terms = []
    for _ in range(3):
        terms.append(total.astype(jnp.bfloat16))
        total = total - terms[-1].astype(jnp.float32)
    return terms


def flat(blocks):
    return blocks.reshape(-1, blocks.shape[-1])


def half_squares(rows):
    sums = 0.0
    for at in range(0, rows.shape[1], 128):
        wide = rows[:, at : at + 128].astype(jnp.float32)
        sums = sums + wide * wide
    ones = jnp.full((16, 128), 0.5, jnp.bfloat16)
    return sum(cross(ones, term) for term in exact_terms(sums))[:1]


def call(kernel, outs, flops, *args, anywhere=0, spaces=None, scratch=()):
    moved = sum(a.size * a.dtype.itemsize for a in (*args, *outs))
    inner = len(args) - 1 - anywhere
    return pl.pallas_call(
        kernel,
        out_shape=outs,
        in_specs=[pl.BlockSpec(memory_space=pltpu.SMEM)]
        + [pl.BlockSpec(memory_space=pltpu.VMEM)] * inner
        + [pl.BlockSpec(memory_space=pl.ANY)] * anywhere,
        out_specs=[pl.BlockSpec(memory_space=spaces or pltpu.VMEM)] * len(outs),
        scratch_shapes=scratch,
        compiler_params=pltpu.CompilerParams(vmem_limit_bytes=20 * 2**20),
        cost_estimate=pl.CostEstimate(flops=flops, bytes_accessed=moved, transcendentals=0),
    )(*args)


def started(sems, *pairs):
    copies = [pltpu.make_async_copy(a, b, sems.at[n]) for n, (a, b) in enumerate(pairs)]
    for copy in copies:
        copy.start()
    return copies


def terms_in_rows(vec):
    row = lax.broadcasted_iota(jnp.int32, (16, vec.shape[1]), 0)
    terms = jnp.zeros(row.shape, jnp.float32)
    for n, term in enumerate(exact_terms(vec)):
        terms = jnp.where(row == n, term.astype(jnp.float32), terms)
    return terms.astype(jnp.bfloat16)


def to_rows(terms):
    ones = jnp.ones((terms.shape[0], 128), jnp.bfloat16)
    return lax.dot_general(
        terms, ones, (((0,), (0,)), ((), ())), preferred_element_type=jnp.float32
    )


def lane_sums(values):
    ones = jnp.ones((16, 128), jnp.bfloat16)
    return sum(cross(ones, term) for term in exact_terms(values))[:1]


def first_lanes(values):
    lane = lax.broadcasted_iota(jnp.int32, (16, 128), 1)
    pick = jnp.where(lane == 0, 1.0, 0.0).astype(jnp.bfloat16)
    return sum(cross(pick, term) for term in exact_terms(values))[:1]


def log_sum_exp(values):
    top = functools.reduce(jnp.maximum, values)
    return top + jnp.log(sum(jnp.exp(v - top) for v in values))


def stack_kernel(at, *refs):
    *blocks, out, sems = refs
    copies = started(sems, *((block, out.at[n]) for n, block in enumerate(blocks)))
    for copy in copies:
        copy.wait()


def halves_kernel(at, next_, last, low, high, sems):
    for copy in started(sems, (next_.at[:2], low), (last.at[2:], high)):
        copy.wait()


def near_place(at, k, r):
    return lax.rem(at[0] + k - 2 * at[4] + 4, 4), lax.rem(at[1] + r, 4)


def far_place(at, k, r):
    return lax.rem(at[0] + r - 2 * at[4] + 4, 4), lax.rem(at[1] + k, 4)


def first_kernel(at, *refs):
    data, noises, (out, x, held, sems) = refs[:4], refs[4:10], refs[10:]
    rows = data[0].shape[0]
    own, other = (pl.ds(pl.multiple_of(r * rows, rows), rows) for r in (at[2], 1 - at[2]))
    places = x.at[0, own], x.at[0, other], x.at[1, own], x.at[1, other]
    copies = started(
        sems, *zip(data, places), *((noise, held.at[n]) for n, noise in enumerate(noises))
    )
    for copy in copies[:4]:
        copy.wait()
    x_sq = 0.0
    for side in range(2):
        for span in range(0, x.shape[2], 128):
            wide = x[side, :, span : span + 128].astype(jnp.float32)
            x_sq = x_sq + wide * wide
    x_sq = jnp.broadcast_to(0.5 * jnp.sum(x_sq, axis=1, keepdims=True), x_sq.shape)
    for n, k in enumerate((0, 1, 3)):
        copies[4 + n].wait()
        for r in (0, 2):
            noise = flat(held[n, r : r + 2])
            value = cross(x[0], noise) - half_squares(noise)
            out[near_place(at, k, r)] = value[:, :128] - x_sq
            out[near_place(at, k, r + 1)] = value[:, 128:] - x_sq
    for r in range(4):
        out[near_place(at, 2, r)] = -x_sq
    for n, k in enumerate((0, 1, 3)):
        copies[7 + n].wait()
        for r in (0, 2):
            noise = flat(held[3 + n, r : r + 2])
            value = cross(x[1], noise) - half_squares(noise)
            out[far_place(at, k, r)] += value[:, :128]
            out[far_place(at, k, r + 1)] += value[:, 128:]


def second_kernel(half, at, x, acc, n_a, n_b, out, held, sems):
    copies = started(sems, *((p, held.at[n]) for n, p in enumerate((n_a, n_b))))
    for block in range(2):
        for j in range(4):
            out[block, j] = acc[2 * half + block, j]
    for copy in copies:
        copy.wait()
    block, _ = near_place(at, 2, 0)

    @pl.when((block >= 2) == bool(half))
    def _():
        for n, r in ((0, 0), (1, 2)):
            noise = flat(held[n])
            value = cross(x[0], noise) - half_squares(noise)
            out[block - 2 * half, near_place(at, 2, r)[1]] += value[:, :128]
            out[block - 2 * half, near_place(at, 2, r + 1)[1]] += value[:, 128:]


def third_kernel(at, x, f_a, f_b, keep, give, held, sems):
    copies = started(sems, *((p, held.at[n]) for n, p in enumerate((f_a, f_b))))
    for copy in copies:
        copy.wait()
    for block in range(4):
        r = lax.rem(2 * at[4] + block - at[0] + 4, 4)
        noise = held[r // 2, lax.rem(r, 2)]
        (keep, give)[block // 2][block % 2] = cross(x[1], noise) - half_squares(noise)


def weights_of(at, weights, place, own_rows):
    rows = weights.shape[2] // 2
    to_l = at[2] if own_rows else 1 - at[2]
    here = pl.ds(pl.multiple_of(to_l * rows, rows), rows)
    parts = []
    for k, rs in ((0, range(4)), (1, range(4)), (3, range(4)), (2, (0, 1)), (2, (2, 3))):
        blocks = [place(at, k, r) for r in rs]
        parts.append(
            jnp.concatenate([weights[block[0], block[1], here] for block in blocks], axis=1)
        )
    total = 0.0
    for value in parts:
        total = total + cross(jnp.ones((16, value.shape[1]), jnp.bfloat16), value)
    return parts, total[:1]


STEP = 256


def product(parts, noise, first):
    span = slice(first, first + STEP)
    return sum(dot(w, flat(p[:, :, span])) for w, p in zip(parts, noise))


def target_1_kernel(at, weights, p0, p1, p3, p2_a, p2_b, low, high):
    parts, total = weights_of(at, weights, far_place, True)
    mid = low.shape[0] - 16
    for first in range(0, p0.shape[-1], STEP):
        value = product(parts, (p0, p1, p3, p2_a, p2_b), first)
        low[:mid, first : first + STEP] = value[:mid].astype(low.dtype)
        high[:mid, first : first + STEP] = value[mid:].astype(high.dtype)
    for n, out in enumerate((low, high)):
        out[mid:, :] = jnp.zeros((16, out.shape[1]), out.dtype)
        out[mid:, :mid] = terms_in_rows(total[:, n * mid : n * mid + mid])


def target_2_kernel(
    place, half, at, weights, p0, p1, p3, p2_a, p2_b, message, values, row_total
):
    parts, total = weights_of(at, weights, place, False)
    mid = values.shape[0]
    kept, sent = (slice(n * mid, n * mid + mid) for n in (half, 1 - half))
    for first in range(0, p0.shape[-1], STEP):
        value = product(parts, (p0, p1, p3, p2_a, p2_b), first)
        message[:, first : first + STEP] = value[sent].astype(message.dtype)
        values[:, first : first + STEP] = value[kept]
    row_total[...] = jnp.broadcast_to(total, row_total.shape)


def target_3_kernel(at, weights, p0, p1, p3, p2_a, p2_b, values, row_total):
    parts, total = weights_of(at, weights, near_place, True)
    for first in range(0, p0.shape[-1], STEP):
        values[:, first : first + STEP] = product(parts, (p0, p1, p3, p2_a, p2_b), first)
    row_total[...] = jnp.broadcast_to(total, row_total.shape)


def add_kernel(half, at, values, row_total, came, out):
    mid = values.shape[0]
    out[:mid, :] = (values[...] + came[:mid].astype(jnp.float32)).astype(out.dtype)
    terms = came[mid:, :mid].astype(jnp.float32)
    total = [row_total[:1, :mid], row_total[:1, mid:]]
    total[half] = total[half] + terms[0:1] + terms[1:2] + terms[2:3]
    out[mid:, :] = jnp.zeros((16, out.shape[1]), out.dtype)
    out[mid:, : 2 * mid] = terms_in_rows(jnp.concatenate(total, axis=1))


def last_kernel(at, own, own_total, l_low, l_high, lh_low, lh_high, out):
    mid = own.shape[0] // 2
    terms = [m[mid:, : 2 * mid] for m in (l_high, lh_low)]
    total = to_rows(jnp.concatenate([terms_in_rows(own_total[:1])] + terms, axis=0))
    for n, messages in enumerate(((l_low, lh_low), (l_high, lh_high))):
        here = slice(n * mid, n * mid + mid)
        for column in range(0, own.shape[1], 128):
            span = slice(column, column + 128)
            value = own[here, span]
            for m in messages:
                value = value + m[:mid, span].astype(jnp.float32)
            out[here, span] = (value / total[here]).astype(out.dtype)


TILE = 64


def rows_1_kernel(scale, at, keep, got, far_keep, far_got, score, sent, tops, sums):
    blocks = keep.shape[0]
    late = lax.rem(at[1] + 2, 4)

    @pl.loop(0, keep.shape[1] // TILE)
    def _(t):
        here = pl.ds(pl.multiple_of(t * TILE, TILE), TILE)
        for b in range(blocks):
            score[b, here] = (keep[b, here] + got[b, here]) * scale
        for b in range(2):
            score[4 * b + late, here] += (far_keep[b, here] + far_got[b, here]) * scale
        top = functools.reduce(jnp.maximum, [score[b, here] for b in range(blocks)])
        top = jnp.broadcast_to(jnp.max(top, axis=1, keepdims=True), top.shape)
        tops[here] = top
        sums[here] = sum(jnp.exp(score[b, here] - top) for b in range(blocks))

    log_row = first_lanes(tops[...]) + jnp.log(lane_sums(sums[...]))
    for n in range(sent.shape[0]):
        sent[n] = log_row


def columns_1_kernel(log_count, at, came, score, row_pot, sent):
    pot = -log_count - log_sum_exp([came[n] for n in range(came.shape[0])])
    row_pot[...] = to_rows(terms_in_rows(pot))
    logs = []
    for b in range(score.shape[0]):
        value = score[b] + row_pot[...]
        top = jnp.max(value, axis=0, keepdims=True)
        total = jnp.sum(jnp.exp(value - top), axis=0, keepdims=True)
        logs.append(top + jnp.log(total))
    logs = jnp.concatenate(logs)
    for n in range(sent.shape[0]):
        sent[n] = logs


def rows_2_kernel(at, came, score, row_pot, plan, sent, sums):
    pot = -log_sum_exp([came[n] for n in range(came.shape[0])])

    @pl.loop(0, score.shape[1] // TILE)
    def _(t):
        here = pl.ds(pl.multiple_of(t * TILE, TILE), TILE)
        total = 0.0
        for b in range(score.shape[0]):
            value = score[b, here] + row_pot[here] + pot[b : b + 1]
            value = jnp.exp(jnp.minimum(value, 0.0))
            plan[b, here] = value
            total = total + value
        sums[here] = total

    row_sum = lane_sums(sums[...])
    for n in range(sent.shape[0]):
        sent[n] = row_sum


def columns_2_kernel(least, at, came, plan, row_scale, sent):
    total = sum(came[n] for n in range(came.shape[0]))
    row_scale[...] = to_rows(terms_in_rows(1.0 / jnp.maximum(total, least)))
    sums = []
    for b in range(plan.shape[0]):
        sums.append(jnp.sum(plan[b] * row_scale[...], axis=0, keepdims=True))
    sums = jnp.concatenate(sums)
    for n in range(sent.shape[0]):
        sent[n] = sums


def weights_kernel(least, at, came, plan, other, row_scale, weights):
    c = at[4]
    mine = sum(came[2 * n + c] for n in range(came.shape[0] // 2))
    theirs = sum(came[2 * n + 1 - c] for n in range(came.shape[0] // 2))
    for half, (values, total) in enumerate(((plan, mine), (other, theirs))):
        scale = 1.0 / jnp.maximum(total, least)
        for b in range(values.shape[0]):
            value = values[b] * row_scale[...] * scale[b : b + 1]
            weights[values.shape[0] * half + b] = value.astype(weights.dtype)


def per_device(data_rows, noise_rows):
    z, y, l, h, c = (lax.axis_index(name) for name in AXES)
    rows, part = data_rows.shape
    width = part * 4
    count = rows * 32
    eps = 0.64 / math.sqrt(width)
    log_count = math.log(count)
    piece = rows // 4

    def float32(*shape):
        return jax.ShapeDtypeStruct(shape, jnp.float32)

    def bfloat16(*shape):
        return jax.ShapeDtypeStruct(shape, jnp.bfloat16)

    at = jnp.stack([z, y, l, h, c])

    wave = lax.optimization_barrier
    mid = rows // 2
    near = lax.dynamic_slice_in_dim(noise_rows, h * mid, mid)
    far = flip(lax.dynamic_slice_in_dim(noise_rows, (1 - h) * mid, mid), "h")
    near_1, near_3 = from_y(near, 1), from_y(near, 3)
    far, data_rows = wave((far, data_rows))
    data_l = flip(data_rows, "l")
    near_2 = from_y(near_1, 1)
    near_3, far_1, far_3, data_rows = wave((near_3, from_z(far, 1), from_z(far, 3), data_rows))
    data_lh = flip(data_rows, "lh")
    far_2, data_l, data_rows = wave((from_z(far_1, 1), data_l, data_rows))
    sems = pltpu.SemaphoreType.DMA((4,))

    def stacked(*blocks):
        out = [bfloat16(4, *blocks[0].shape)]
        return call(
            stack_kernel, out, 0, at, *blocks, anywhere=4, spaces=pl.ANY, scratch=[sems]
        )[0]

    def halves(next_, last):
        out = [bfloat16(2, *next_.shape[1:])] * 2
        return call(
            halves_kernel, out, 0, at, next_, last, anywhere=2, spaces=pl.ANY, scratch=[sems]
        )

    near, far = stacked(near, near_1, near_2, near_3), stacked(far, far_1, far_2, far_3)
    near_next, near_last = from_z(near, 1), from_z(near, 3)
    far_next, far_last = from_y(far, 1), from_y(far, 3)
    data_lh, data_rows = wave((data_lh, data_rows))
    data_h = flip(data_rows, "h")
    far_next, far_last, data_h = wave((far_next, far_last, data_h))
    nears, fars = (near, near_next, near_last), (far, far_next, far_last)
    low, high = halves(near_next, near_last)
    near_two = from_z(low, 1), from_z(high, 3)
    low, high = halves(far_next, far_last)
    far_two = from_y(low, 1), from_y(high, 3)

    one = 2 * 2 * rows * part * 2 * 2 * piece
    noise_shape = 4, 2 * piece, part
    scores, x_all = call(
        first_kernel,
        [float32(4, 4, 2 * rows, 2 * piece), bfloat16(2, 2 * rows, part)],
        12 * one,
        *(at, data_rows, data_l, data_h, data_lh, *nears, *fars),
        anywhere=10,
        scratch=[pltpu.VMEM((6, *noise_shape), jnp.bfloat16), pltpu.SemaphoreType.DMA((10,))],
    )
    give, keep = (
        call(
            functools.partial(second_kernel, half),
            [float32(2, 4, 2 * rows, 2 * piece)],
            100 * one,
            *(at, x_all, scores, *near_two),
            anywhere=2,
            scratch=[pltpu.VMEM((2, 2, *noise_shape[1:]), jnp.bfloat16), sems],
        )[0]
        for half in (1, 0)
    )
    far_keep, far_give = call(
        third_kernel,
        [float32(2, 2 * rows, 2 * piece)] * 2,
        2 * one,
        *(at, x_all, *far_two),
        anywhere=2,
        scratch=[pltpu.VMEM((2, 2, *noise_shape[1:]), jnp.bfloat16), sems],
    )

    blocks = (8, 2 * rows, 2 * piece)
    tall = 2 * rows, 2 * piece
    least = 0.5 / count
    row_axes, col_axes = ("l", "h", "c"), ("z", "y")
    row_sent, col_sent = float32(8, 1, 2 * rows), float32(16, 8, 2 * piece)

    def exchange(sent, axes):
        return lax.all_to_all(sent, axes, 0, 0, tiled=True)

    keep, give = keep.reshape(blocks), give.reshape(blocks)
    kernel = functools.partial(rows_1_kernel, 2.0 / (width * eps))
    score, sent = call(
        kernel,
        [float32(*blocks), row_sent],
        0,
        *(at, keep, flip(give, "c"), far_keep, flip(far_give, "c")),
        scratch=[pltpu.VMEM(tall, jnp.float32)] * 2,
    )
    kernel = functools.partial(columns_1_kernel, log_count)
    row_pot, sent = call(
        kernel, [float32(*tall), col_sent], 0, at, exchange(sent, row_axes), score
    )
    plan, sent = call(
        rows_2_kernel,
        [float32(*blocks), row_sent],
        0,
        *(at, exchange(sent, col_axes), score, row_pot),
        scratch=[pltpu.VMEM(tall, jnp.float32)],
    )
    plan_other = flip(plan, "c")
    kernel = functools.partial(columns_2_kernel, least)
    col_sent = float32(32, 8, 2 * piece)
    row_scale, sent = call(
        kernel, [float32(*tall), col_sent], 0, at, exchange(sent, row_axes), plan
    )
    kernel = functools.partial(weights_kernel, least)
    (weights,) = call(
        kernel,
        [bfloat16(16, *blocks[1:])],
        0,
        *(at, exchange(sent, ("z", "y", "c")), plan, plan_other, row_scale),
    )
    weights = weights.reshape(4, 4, *blocks[1:])

    near_noise, far_noise = (*nears, *near_two), (*fars, *far_two)
    message = bfloat16(mid + 16, part)
    low, high = call(target_1_kernel, [message] * 2, 8 * one, at, weights, *far_noise)
    low, high = flip(low, "l"), flip(high, "lh")

    def other_rows(place, half, came, names):
        noise = near_noise if place is near_place else far_noise
        kernel = functools.partial(target_2_kernel, place, half)
        outs = [bfloat16(mid, part), float32(mid, part), float32(8, rows)]
        sent, *kept = call(kernel, outs, 8 * one, at, weights, *noise)
        added = call(functools.partial(add_kernel, half), [message], 0, at, *kept, came)[0]
        return flip(sent, names), flip(added, names)

    lh_high, lh_low = other_rows(far_place, 0, low, "lh")
    l_low, l_high = other_rows(near_place, 1, high, "l")
    own = call(
        target_3_kernel,
        [float32(rows, part), float32(8, rows)],
        64 * one,
        *(at, weights, *near_noise),
    )
    messages = l_low, l_high, lh_low, lh_high
    return call(last_kernel, [bfloat16(rows, part)], 0, at, *own, *messages)[0]


def solution(mesh):
    fine = Mesh(mesh.devices.reshape(SIZES), AXES)
    spec = P(("z", "y", "l"), ("h", "c"))
    return jax.shard_map(
        per_device, mesh=fine, in_specs=(spec, spec), out_specs=spec, check_vma=False
    )
```

```python
import functools
import itertools
import math

import jax
import jax.numpy as jnp
from jax import lax
from jax.experimental import pallas as pl
from jax.experimental.pallas import tpu as pltpu
from jax.sharding import Mesh, PartitionSpec as P

AXES = ("z", "y", "l", "h", "c")
SIZES = (4, 4, 2, 2, 2)


def index_of(*place):
    index = 0
    for n, a in zip(SIZES, place):
        index = index * n + a % n
    return index


def move(value, dest):
    places = itertools.product(*(range(n) for n in SIZES))
    pairs = [(index_of(*place), index_of(*dest(*place))) for place in places]
    return lax.ppermute(value, AXES, pairs)


def from_y(value, k):
    return move(value, lambda z, y, l, h, c: (z, y - k, l, h, c))


def from_z(value, k):
    return move(value, lambda z, y, l, h, c: (z - k, y, l, h, c))


def flip(value, names):
    return move(
        value,
        lambda *place: [1 - a if name in names else a for name, a in zip(AXES, place)],
    )


def cross(a, b):
    return lax.dot_general(a, b, (((1,), (1,)), ((), ())), preferred_element_type=jnp.float32)


def dot(a, b):
    return jnp.dot(a, b, preferred_element_type=jnp.float32)


def exact_terms(total):
    terms = []
    for _ in range(3):
        terms.append(total.astype(jnp.bfloat16))
        total = total - terms[-1].astype(jnp.float32)
    return terms


def flat(blocks):
    return blocks.reshape(-1, blocks.shape[-1])


def half_squares(rows):
    sums = 0.0
    for at in range(0, rows.shape[1], 128):
        wide = rows[:, at : at + 128].astype(jnp.float32)
        sums = sums + wide * wide
    ones = jnp.full((16, 128), 0.5, jnp.bfloat16)
    return sum(cross(ones, term) for term in exact_terms(sums))[:1]


def call(kernel, outs, flops, *args, anywhere=0, spaces=None, scratch=()):
    moved = sum(a.size * a.dtype.itemsize for a in (*args, *outs))
    inner = len(args) - 1 - anywhere
    return pl.pallas_call(
        kernel,
        out_shape=outs,
        in_specs=[pl.BlockSpec(memory_space=pltpu.SMEM)]
        + [pl.BlockSpec(memory_space=pltpu.VMEM)] * inner
        + [pl.BlockSpec(memory_space=pl.ANY)] * anywhere,
        out_specs=[pl.BlockSpec(memory_space=spaces or pltpu.VMEM)] * len(outs),
        scratch_shapes=scratch,
        compiler_params=pltpu.CompilerParams(vmem_limit_bytes=20 * 2**20),
        cost_estimate=pl.CostEstimate(flops=flops, bytes_accessed=moved, transcendentals=0),
    )(*args)


def started(sems, *pairs):
    copies = [pltpu.make_async_copy(a, b, sems.at[n]) for n, (a, b) in enumerate(pairs)]
    for copy in copies:
        copy.start()
    return copies


def terms_in_rows(vec):
    row = lax.broadcasted_iota(jnp.int32, (16, vec.shape[1]), 0)
    terms = jnp.zeros(row.shape, jnp.float32)
    for n, term in enumerate(exact_terms(vec)):
        terms = jnp.where(row == n, term.astype(jnp.float32), terms)
    return terms.astype(jnp.bfloat16)


def to_rows(terms):
    ones = jnp.ones((terms.shape[0], 128), jnp.bfloat16)
    return lax.dot_general(
        terms, ones, (((0,), (0,)), ((), ())), preferred_element_type=jnp.float32
    )


def lane_sums(values):
    ones = jnp.ones((16, 128), jnp.bfloat16)
    return sum(cross(ones, term) for term in exact_terms(values))[:1]


def first_lanes(values):
    lane = lax.broadcasted_iota(jnp.int32, (16, 128), 1)
    pick = jnp.where(lane == 0, 1.0, 0.0).astype(jnp.bfloat16)
    return sum(cross(pick, term) for term in exact_terms(values))[:1]


def log_sum_exp(values):
    top = functools.reduce(jnp.maximum, values)
    return top + jnp.log(sum(jnp.exp(v - top) for v in values))


def stack_kernel(at, *refs):
    *blocks, out, sems = refs
    copies = started(sems, *((block, out.at[n]) for n, block in enumerate(blocks)))
    for copy in copies:
        copy.wait()


def halves_kernel(at, next_, last, low, high, sems):
    for copy in started(sems, (next_.at[:2], low), (last.at[2:], high)):
        copy.wait()


def near_place(at, k, r):
    return lax.rem(at[0] + k - 2 * at[4] + 4, 4), lax.rem(at[1] + r, 4)


def far_place(at, k, r):
    return lax.rem(at[0] + r - 2 * at[4] + 4, 4), lax.rem(at[1] + k, 4)


def first_kernel(at, *refs):
    data, noises, (out, x, held, sems) = refs[:4], refs[4:10], refs[10:]
    rows = data[0].shape[0]
    own, other = (pl.ds(pl.multiple_of(r * rows, rows), rows) for r in (at[2], 1 - at[2]))
    places = x.at[0, own], x.at[0, other], x.at[1, own], x.at[1, other]
    copies = started(
        sems, *zip(data, places), *((noise, held.at[n]) for n, noise in enumerate(noises))
    )
    for copy in copies[:4]:
        copy.wait()
    x_sq = 0.0
    for side in range(2):
        for span in range(0, x.shape[2], 128):
            wide = x[side, :, span : span + 128].astype(jnp.float32)
            x_sq = x_sq + wide * wide
    x_sq = jnp.broadcast_to(0.5 * jnp.sum(x_sq, axis=1, keepdims=True), x_sq.shape)
    for n, k in enumerate((0, 1, 3)):
        copies[4 + n].wait()
        for r in (0, 2):
            noise = flat(held[n, r : r + 2])
            value = cross(x[0], noise) - half_squares(noise)
            out[near_place(at, k, r)] = value[:, :128] - x_sq
            out[near_place(at, k, r + 1)] = value[:, 128:] - x_sq
    for r in range(4):
        out[near_place(at, 2, r)] = -x_sq
    for n, k in enumerate((0, 1, 3)):
        copies[7 + n].wait()
        for r in (0, 2):
            noise = flat(held[3 + n, r : r + 2])
            value = cross(x[1], noise) - half_squares(noise)
            out[far_place(at, k, r)] += value[:, :128]
            out[far_place(at, k, r + 1)] += value[:, 128:]


def second_kernel(half, at, x, acc, n_a, n_b, out, held, sems):
    copies = started(sems, *((p, held.at[n]) for n, p in enumerate((n_a, n_b))))
    for block in range(2):
        for j in range(4):
            out[block, j] = acc[2 * half + block, j]
    for copy in copies:
        copy.wait()
    block, _ = near_place(at, 2, 0)

    @pl.when((block >= 2) == bool(half))
    def _():
        for n, r in ((0, 0), (1, 2)):
            noise = flat(held[n])
            value = cross(x[0], noise) - half_squares(noise)
            out[block - 2 * half, near_place(at, 2, r)[1]] += value[:, :128]
            out[block - 2 * half, near_place(at, 2, r + 1)[1]] += value[:, 128:]


def third_kernel(at, x, f_a, f_b, keep, give, held, sems):
    copies = started(sems, *((p, held.at[n]) for n, p in enumerate((f_a, f_b))))
    for copy in copies:
        copy.wait()
    for block in range(4):
        r = lax.rem(2 * at[4] + block - at[0] + 4, 4)
        noise = held[r // 2, lax.rem(r, 2)]
        (keep, give)[block // 2][block % 2] = cross(x[1], noise) - half_squares(noise)


def weights_of(at, weights, place, own_rows):
    rows = weights.shape[2] // 2
    to_l = at[2] if own_rows else 1 - at[2]
    here = pl.ds(pl.multiple_of(to_l * rows, rows), rows)
    parts = []
    for k, rs in ((0, range(4)), (1, range(4)), (3, range(4)), (2, (0, 1)), (2, (2, 3))):
        blocks = [place(at, k, r) for r in rs]
        parts.append(
            jnp.concatenate([weights[block[0], block[1], here] for block in blocks], axis=1)
        )
    total = 0.0
    for value in parts:
        total = total + cross(jnp.ones((16, value.shape[1]), jnp.bfloat16), value)
    return parts, total[:1]


STEP = 256


def product(parts, noise, first):
    span = slice(first, first + STEP)
    return sum(dot(w, flat(p[:, :, span])) for w, p in zip(parts, noise))


def target_1_kernel(at, weights, p0, p1, p3, p2_a, p2_b, low, high):
    parts, total = weights_of(at, weights, far_place, True)
    mid = low.shape[0] - 16
    for first in range(0, p0.shape[-1], STEP):
        value = product(parts, (p0, p1, p3, p2_a, p2_b), first)
        low[:mid, first : first + STEP] = value[:mid].astype(low.dtype)
        high[:mid, first : first + STEP] = value[mid:].astype(high.dtype)
    for n, out in enumerate((low, high)):
        out[mid:, :] = jnp.zeros((16, out.shape[1]), out.dtype)
        out[mid:, :mid] = terms_in_rows(total[:, n * mid : n * mid + mid])


def target_2_kernel(
    place, half, at, weights, p0, p1, p3, p2_a, p2_b, message, values, row_total
):
    parts, total = weights_of(at, weights, place, False)
    mid = values.shape[0]
    kept, sent = (slice(n * mid, n * mid + mid) for n in (half, 1 - half))
    for first in range(0, p0.shape[-1], STEP):
        value = product(parts, (p0, p1, p3, p2_a, p2_b), first)
        message[:, first : first + STEP] = value[sent].astype(message.dtype)
        values[:, first : first + STEP] = value[kept]
    row_total[...] = jnp.broadcast_to(total, row_total.shape)


def target_3_kernel(at, weights, p0, p1, p3, p2_a, p2_b, values, row_total):
    parts, total = weights_of(at, weights, near_place, True)
    for first in range(0, p0.shape[-1], STEP):
        values[:, first : first + STEP] = product(parts, (p0, p1, p3, p2_a, p2_b), first)
    row_total[...] = jnp.broadcast_to(total, row_total.shape)


def add_kernel(half, at, values, row_total, came, out):
    mid = values.shape[0]
    out[:mid, :] = (values[...] + came[:mid].astype(jnp.float32)).astype(out.dtype)
    terms = came[mid:, :mid].astype(jnp.float32)
    total = [row_total[:1, :mid], row_total[:1, mid:]]
    total[half] = total[half] + terms[0:1] + terms[1:2] + terms[2:3]
    out[mid:, :] = jnp.zeros((16, out.shape[1]), out.dtype)
    out[mid:, : 2 * mid] = terms_in_rows(jnp.concatenate(total, axis=1))


def last_kernel(at, own, own_total, l_low, l_high, lh_low, lh_high, out):
    mid = own.shape[0] // 2
    terms = [m[mid:, : 2 * mid] for m in (l_high, lh_low)]
    total = to_rows(jnp.concatenate([terms_in_rows(own_total[:1])] + terms, axis=0))
    for n, messages in enumerate(((l_low, lh_low), (l_high, lh_high))):
        here = slice(n * mid, n * mid + mid)
        for column in range(0, own.shape[1], 128):
            span = slice(column, column + 128)
            value = own[here, span]
            for m in messages:
                value = value + m[:mid, span].astype(jnp.float32)
            out[here, span] = (value / total[here]).astype(out.dtype)


TILE = 64


def rows_1_kernel(scale, at, keep, got, far_keep, far_got, score, sent, tops, sums):
    blocks = keep.shape[0]
    late = lax.rem(at[1] + 2, 4)

    @pl.loop(0, keep.shape[1] // TILE)
    def _(t):
        here = pl.ds(pl.multiple_of(t * TILE, TILE), TILE)
        for b in range(blocks):
            score[b, here] = (keep[b, here] + got[b, here]) * scale
        for b in range(2):
            score[4 * b + late, here] += (far_keep[b, here] + far_got[b, here]) * scale
        top = functools.reduce(jnp.maximum, [score[b, here] for b in range(blocks)])
        top = jnp.broadcast_to(jnp.max(top, axis=1, keepdims=True), top.shape)
        tops[here] = top
        sums[here] = sum(jnp.exp(score[b, here] - top) for b in range(blocks))

    log_row = first_lanes(tops[...]) + jnp.log(lane_sums(sums[...]))
    for n in range(sent.shape[0]):
        sent[n] = log_row


def columns_1_kernel(log_count, at, came, score, row_pot, sent):
    pot = -log_count - log_sum_exp([came[n] for n in range(came.shape[0])])
    row_pot[...] = to_rows(terms_in_rows(pot))
    logs = []
    for b in range(score.shape[0]):
        value = score[b] + row_pot[...]
        top = jnp.max(value, axis=0, keepdims=True)
        total = jnp.sum(jnp.exp(value - top), axis=0, keepdims=True)
        logs.append(top + jnp.log(total))
    logs = jnp.concatenate(logs)
    for n in range(sent.shape[0]):
        sent[n] = logs


def rows_2_kernel(at, came, score, row_pot, plan, sent, sums):
    pot = -log_sum_exp([came[n] for n in range(came.shape[0])])

    @pl.loop(0, score.shape[1] // TILE)
    def _(t):
        here = pl.ds(pl.multiple_of(t * TILE, TILE), TILE)
        total = 0.0
        for b in range(score.shape[0]):
            value = score[b, here] + row_pot[here] + pot[b : b + 1]
            value = jnp.exp(jnp.minimum(value, 0.0))
            plan[b, here] = value
            total = total + value
        sums[here] = total

    row_sum = lane_sums(sums[...])
    for n in range(sent.shape[0]):
        sent[n] = row_sum


def columns_2_kernel(least, at, came, plan, row_scale, sent):
    total = sum(came[n] for n in range(came.shape[0]))
    row_scale[...] = to_rows(terms_in_rows(1.0 / jnp.maximum(total, least)))
    sums = []
    for b in range(plan.shape[0]):
        sums.append(jnp.sum(plan[b] * row_scale[...], axis=0, keepdims=True))
    sums = jnp.concatenate(sums)
    for n in range(sent.shape[0]):
        sent[n] = sums


def weights_kernel(least, at, came, plan, other, row_scale, weights):
    c = at[4]
    mine = sum(came[2 * n + c] for n in range(came.shape[0] // 2))
    theirs = sum(came[2 * n + 1 - c] for n in range(came.shape[0] // 2))
    for half, (values, total) in enumerate(((plan, mine), (other, theirs))):
        scale = 1.0 / jnp.maximum(total, least)
        for b in range(values.shape[0]):
            value = values[b] * row_scale[...] * scale[b : b + 1]
            weights[values.shape[0] * half + b] = value.astype(weights.dtype)


def per_device(data_rows, noise_rows):
    z, y, l, h, c = (lax.axis_index(name) for name in AXES)
    rows, part = data_rows.shape
    width = part * 4
    count = rows * 32
    eps = 0.64 / math.sqrt(width)
    log_count = math.log(count)
    piece = rows // 4

    def float32(*shape):
        return jax.ShapeDtypeStruct(shape, jnp.float32)

    def bfloat16(*shape):
        return jax.ShapeDtypeStruct(shape, jnp.bfloat16)

    at = jnp.stack([z, y, l, h, c])

    wave = lax.optimization_barrier
    mid = rows // 2
    near = lax.dynamic_slice_in_dim(noise_rows, h * mid, mid)
    far = flip(lax.dynamic_slice_in_dim(noise_rows, (1 - h) * mid, mid), "h")
    near_1, near_3 = from_y(near, 1), from_y(near, 3)
    far, data_rows = wave((far, data_rows))
    data_l = flip(data_rows, "l")
    near_2 = from_y(near_1, 1)
    near_3, far_1, far_3, data_rows = wave((near_3, from_z(far, 1), from_z(far, 3), data_rows))
    data_lh = flip(data_rows, "lh")
    far_2, data_l, data_rows = wave((from_z(far, 2), data_l, data_rows))
    sems = pltpu.SemaphoreType.DMA((4,))

    def stacked(*blocks):
        out = [bfloat16(4, *blocks[0].shape)]
        return call(
            stack_kernel, out, 0, at, *blocks, anywhere=4, spaces=pl.ANY, scratch=[sems]
        )[0]

    def halves(next_, last):
        out = [bfloat16(2, *next_.shape[1:])] * 2
        return call(
            halves_kernel, out, 0, at, next_, last, anywhere=2, spaces=pl.ANY, scratch=[sems]
        )

    near, far = stacked(near, near_1, near_2, near_3), stacked(far, far_1, far_2, far_3)
    near_next, near_last = from_z(near, 1), from_z(near, 3)
    far_next, far_last = from_y(far, 1), from_y(far, 3)
    data_lh, data_rows = wave((data_lh, data_rows))
    data_h = flip(data_rows, "h")
    far_next, far_last, data_h = wave((far_next, far_last, data_h))
    nears, fars = (near, near_next, near_last), (far, far_next, far_last)
    low, high = halves(near_next, near_last)
    near_two = from_z(low, 1), from_z(high, 3)
    low, high = halves(far_next, far_last)
    far_two = from_y(low, 1), from_y(high, 3)

    one = 2 * 2 * rows * part * 2 * 2 * piece
    noise_shape = 4, 2 * piece, part
    scores, x_all = call(
        first_kernel,
        [float32(4, 4, 2 * rows, 2 * piece), bfloat16(2, 2 * rows, part)],
        12 * one,
        *(at, data_rows, data_l, data_h, data_lh, *nears, *fars),
        anywhere=10,
        scratch=[pltpu.VMEM((6, *noise_shape), jnp.bfloat16), pltpu.SemaphoreType.DMA((10,))],
    )
    give, keep = (
        call(
            functools.partial(second_kernel, half),
            [float32(2, 4, 2 * rows, 2 * piece)],
            100 * one,
            *(at, x_all, scores, *near_two),
            anywhere=2,
            scratch=[pltpu.VMEM((2, 2, *noise_shape[1:]), jnp.bfloat16), sems],
        )[0]
        for half in (1, 0)
    )
    far_keep, far_give = call(
        third_kernel,
        [float32(2, 2 * rows, 2 * piece)] * 2,
        2 * one,
        *(at, x_all, *far_two),
        anywhere=2,
        scratch=[pltpu.VMEM((2, 2, *noise_shape[1:]), jnp.bfloat16), sems],
    )

    blocks = (8, 2 * rows, 2 * piece)
    tall = 2 * rows, 2 * piece
    least = 0.5 / count
    row_axes, col_axes = ("l", "h", "c"), ("z", "y")
    row_sent, col_sent = float32(8, 1, 2 * rows), float32(16, 8, 2 * piece)

    def exchange(sent, axes):
        return lax.all_to_all(sent, axes, 0, 0, tiled=True)

    keep, give = keep.reshape(blocks), give.reshape(blocks)
    kernel = functools.partial(rows_1_kernel, 2.0 / (width * eps))
    score, sent = call(
        kernel,
        [float32(*blocks), row_sent],
        0,
        *(at, keep, flip(give, "c"), far_keep, flip(far_give, "c")),
        scratch=[pltpu.VMEM(tall, jnp.float32)] * 2,
    )
    kernel = functools.partial(columns_1_kernel, log_count)
    row_pot, sent = call(
        kernel, [float32(*tall), col_sent], 0, at, exchange(sent, row_axes), score
    )
    plan, sent = call(
        rows_2_kernel,
        [float32(*blocks), row_sent],
        0,
        *(at, exchange(sent, col_axes), score, row_pot),
        scratch=[pltpu.VMEM(tall, jnp.float32)],
    )
    plan_other = flip(plan, "c")
    kernel = functools.partial(columns_2_kernel, least)
    col_sent = float32(32, 8, 2 * piece)
    row_scale, sent = call(
        kernel, [float32(*tall), col_sent], 0, at, exchange(sent, row_axes), plan
    )
    kernel = functools.partial(weights_kernel, least)
    (weights,) = call(
        kernel,
        [bfloat16(16, *blocks[1:])],
        0,
        *(at, exchange(sent, ("z", "y", "c")), plan, plan_other, row_scale),
    )
    weights = weights.reshape(4, 4, *blocks[1:])

    near_noise, far_noise = (*nears, *near_two), (*fars, *far_two)
    message = bfloat16(mid + 16, part)
    low, high = call(target_1_kernel, [message] * 2, 8 * one, at, weights, *far_noise)
    low, high = flip(low, "l"), flip(high, "lh")

    def other_rows(place, half, came, names):
        noise = near_noise if place is near_place else far_noise
        kernel = functools.partial(target_2_kernel, place, half)
        outs = [bfloat16(mid, part), float32(mid, part), float32(8, rows)]
        sent, *kept = call(kernel, outs, 8 * one, at, weights, *noise)
        added = call(functools.partial(add_kernel, half), [message], 0, at, *kept, came)[0]
        return flip(sent, names), flip(added, names)

    lh_high, lh_low = other_rows(far_place, 0, low, "lh")
    l_low, l_high = other_rows(near_place, 1, high, "l")
    own = call(
        target_3_kernel,
        [float32(rows, part), float32(8, rows)],
        64 * one,
        *(at, weights, *near_noise),
    )
    messages = l_low, l_high, lh_low, lh_high
    return call(last_kernel, [bfloat16(rows, part)], 0, at, *own, *messages)[0]


def solution(mesh):
    fine = Mesh(mesh.devices.reshape(SIZES), AXES)
    spec = P(("z", "y", "l"), ("h", "c"))
    return jax.shard_map(
        per_device, mesh=fine, in_specs=(spec, spec), out_specs=spec, check_vma=False
    )
```

```python
import functools
import itertools
import math

import jax
import jax.numpy as jnp
from jax import lax
from jax.experimental import pallas as pl
from jax.experimental.pallas import tpu as pltpu
from jax.sharding import Mesh, PartitionSpec as P

AXES = ("z", "y", "l", "h", "c")
SIZES = (4, 4, 2, 2, 2)


def index_of(*place):
    index = 0
    for n, a in zip(SIZES, place):
        index = index * n + a % n
    return index


def move(value, dest):
    places = itertools.product(*(range(n) for n in SIZES))
    pairs = [(index_of(*place), index_of(*dest(*place))) for place in places]
    return lax.ppermute(value, AXES, pairs)


def from_y(value, k):
    return move(value, lambda z, y, l, h, c: (z, y - k, l, h, c))


def from_z(value, k):
    return move(value, lambda z, y, l, h, c: (z - k, y, l, h, c))


def flip(value, names):
    return move(
        value,
        lambda *place: [1 - a if name in names else a for name, a in zip(AXES, place)],
    )


def cross(a, b):
    return lax.dot_general(a, b, (((1,), (1,)), ((), ())), preferred_element_type=jnp.float32)


def dot(a, b):
    return jnp.dot(a, b, preferred_element_type=jnp.float32)


def exact_terms(total):
    terms = []
    for _ in range(3):
        terms.append(total.astype(jnp.bfloat16))
        total = total - terms[-1].astype(jnp.float32)
    return terms


def flat(blocks):
    return blocks.reshape(-1, blocks.shape[-1])


def half_squares(rows):
    sums = 0.0
    for at in range(0, rows.shape[1], 128):
        wide = rows[:, at : at + 128].astype(jnp.float32)
        sums = sums + wide * wide
    ones = jnp.full((16, 128), 0.5, jnp.bfloat16)
    return sum(cross(ones, term) for term in exact_terms(sums))[:1]


def call(kernel, outs, flops, *args, anywhere=0, spaces=None, scratch=()):
    moved = sum(a.size * a.dtype.itemsize for a in (*args, *outs))
    inner = len(args) - 1 - anywhere
    return pl.pallas_call(
        kernel,
        out_shape=outs,
        in_specs=[pl.BlockSpec(memory_space=pltpu.SMEM)]
        + [pl.BlockSpec(memory_space=pltpu.VMEM)] * inner
        + [pl.BlockSpec(memory_space=pl.ANY)] * anywhere,
        out_specs=[pl.BlockSpec(memory_space=spaces or pltpu.VMEM)] * len(outs),
        scratch_shapes=scratch,
        compiler_params=pltpu.CompilerParams(vmem_limit_bytes=20 * 2**20),
        cost_estimate=pl.CostEstimate(flops=flops, bytes_accessed=moved, transcendentals=0),
    )(*args)


def started(sems, *pairs):
    copies = [pltpu.make_async_copy(a, b, sems.at[n]) for n, (a, b) in enumerate(pairs)]
    for copy in copies:
        copy.start()
    return copies


def terms_in_rows(vec):
    row = lax.broadcasted_iota(jnp.int32, (16, vec.shape[1]), 0)
    terms = jnp.zeros(row.shape, jnp.float32)
    for n, term in enumerate(exact_terms(vec)):
        terms = jnp.where(row == n, term.astype(jnp.float32), terms)
    return terms.astype(jnp.bfloat16)


def to_rows(terms):
    ones = jnp.ones((terms.shape[0], 128), jnp.bfloat16)
    return lax.dot_general(
        terms, ones, (((0,), (0,)), ((), ())), preferred_element_type=jnp.float32
    )


def lane_sums(values):
    ones = jnp.ones((16, 128), jnp.bfloat16)
    return sum(cross(ones, term) for term in exact_terms(values))[:1]


def first_lanes(values):
    lane = lax.broadcasted_iota(jnp.int32, (16, 128), 1)
    pick = jnp.where(lane == 0, 1.0, 0.0).astype(jnp.bfloat16)
    return sum(cross(pick, term) for term in exact_terms(values))[:1]


def log_sum_exp(values):
    top = functools.reduce(jnp.maximum, values)
    return top + jnp.log(sum(jnp.exp(v - top) for v in values))


def stack_kernel(at, *refs):
    *blocks, out, sems = refs
    copies = started(sems, *((block, out.at[n]) for n, block in enumerate(blocks)))
    for copy in copies:
        copy.wait()


def halves_kernel(at, next_, last, low, high, sems):
    for copy in started(sems, (next_.at[:2], low), (last.at[2:], high)):
        copy.wait()


def near_place(at, k, r):
    return lax.rem(at[0] + k - 2 * at[4] + 4, 4), lax.rem(at[1] + r, 4)


def far_place(at, k, r):
    return lax.rem(at[0] + r - 2 * at[4] + 4, 4), lax.rem(at[1] + k, 4)


def first_kernel(at, *refs):
    data, noises, (out, x, held, sems) = refs[:4], refs[4:10], refs[10:]
    rows = data[0].shape[0]
    own, other = (pl.ds(pl.multiple_of(r * rows, rows), rows) for r in (at[2], 1 - at[2]))
    places = x.at[0, own], x.at[0, other], x.at[1, own], x.at[1, other]
    copies = started(
        sems, *zip(data, places), *((noise, held.at[n]) for n, noise in enumerate(noises))
    )
    for copy in copies[:4]:
        copy.wait()
    x_sq = 0.0
    for side in range(2):
        for span in range(0, x.shape[2], 128):
            wide = x[side, :, span : span + 128].astype(jnp.float32)
            x_sq = x_sq + wide * wide
    x_sq = jnp.broadcast_to(0.5 * jnp.sum(x_sq, axis=1, keepdims=True), x_sq.shape)
    for n, k in enumerate((0, 1, 3)):
        copies[4 + n].wait()
        for r in (0, 2):
            noise = flat(held[n, r : r + 2])
            value = cross(x[0], noise) - half_squares(noise)
            out[near_place(at, k, r)] = value[:, :128] - x_sq
            out[near_place(at, k, r + 1)] = value[:, 128:] - x_sq
    for r in range(4):
        out[near_place(at, 2, r)] = -x_sq
    for n, k in enumerate((0, 1, 3)):
        copies[7 + n].wait()
        for r in (0, 2):
            noise = flat(held[3 + n, r : r + 2])
            value = cross(x[1], noise) - half_squares(noise)
            out[far_place(at, k, r)] += value[:, :128]
            out[far_place(at, k, r + 1)] += value[:, 128:]


def second_kernel(half, at, x, acc, n_a, n_b, out, held, sems):
    copies = started(sems, *((p, held.at[n]) for n, p in enumerate((n_a, n_b))))
    for block in range(2):
        for j in range(4):
            out[block, j] = acc[2 * half + block, j]
    for copy in copies:
        copy.wait()
    block, _ = near_place(at, 2, 0)

    @pl.when((block >= 2) == bool(half))
    def _():
        for n, r in ((0, 0), (1, 2)):
            noise = flat(held[n])
            value = cross(x[0], noise) - half_squares(noise)
            out[block - 2 * half, near_place(at, 2, r)[1]] += value[:, :128]
            out[block - 2 * half, near_place(at, 2, r + 1)[1]] += value[:, 128:]


def third_kernel(at, x, f_a, f_b, keep, give, held, sems):
    copies = started(sems, *((p, held.at[n]) for n, p in enumerate((f_a, f_b))))
    for n, copy in enumerate(copies):
        copy.wait()
        noise = flat(held[n])
        value = cross(x[1], noise) - half_squares(noise)
        for side in range(2):
            block, _ = far_place(at, 2, 2 * n + side)
            part = value[:, 128 * side : 128 * side + 128]

            @pl.when(block < 2)
            def _():
                keep[block] = part

            @pl.when(block >= 2)
            def _():
                give[block - 2] = part


def weights_of(at, weights, place, own_rows):
    rows = weights.shape[2] // 2
    to_l = at[2] if own_rows else 1 - at[2]
    here = pl.ds(pl.multiple_of(to_l * rows, rows), rows)
    parts = []
    for k, rs in ((0, range(4)), (1, range(4)), (3, range(4)), (2, (0, 1)), (2, (2, 3))):
        blocks = [place(at, k, r) for r in rs]
        parts.append(
            jnp.concatenate([weights[block[0], block[1], here] for block in blocks], axis=1)
        )
    total = 0.0
    for value in parts:
        total = total + cross(jnp.ones((16, value.shape[1]), jnp.bfloat16), value)
    return parts, total[:1]


STEP = 256


def product(parts, noise, first):
    span = slice(first, first + STEP)
    return sum(dot(w, flat(p[:, :, span])) for w, p in zip(parts, noise))


def target_1_kernel(
    least, at, came, plan, other, row_scale, p0, p1, p3, p2_a, p2_b, weights, low, high
):
    c = at[4]
    mine = sum(came[2 * n + c] for n in range(came.shape[0] // 2))
    theirs = sum(came[2 * n + 1 - c] for n in range(came.shape[0] // 2))
    for half, (values, total) in enumerate(((plan, mine), (other, theirs))):
        scale = 1.0 / jnp.maximum(total, least)
        for b in range(values.shape[0]):
            value = values[b] * row_scale[...] * scale[b : b + 1]
            weights[2 * half + b // 4, b % 4] = value.astype(weights.dtype)
    parts, total = weights_of(at, weights, far_place, True)
    mid = low.shape[0] - 16
    for first in range(0, p0.shape[-1], STEP):
        value = product(parts, (p0, p1, p3, p2_a, p2_b), first)
        low[:mid, first : first + STEP] = value[:mid].astype(low.dtype)
        high[:mid, first : first + STEP] = value[mid:].astype(high.dtype)
    for n, out in enumerate((low, high)):
        out[mid:, :] = jnp.zeros((16, out.shape[1]), out.dtype)
        out[mid:, :mid] = terms_in_rows(total[:, n * mid : n * mid + mid])


def target_2_kernel(
    place, half, at, weights, p0, p1, p3, p2_a, p2_b, message, values, row_total
):
    parts, total = weights_of(at, weights, place, False)
    mid = values.shape[0]
    kept, sent = (slice(n * mid, n * mid + mid) for n in (half, 1 - half))
    for first in range(0, p0.shape[-1], STEP):
        value = product(parts, (p0, p1, p3, p2_a, p2_b), first)
        message[:, first : first + STEP] = value[sent].astype(message.dtype)
        values[:, first : first + STEP] = value[kept]
    row_total[...] = jnp.broadcast_to(total, row_total.shape)


def target_3_kernel(at, weights, p0, p1, p3, p2_a, p2_b, values, row_total):
    parts, total = weights_of(at, weights, near_place, True)
    for first in range(0, p0.shape[-1], STEP):
        values[:, first : first + STEP] = product(parts, (p0, p1, p3, p2_a, p2_b), first)
    row_total[...] = jnp.broadcast_to(total, row_total.shape)


def add_kernel(half, at, values, row_total, came, out):
    mid = values.shape[0]
    out[:mid, :] = (values[...] + came[:mid].astype(jnp.float32)).astype(out.dtype)
    terms = came[mid:, :mid].astype(jnp.float32)
    total = [row_total[:1, :mid], row_total[:1, mid:]]
    total[half] = total[half] + terms[0:1] + terms[1:2] + terms[2:3]
    out[mid:, :] = jnp.zeros((16, out.shape[1]), out.dtype)
    out[mid:, : 2 * mid] = terms_in_rows(jnp.concatenate(total, axis=1))


def last_kernel(at, own, own_total, l_low, l_high, lh_low, lh_high, out):
    mid = own.shape[0] // 2
    terms = [m[mid:, : 2 * mid] for m in (l_high, lh_low)]
    total = 1.0 / to_rows(jnp.concatenate([terms_in_rows(own_total[:1])] + terms, axis=0))
    for n, messages in enumerate(((l_low, lh_low), (l_high, lh_high))):
        here = slice(n * mid, n * mid + mid)
        for column in range(0, own.shape[1], 128):
            span = slice(column, column + 128)
            value = own[here, span]
            for m in messages:
                value = value + m[:mid, span].astype(jnp.float32)
            out[here, span] = (value * total[here]).astype(out.dtype)


TILE = 32


def rows_1_kernel(scale, at, keep, got, far_keep, far_got, score, sent, tops, sums):
    late = lax.rem(at[1] + 2, 4)
    scales = [jnp.where(late == j, scale, 0.0) for j in range(4)]

    @pl.loop(0, keep.shape[1] // TILE)
    def _(t):
        here = pl.ds(pl.multiple_of(t * TILE, TILE), TILE)
        far = [far_keep[b, here] + far_got[b, here] for b in range(2)]
        values = []
        for b in range(keep.shape[0]):
            value = (keep[b, here] + got[b, here]) * scale + far[b // 4] * scales[b % 4]
            score[b, here] = value
            values.append(value)
        top = functools.reduce(jnp.maximum, values)
        top = jnp.broadcast_to(jnp.max(top, axis=1, keepdims=True), top.shape)
        tops[here] = top
        sums[here] = sum(jnp.exp(value - top) for value in values)

    log_row = first_lanes(tops[...]) + jnp.log(lane_sums(sums[...]))
    for n in range(sent.shape[0]):
        sent[n] = log_row


def columns_1_kernel(log_count, at, came, score, row_pot, sent):
    pot = -log_count - log_sum_exp([came[n] for n in range(came.shape[0])])
    row_pot[...] = to_rows(terms_in_rows(pot))
    logs = []
    for b in range(score.shape[0]):
        value = score[b] + row_pot[...]
        top = jnp.max(value, axis=0, keepdims=True)
        total = jnp.sum(jnp.exp(value - top), axis=0, keepdims=True)
        logs.append(top + jnp.log(total))
    logs = jnp.concatenate(logs)
    for n in range(sent.shape[0]):
        sent[n] = logs


def rows_2_kernel(at, came, score, row_pot, plan, sent, sums):
    pot = -log_sum_exp([came[n] for n in range(came.shape[0])])

    @pl.loop(0, score.shape[1] // TILE)
    def _(t):
        here = pl.ds(pl.multiple_of(t * TILE, TILE), TILE)
        total = 0.0
        for b in range(score.shape[0]):
            value = score[b, here] + row_pot[here] + pot[b : b + 1]
            value = jnp.exp(jnp.minimum(value, 0.0))
            plan[b, here] = value
            total = total + value
        sums[here] = total

    row_sum = lane_sums(sums[...])
    for n in range(sent.shape[0]):
        sent[n] = row_sum


def columns_2_kernel(least, at, came, plan, row_scale, sent):
    total = sum(came[n] for n in range(came.shape[0]))
    row_scale[...] = to_rows(terms_in_rows(1.0 / jnp.maximum(total, least)))
    sums = []
    for b in range(plan.shape[0]):
        sums.append(jnp.sum(plan[b] * row_scale[...], axis=0, keepdims=True))
    sums = jnp.concatenate(sums)
    for n in range(sent.shape[0]):
        sent[n] = sums


def per_device(data_rows, noise_rows):
    z, y, l, h, c = (lax.axis_index(name) for name in AXES)
    rows, part = data_rows.shape
    width = part * 4
    count = rows * 32
    eps = 0.64 / math.sqrt(width)
    log_count = math.log(count)
    piece = rows // 4

    def float32(*shape):
        return jax.ShapeDtypeStruct(shape, jnp.float32)

    def bfloat16(*shape):
        return jax.ShapeDtypeStruct(shape, jnp.bfloat16)

    at = jnp.stack([z, y, l, h, c])

    wave = lax.optimization_barrier
    mid = rows // 2
    near = lax.dynamic_slice_in_dim(noise_rows, h * mid, mid)
    far = flip(lax.dynamic_slice_in_dim(noise_rows, (1 - h) * mid, mid), "h")
    near_1, near_3 = from_y(near, 1), from_y(near, 3)
    far, data_rows = wave((far, data_rows))
    data_l, data_lh = flip(data_rows, "l"), flip(data_rows, "lh")
    near_2 = from_y(near_1, 1)
    near_3, far_1, far_3 = wave((near_3, from_z(far, 1), from_z(far, 3)))
    far_2, data_l, data_lh, data_rows = wave((from_z(far_1, 1), data_l, data_lh, data_rows))
    sems = pltpu.SemaphoreType.DMA((4,))

    def stacked(*blocks):
        out = [bfloat16(4, *blocks[0].shape)]
        return call(
            stack_kernel, out, 0, at, *blocks, anywhere=4, spaces=pl.ANY, scratch=[sems]
        )[0]

    def halves(next_, last):
        out = [bfloat16(2, *next_.shape[1:])] * 2
        return call(
            halves_kernel, out, 0, at, next_, last, anywhere=2, spaces=pl.ANY, scratch=[sems]
        )

    near, far = stacked(near, near_1, near_2, near_3), stacked(far, far_1, far_2, far_3)
    near_next, near_last = from_z(near, 1), from_z(near, 3)
    far_next, far_last = from_y(far, 1), from_y(far, 3)
    data_h = flip(data_rows, "h")
    far_next, far_last, data_h = wave((far_next, far_last, data_h))
    nears, fars = (near, near_next, near_last), (far, far_next, far_last)
    low, high = halves(near_next, near_last)
    near_two = from_z(low, 1), from_z(high, 3)
    low, high = halves(far_next, far_last)
    far_two = from_y(low, 1), from_y(high, 3)

    one = 2 * 2 * rows * part * 2 * 2 * piece
    noise_shape = 4, 2 * piece, part
    scores, x_all = call(
        first_kernel,
        [float32(4, 4, 2 * rows, 2 * piece), bfloat16(2, 2 * rows, part)],
        12 * one,
        *(at, data_rows, data_l, data_h, data_lh, *nears, *fars),
        anywhere=10,
        scratch=[pltpu.VMEM((6, *noise_shape), jnp.bfloat16), pltpu.SemaphoreType.DMA((10,))],
    )
    give, keep = (
        call(
            functools.partial(second_kernel, half),
            [float32(2, 4, 2 * rows, 2 * piece)],
            100 * one,
            *(at, x_all, scores, *near_two),
            anywhere=2,
            scratch=[pltpu.VMEM((2, 2, *noise_shape[1:]), jnp.bfloat16), sems],
        )[0]
        for half in (1, 0)
    )
    far_keep, far_give = call(
        third_kernel,
        [float32(2, 2 * rows, 2 * piece)] * 2,
        2 * one,
        *(at, x_all, *far_two),
        anywhere=2,
        scratch=[pltpu.VMEM((2, 2, *noise_shape[1:]), jnp.bfloat16), sems],
    )

    blocks = (8, 2 * rows, 2 * piece)
    tall = 2 * rows, 2 * piece
    least = 0.5 / count
    row_axes, col_axes = ("l", "h", "c"), ("z", "y")
    row_sent, col_sent = float32(8, 1, 2 * rows), float32(16, 8, 2 * piece)

    def exchange(sent, axes):
        return lax.all_to_all(sent, axes, 0, 0, tiled=True)

    keep, give = keep.reshape(blocks), give.reshape(blocks)
    kernel = functools.partial(rows_1_kernel, 2.0 / (width * eps))
    score, sent = call(
        kernel,
        [float32(*blocks), row_sent],
        0,
        *(at, keep, flip(give, "c"), far_keep, flip(far_give, "c")),
        scratch=[pltpu.VMEM(tall, jnp.float32)] * 2,
    )
    kernel = functools.partial(columns_1_kernel, log_count)
    row_pot, sent = call(
        kernel, [float32(*tall), col_sent], 0, at, exchange(sent, row_axes), score
    )
    plan, sent = call(
        rows_2_kernel,
        [float32(*blocks), row_sent],
        0,
        *(at, exchange(sent, col_axes), score, row_pot),
        scratch=[pltpu.VMEM(tall, jnp.float32)],
    )
    plan_other = flip(plan, "c")
    kernel = functools.partial(columns_2_kernel, least)
    col_sent = float32(32, 8, 2 * piece)
    row_scale, sent = call(
        kernel, [float32(*tall), col_sent], 0, at, exchange(sent, row_axes), plan
    )
    near_noise, far_noise = (*nears, *near_two), (*fars, *far_two)
    message = bfloat16(mid + 16, part)
    weights, low, high = call(
        functools.partial(target_1_kernel, least),
        [bfloat16(4, 4, *blocks[1:]), message, message],
        8 * one,
        *(at, exchange(sent, ("z", "y", "c")), plan, plan_other, row_scale, *far_noise),
    )
    low, high = flip(low, "l"), flip(high, "lh")

    def other_rows(place, half, came, names):
        noise = near_noise if place is near_place else far_noise
        kernel = functools.partial(target_2_kernel, place, half)
        outs = [bfloat16(mid, part), float32(mid, part), float32(8, rows)]
        sent, *kept = call(kernel, outs, 8 * one, at, weights, *noise)
        added = call(functools.partial(add_kernel, half), [message], 0, at, *kept, came)[0]
        return flip(sent, names), flip(added, names)

    lh_high, lh_low = other_rows(far_place, 0, low, "lh")
    l_low, l_high = other_rows(near_place, 1, high, "l")
    own = call(
        target_3_kernel,
        [float32(rows, part), float32(8, rows)],
        64 * one,
        *(at, weights, *near_noise),
    )
    messages = l_low, l_high, lh_low, lh_high
    return call(last_kernel, [bfloat16(rows, part)], 0, at, *own, *messages)[0]


def solution(mesh):
    fine = Mesh(mesh.devices.reshape(SIZES), AXES)
    spec = P(("z", "y", "l"), ("h", "c"))
    return jax.shard_map(
        per_device, mesh=fine, in_specs=(spec, spec), out_specs=spec, check_vma=False
    )
```

```python
import functools
import itertools
import math

import jax
import jax.numpy as jnp
from jax import lax
from jax.experimental import pallas as pl
from jax.experimental.pallas import tpu as pltpu
from jax.sharding import Mesh, PartitionSpec as P

AXES = ("z", "y", "l", "h", "c")
SIZES = (4, 4, 2, 2, 2)


def index_of(*place):
    index = 0
    for n, a in zip(SIZES, place):
        index = index * n + a % n
    return index


def move(value, dest):
    places = itertools.product(*(range(n) for n in SIZES))
    pairs = [(index_of(*place), index_of(*dest(*place))) for place in places]
    return lax.ppermute(value, AXES, pairs)


def from_y(value, k):
    return move(value, lambda z, y, l, h, c: (z, y - k, l, h, c))


def from_z(value, k):
    return move(value, lambda z, y, l, h, c: (z - k, y, l, h, c))


def flip(value, names):
    return move(
        value,
        lambda *place: [1 - a if name in names else a for name, a in zip(AXES, place)],
    )


def cross(a, b):
    return lax.dot_general(a, b, (((1,), (1,)), ((), ())), preferred_element_type=jnp.float32)


def dot(a, b):
    return jnp.dot(a, b, preferred_element_type=jnp.float32)


def exact_terms(total):
    terms = []
    for _ in range(3):
        terms.append(total.astype(jnp.bfloat16))
        total = total - terms[-1].astype(jnp.float32)
    return terms


def flat(blocks):
    return blocks.reshape(-1, blocks.shape[-1])


def half_squares(rows):
    sums = 0.0
    for at in range(0, rows.shape[1], 128):
        wide = rows[:, at : at + 128].astype(jnp.float32)
        sums = sums + wide * wide
    ones = jnp.full((16, 128), 0.5, jnp.bfloat16)
    return sum(cross(ones, term) for term in exact_terms(sums))[:1]


def call(kernel, outs, flops, *args, anywhere=0, spaces=None, scratch=()):
    moved = sum(a.size * a.dtype.itemsize for a in (*args, *outs))
    inner = len(args) - 1 - anywhere
    return pl.pallas_call(
        kernel,
        out_shape=outs,
        in_specs=[pl.BlockSpec(memory_space=pltpu.SMEM)]
        + [pl.BlockSpec(memory_space=pltpu.VMEM)] * inner
        + [pl.BlockSpec(memory_space=pl.ANY)] * anywhere,
        out_specs=[pl.BlockSpec(memory_space=spaces or pltpu.VMEM)] * len(outs),
        scratch_shapes=scratch,
        compiler_params=pltpu.CompilerParams(vmem_limit_bytes=20 * 2**20),
        cost_estimate=pl.CostEstimate(flops=flops, bytes_accessed=moved, transcendentals=0),
    )(*args)


def started(sems, *pairs):
    copies = [pltpu.make_async_copy(a, b, sems.at[n]) for n, (a, b) in enumerate(pairs)]
    for copy in copies:
        copy.start()
    return copies


def terms_in_rows(vec):
    row = lax.broadcasted_iota(jnp.int32, (16, vec.shape[1]), 0)
    terms = jnp.zeros(row.shape, jnp.float32)
    for n, term in enumerate(exact_terms(vec)):
        terms = jnp.where(row == n, term.astype(jnp.float32), terms)
    return terms.astype(jnp.bfloat16)


def to_rows(terms):
    ones = jnp.ones((terms.shape[0], 128), jnp.bfloat16)
    return lax.dot_general(
        terms, ones, (((0,), (0,)), ((), ())), preferred_element_type=jnp.float32
    )


def lane_sums(values):
    ones = jnp.ones((16, 128), jnp.bfloat16)
    return sum(cross(ones, term) for term in exact_terms(values))[:1]


def first_lanes(values):
    lane = lax.broadcasted_iota(jnp.int32, (16, 128), 1)
    pick = jnp.where(lane == 0, 1.0, 0.0).astype(jnp.bfloat16)
    return sum(cross(pick, term) for term in exact_terms(values))[:1]


def log_sum_exp(values):
    top = functools.reduce(jnp.maximum, values)
    return top + jnp.log(sum(jnp.exp(v - top) for v in values))


def stack_kernel(at, *refs):
    *blocks, out, sems = refs
    copies = started(sems, *((block, out.at[n]) for n, block in enumerate(blocks)))
    for copy in copies:
        copy.wait()


def halves_kernel(at, next_, last, low, high, sems):
    for copy in started(sems, (next_.at[:2], low), (last.at[2:], high)):
        copy.wait()


def near_place(at, k, r):
    return lax.rem(at[0] + k - 2 * at[4] + 4, 4), lax.rem(at[1] + r, 4)


def far_place(at, k, r):
    return lax.rem(at[0] + r - 2 * at[4] + 4, 4), lax.rem(at[1] + k, 4)


def first_kernel(at, *refs):
    data, noises, (out, x, held, sems) = refs[:4], refs[4:10], refs[10:]
    rows = data[0].shape[0]
    own, other = (pl.ds(pl.multiple_of(r * rows, rows), rows) for r in (at[2], 1 - at[2]))
    places = x.at[0, own], x.at[0, other], x.at[1, own], x.at[1, other]
    copies = started(
        sems, *zip(data, places), *((noise, held.at[n]) for n, noise in enumerate(noises))
    )
    for copy in copies[:4]:
        copy.wait()
    for n, k in enumerate((0, 1, 3)):
        copies[4 + n].wait()
        for r in (0, 2):
            noise = flat(held[n, r : r + 2])
            value = cross(x[0], noise) - half_squares(noise)
            out[near_place(at, k, r)] = value[:, :128]
            out[near_place(at, k, r + 1)] = value[:, 128:]
    x_sq = 0.0
    for side in range(2):
        for span in range(0, x.shape[2], 128):
            wide = x[side, :, span : span + 128].astype(jnp.float32)
            x_sq = x_sq + wide * wide
    x_sq = jnp.broadcast_to(0.5 * jnp.sum(x_sq, axis=1, keepdims=True), x_sq.shape)
    for r in range(4):
        out[near_place(at, 2, r)] = -x_sq
    for n, k in enumerate((0, 1, 3)):
        copies[7 + n].wait()
        for r in (0, 2):
            noise = flat(held[3 + n, r : r + 2])
            value = cross(x[1], noise) - half_squares(noise)
            out[far_place(at, k, r)] += value[:, :128]
            out[far_place(at, k, r + 1)] += value[:, 128:]
    for n, k in enumerate((0, 1, 3)):
        for r in range(4):
            out[near_place(at, k, r)] -= x_sq


def second_kernel(half, at, x, acc, n_a, n_b, out, held, sems):
    copies = started(sems, *((p, held.at[n]) for n, p in enumerate((n_a, n_b))))
    for block in range(2):
        for j in range(4):
            out[block, j] = acc[2 * half + block, j]
    for copy in copies:
        copy.wait()
    block, _ = near_place(at, 2, 0)

    @pl.when((block >= 2) == bool(half))
    def _():
        for n, r in ((0, 0), (1, 2)):
            noise = flat(held[n])
            value = cross(x[0], noise) - half_squares(noise)
            out[block - 2 * half, near_place(at, 2, r)[1]] += value[:, :128]
            out[block - 2 * half, near_place(at, 2, r + 1)[1]] += value[:, 128:]


def third_kernel(at, x, f_a, f_b, keep, give, held, sems):
    copies = started(sems, *((p, held.at[n]) for n, p in enumerate((f_a, f_b))))
    for n, copy in enumerate(copies):
        copy.wait()
        noise = flat(held[n])
        value = cross(x[1], noise) - half_squares(noise)
        for side in range(2):
            block, _ = far_place(at, 2, 2 * n + side)
            part = value[:, 128 * side : 128 * side + 128]

            @pl.when(block < 2)
            def _():
                keep[block] = part

            @pl.when(block >= 2)
            def _():
                give[block - 2] = part


def weights_of(at, weights, place, own_rows):
    rows = weights.shape[2] // 2
    to_l = at[2] if own_rows else 1 - at[2]
    here = pl.ds(pl.multiple_of(to_l * rows, rows), rows)
    parts = []
    for k, rs in ((0, range(4)), (1, range(4)), (3, range(4)), (2, (0, 1)), (2, (2, 3))):
        blocks = [place(at, k, r) for r in rs]
        parts.append(
            jnp.concatenate([weights[block[0], block[1], here] for block in blocks], axis=1)
        )
    total = 0.0
    for value in parts:
        total = total + cross(jnp.ones((16, value.shape[1]), jnp.bfloat16), value)
    return parts, total[:1]


STEP = 256


def product(parts, noise, first):
    span = slice(first, first + STEP)
    return sum(dot(w, flat(p[:, :, span])) for w, p in zip(parts, noise))


def target_1_kernel(
    least, at, came, plan, other, row_scale, p0, p1, p3, p2_a, p2_b, weights, low, high
):
    c = at[4]
    mine = sum(came[2 * n + c] for n in range(came.shape[0] // 2))
    theirs = sum(came[2 * n + 1 - c] for n in range(came.shape[0] // 2))
    for half, (values, total) in enumerate(((plan, mine), (other, theirs))):
        scale = 1.0 / jnp.maximum(total, least)
        for b in range(values.shape[0]):
            value = values[b] * row_scale[...] * scale[b : b + 1]
            weights[2 * half + b // 4, b % 4] = value.astype(weights.dtype)
    parts, total = weights_of(at, weights, far_place, True)
    mid = low.shape[0] - 16
    for first in range(0, p0.shape[-1], STEP):
        value = product(parts, (p0, p1, p3, p2_a, p2_b), first)
        low[:mid, first : first + STEP] = value[:mid].astype(low.dtype)
        high[:mid, first : first + STEP] = value[mid:].astype(high.dtype)
    for n, out in enumerate((low, high)):
        out[mid:, :] = jnp.zeros((16, out.shape[1]), out.dtype)
        out[mid:, :mid] = terms_in_rows(total[:, n * mid : n * mid + mid])


def target_2_kernel(
    place, half, at, weights, p0, p1, p3, p2_a, p2_b, message, values, row_total
):
    parts, total = weights_of(at, weights, place, False)
    mid = values.shape[0]
    kept, sent = (slice(n * mid, n * mid + mid) for n in (half, 1 - half))
    for first in range(0, p0.shape[-1], STEP):
        value = product(parts, (p0, p1, p3, p2_a, p2_b), first)
        message[:, first : first + STEP] = value[sent].astype(message.dtype)
        values[:, first : first + STEP] = value[kept]
    row_total[...] = jnp.broadcast_to(total, row_total.shape)


def target_3_kernel(at, weights, p0, p1, p3, p2_a, p2_b, values, row_total):
    parts, total = weights_of(at, weights, near_place, True)
    for first in range(0, p0.shape[-1], STEP):
        values[:, first : first + STEP] = product(parts, (p0, p1, p3, p2_a, p2_b), first)
    row_total[...] = jnp.broadcast_to(total, row_total.shape)


def add_kernel(half, at, values, row_total, came, out):
    mid = values.shape[0]
    out[:mid, :] = (values[...] + came[:mid].astype(jnp.float32)).astype(out.dtype)
    terms = came[mid:, :mid].astype(jnp.float32)
    total = [row_total[:1, :mid], row_total[:1, mid:]]
    total[half] = total[half] + terms[0:1] + terms[1:2] + terms[2:3]
    out[mid:, :] = jnp.zeros((16, out.shape[1]), out.dtype)
    out[mid:, : 2 * mid] = terms_in_rows(jnp.concatenate(total, axis=1))


def last_kernel(at, own, own_total, l_low, l_high, lh_low, lh_high, out):
    mid = own.shape[0] // 2
    terms = [m[mid:, : 2 * mid] for m in (l_high, lh_low)]
    total = 1.0 / to_rows(jnp.concatenate([terms_in_rows(own_total[:1])] + terms, axis=0))
    for n, messages in enumerate(((l_low, lh_low), (l_high, lh_high))):
        here = slice(n * mid, n * mid + mid)
        for column in range(0, own.shape[1], 128):
            span = slice(column, column + 128)
            value = own[here, span]
            for m in messages:
                value = value + m[:mid, span].astype(jnp.float32)
            out[here, span] = (value * total[here]).astype(out.dtype)


TILE = 64


def rows_1_kernel(scale, at, keep, got, far_keep, far_got, score, sent, tops, sums):
    late = lax.rem(at[1] + 2, 4)
    scales = [jnp.where(late == j, scale, 0.0) for j in range(4)]
    blocks = range(keep.shape[0])

    @pl.loop(0, keep.shape[1] // TILE)
    def _(t):
        here = pl.ds(pl.multiple_of(t * TILE, TILE), TILE)
        far = [far_keep[b, here] + far_got[b, here] for b in range(2)]
        top = None
        for b in blocks:
            value = (keep[b, here] + got[b, here]) * scale + far[b // 4] * scales[b % 4]
            score[b, here] = value
            top = value if top is None else jnp.maximum(top, value)
        tops[here] = top

    tops[...] = jnp.broadcast_to(jnp.max(tops[...], axis=1, keepdims=True), tops.shape)

    @pl.loop(0, keep.shape[1] // TILE)
    def _(t):
        here = pl.ds(pl.multiple_of(t * TILE, TILE), TILE)
        top = tops[here]
        sums[here] = sum(jnp.exp(score[b, here] - top) for b in blocks)

    log_row = first_lanes(tops[...]) + jnp.log(lane_sums(sums[...]))
    for n in range(sent.shape[0]):
        sent[n] = log_row


def columns_1_kernel(log_count, at, came, score, row_pot, sent):
    pot = -log_count - log_sum_exp([came[n] for n in range(came.shape[0])])
    row_pot[...] = to_rows(terms_in_rows(pot))
    logs = []
    for b in range(score.shape[0]):
        value = score[b] + row_pot[...]
        top = jnp.max(value, axis=0, keepdims=True)
        total = jnp.sum(jnp.exp(value - top), axis=0, keepdims=True)
        logs.append(top + jnp.log(total))
    logs = jnp.concatenate(logs)
    for n in range(sent.shape[0]):
        sent[n] = logs


def rows_2_kernel(at, came, score, row_pot, plan, sent, sums):
    pot = -log_sum_exp([came[n] for n in range(came.shape[0])])

    @pl.loop(0, score.shape[1] // TILE)
    def _(t):
        here = pl.ds(pl.multiple_of(t * TILE, TILE), TILE)
        total = 0.0
        for b in range(score.shape[0]):
            value = score[b, here] + row_pot[here] + pot[b : b + 1]
            value = jnp.exp(jnp.minimum(value, 0.0))
            plan[b, here] = value
            total = total + value
        sums[here] = total

    row_sum = lane_sums(sums[...])
    for n in range(sent.shape[0]):
        sent[n] = row_sum


def columns_2_kernel(least, at, came, plan, row_scale, sent):
    total = sum(came[n] for n in range(came.shape[0]))
    row_scale[...] = to_rows(terms_in_rows(1.0 / jnp.maximum(total, least)))
    sums = []
    for b in range(plan.shape[0]):
        sums.append(jnp.sum(plan[b] * row_scale[...], axis=0, keepdims=True))
    sums = jnp.concatenate(sums)
    for n in range(sent.shape[0]):
        sent[n] = sums


def per_device(data_rows, noise_rows):
    z, y, l, h, c = (lax.axis_index(name) for name in AXES)
    rows, part = data_rows.shape
    width = part * 4
    count = rows * 32
    eps = 0.64 / math.sqrt(width)
    log_count = math.log(count)
    piece = rows // 4

    def float32(*shape):
        return jax.ShapeDtypeStruct(shape, jnp.float32)

    def bfloat16(*shape):
        return jax.ShapeDtypeStruct(shape, jnp.bfloat16)

    at = jnp.stack([z, y, l, h, c])

    wave = lax.optimization_barrier
    mid = rows // 2
    near = lax.dynamic_slice_in_dim(noise_rows, h * mid, mid)
    far = flip(lax.dynamic_slice_in_dim(noise_rows, (1 - h) * mid, mid), "h")
    near_1, near_3 = from_y(near, 1), from_y(near, 3)
    far, data_rows = wave((far, data_rows))
    data_l = flip(data_rows, "l")
    near_2 = from_y(near_1, 1)
    near_3, far_1, far_3, data_rows = wave((near_3, from_z(far, 1), from_z(far, 3), data_rows))
    data_lh = flip(data_rows, "lh")
    far_2, data_l, data_rows = wave((from_z(far_1, 1), data_l, data_rows))
    sems = pltpu.SemaphoreType.DMA((4,))

    def stacked(*blocks):
        out = [bfloat16(4, *blocks[0].shape)]
        return call(
            stack_kernel, out, 0, at, *blocks, anywhere=4, spaces=pl.ANY, scratch=[sems]
        )[0]

    def halves(next_, last):
        out = [bfloat16(2, *next_.shape[1:])] * 2
        return call(
            halves_kernel, out, 0, at, next_, last, anywhere=2, spaces=pl.ANY, scratch=[sems]
        )

    near, far = stacked(near, near_1, near_2, near_3), stacked(far, far_1, far_2, far_3)
    near_next, near_last = from_z(near, 1), from_z(near, 3)
    far_next, far_last = from_y(far, 1), from_y(far, 3)
    data_lh, data_rows = wave((data_lh, data_rows))
    data_h = flip(data_rows, "h")
    far_next, far_last, data_h = wave((far_next, far_last, data_h))
    nears, fars = (near, near_next, near_last), (far, far_next, far_last)
    low, high = halves(near_next, near_last)
    near_two = from_z(low, 1), from_z(high, 3)
    low, high = halves(far_next, far_last)
    far_two = from_y(low, 1), from_y(high, 3)

    one = 2 * 2 * rows * part * 2 * 2 * piece
    noise_shape = 4, 2 * piece, part
    scores, x_all = call(
        first_kernel,
        [float32(4, 4, 2 * rows, 2 * piece), bfloat16(2, 2 * rows, part)],
        12 * one,
        *(at, data_rows, data_l, data_h, data_lh, *nears, *fars),
        anywhere=10,
        scratch=[pltpu.VMEM((6, *noise_shape), jnp.bfloat16), pltpu.SemaphoreType.DMA((10,))],
    )
    give, keep = (
        call(
            functools.partial(second_kernel, half),
            [float32(2, 4, 2 * rows, 2 * piece)],
            100 * one,
            *(at, x_all, scores, *near_two),
            anywhere=2,
            scratch=[pltpu.VMEM((2, 2, *noise_shape[1:]), jnp.bfloat16), sems],
        )[0]
        for half in (1, 0)
    )
    far_keep, far_give = call(
        third_kernel,
        [float32(2, 2 * rows, 2 * piece)] * 2,
        2 * one,
        *(at, x_all, *far_two),
        anywhere=2,
        scratch=[pltpu.VMEM((2, 2, *noise_shape[1:]), jnp.bfloat16), sems],
    )

    blocks = (8, 2 * rows, 2 * piece)
    tall = 2 * rows, 2 * piece
    least = 0.5 / count
    row_axes, col_axes = ("l", "h", "c"), ("z", "y")
    row_sent, col_sent = float32(8, 1, 2 * rows), float32(16, 8, 2 * piece)

    def exchange(sent, axes):
        return lax.all_to_all(sent, axes, 0, 0, tiled=True)

    keep, give = keep.reshape(blocks), give.reshape(blocks)
    kernel = functools.partial(rows_1_kernel, 2.0 / (width * eps))
    score, sent = call(
        kernel,
        [float32(*blocks), row_sent],
        0,
        *(at, keep, flip(give, "c"), far_keep, flip(far_give, "c")),
        scratch=[pltpu.VMEM(tall, jnp.float32)] * 2,
    )
    kernel = functools.partial(columns_1_kernel, log_count)
    row_pot, sent = call(
        kernel, [float32(*tall), col_sent], 0, at, exchange(sent, row_axes), score
    )
    plan, sent = call(
        rows_2_kernel,
        [float32(*blocks), row_sent],
        0,
        *(at, exchange(sent, col_axes), score, row_pot),
        scratch=[pltpu.VMEM(tall, jnp.float32)],
    )
    plan_other = flip(plan, "c")
    kernel = functools.partial(columns_2_kernel, least)
    col_sent = float32(32, 8, 2 * piece)
    row_scale, sent = call(
        kernel, [float32(*tall), col_sent], 0, at, exchange(sent, row_axes), plan
    )
    near_noise, far_noise = (*nears, *near_two), (*fars, *far_two)
    message = bfloat16(mid + 16, part)
    weights, low, high = call(
        functools.partial(target_1_kernel, least),
        [bfloat16(4, 4, *blocks[1:]), message, message],
        8 * one,
        *(at, exchange(sent, ("z", "y", "c")), plan, plan_other, row_scale, *far_noise),
    )
    low, high = flip(low, "l"), flip(high, "lh")

    def other_rows(place, half, came, names):
        noise = near_noise if place is near_place else far_noise
        kernel = functools.partial(target_2_kernel, place, half)
        outs = [bfloat16(mid, part), float32(mid, part), float32(8, rows)]
        sent, *kept = call(kernel, outs, 8 * one, at, weights, *noise)
        added = call(functools.partial(add_kernel, half), [message], 0, at, *kept, came)[0]
        return flip(sent, names), flip(added, names)

    lh_high, lh_low = other_rows(far_place, 0, low, "lh")
    l_low, l_high = other_rows(near_place, 1, high, "l")
    own = call(
        target_3_kernel,
        [float32(rows, part), float32(8, rows)],
        64 * one,
        *(at, weights, *near_noise),
    )
    messages = l_low, l_high, lh_low, lh_high
    return call(last_kernel, [bfloat16(rows, part)], 0, at, *own, *messages)[0]


def solution(mesh):
    fine = Mesh(mesh.devices.reshape(SIZES), AXES)
    spec = P(("z", "y", "l"), ("h", "c"))
    return jax.shard_map(
        per_device, mesh=fine, in_specs=(spec, spec), out_specs=spec, check_vma=False
    )
```

```python
import functools
import itertools
import math

import jax
import jax.numpy as jnp
from jax import lax
from jax.experimental import pallas as pl
from jax.experimental.pallas import tpu as pltpu
from jax.sharding import Mesh, PartitionSpec as P

AXES = ("z", "y", "l", "h", "c")
SIZES = (4, 4, 2, 2, 2)


def index_of(*place):
    index = 0
    for n, a in zip(SIZES, place):
        index = index * n + a % n
    return index


def move(value, dest):
    places = itertools.product(*(range(n) for n in SIZES))
    pairs = [(index_of(*place), index_of(*dest(*place))) for place in places]
    return lax.ppermute(value, AXES, pairs)


def from_y(value, k):
    return move(value, lambda z, y, l, h, c: (z, y - k, l, h, c))


def from_z(value, k):
    return move(value, lambda z, y, l, h, c: (z - k, y, l, h, c))


def flip(value, names):
    return move(
        value,
        lambda *place: [1 - a if name in names else a for name, a in zip(AXES, place)],
    )


def cross(a, b):
    return lax.dot_general(a, b, (((1,), (1,)), ((), ())), preferred_element_type=jnp.float32)


def dot(a, b):
    return jnp.dot(a, b, preferred_element_type=jnp.float32)


def exact_terms(total):
    terms = []
    for _ in range(3):
        terms.append(total.astype(jnp.bfloat16))
        total = total - terms[-1].astype(jnp.float32)
    return terms


def flat(blocks):
    return blocks.reshape(-1, blocks.shape[-1])


def half_squares(rows):
    sums = 0.0
    for at in range(0, rows.shape[1], 128):
        wide = rows[:, at : at + 128].astype(jnp.float32)
        sums = sums + wide * wide
    ones = jnp.full((16, 128), 0.5, jnp.bfloat16)
    return sum(cross(ones, term) for term in exact_terms(sums))[:1]


def call(kernel, outs, flops, *args, anywhere=0, spaces=None, scratch=()):
    moved = sum(a.size * a.dtype.itemsize for a in (*args, *outs))
    inner = len(args) - 1 - anywhere
    return pl.pallas_call(
        kernel,
        out_shape=outs,
        in_specs=[pl.BlockSpec(memory_space=pltpu.SMEM)]
        + [pl.BlockSpec(memory_space=pltpu.VMEM)] * inner
        + [pl.BlockSpec(memory_space=pl.ANY)] * anywhere,
        out_specs=[pl.BlockSpec(memory_space=spaces or pltpu.VMEM)] * len(outs),
        scratch_shapes=scratch,
        compiler_params=pltpu.CompilerParams(vmem_limit_bytes=20 * 2**20),
        cost_estimate=pl.CostEstimate(flops=flops, bytes_accessed=moved, transcendentals=0),
    )(*args)


def started(sems, *pairs):
    copies = [pltpu.make_async_copy(a, b, sems.at[n]) for n, (a, b) in enumerate(pairs)]
    for copy in copies:
        copy.start()
    return copies


def terms_in_rows(vec):
    row = lax.broadcasted_iota(jnp.int32, (16, vec.shape[1]), 0)
    terms = jnp.zeros(row.shape, jnp.float32)
    for n, term in enumerate(exact_terms(vec)):
        terms = jnp.where(row == n, term.astype(jnp.float32), terms)
    return terms.astype(jnp.bfloat16)


def to_rows(terms):
    ones = jnp.ones((terms.shape[0], 128), jnp.bfloat16)
    return lax.dot_general(
        terms, ones, (((0,), (0,)), ((), ())), preferred_element_type=jnp.float32
    )


def lane_sums(values):
    ones = jnp.ones((16, 128), jnp.bfloat16)
    return sum(cross(ones, term) for term in exact_terms(values))[:1]


def first_lanes(values):
    lane = lax.broadcasted_iota(jnp.int32, (16, 128), 1)
    pick = jnp.where(lane == 0, 1.0, 0.0).astype(jnp.bfloat16)
    return sum(cross(pick, term) for term in exact_terms(values))[:1]


def log_sum_exp(values):
    top = functools.reduce(jnp.maximum, values)
    return top + jnp.log(sum(jnp.exp(v - top) for v in values))


def stack_kernel(at, *refs):
    *blocks, out, sems = refs
    copies = started(sems, *((block, out.at[n]) for n, block in enumerate(blocks)))
    for copy in copies:
        copy.wait()


def halves_kernel(at, next_, last, low, high, sems):
    for copy in started(sems, (next_.at[:2], low), (last.at[2:], high)):
        copy.wait()


def near_place(at, k, r):
    return lax.rem(at[0] + k - 2 * at[4] + 4, 4), lax.rem(at[1] + r, 4)


def far_place(at, k, r):
    return lax.rem(at[0] + r - 2 * at[4] + 4, 4), lax.rem(at[1] + k, 4)


def first_kernel(at, *refs):
    data, noises, (out, x, held, sems) = refs[:4], refs[4:10], refs[10:]
    rows = data[0].shape[0]
    own, other = (pl.ds(pl.multiple_of(r * rows, rows), rows) for r in (at[2], 1 - at[2]))
    places = x.at[0, own], x.at[0, other], x.at[1, own], x.at[1, other]
    copies = started(
        sems, *zip(data, places), *((noise, held.at[n]) for n, noise in enumerate(noises))
    )
    for copy in copies[:4]:
        copy.wait()
    for n, k in enumerate((0, 1, 3)):
        copies[4 + n].wait()
        for r in (0, 2):
            noise = flat(held[n, r : r + 2])
            value = cross(x[0], noise) - half_squares(noise)
            out[near_place(at, k, r)] = value[:, :128]
            out[near_place(at, k, r + 1)] = value[:, 128:]
    x_sq = 0.0
    for side in range(2):
        for span in range(0, x.shape[2], 128):
            wide = x[side, :, span : span + 128].astype(jnp.float32)
            x_sq = x_sq + wide * wide
    x_sq = jnp.broadcast_to(0.5 * jnp.sum(x_sq, axis=1, keepdims=True), x_sq.shape)
    for r in range(4):
        out[near_place(at, 2, r)] = -x_sq
    for n, k in enumerate((0, 1, 3)):
        copies[7 + n].wait()
        for r in (0, 2):
            noise = flat(held[3 + n, r : r + 2])
            value = cross(x[1], noise) - half_squares(noise)
            out[far_place(at, k, r)] += value[:, :128]
            out[far_place(at, k, r + 1)] += value[:, 128:]
    for n, k in enumerate((0, 1, 3)):
        for r in range(4):
            out[near_place(at, k, r)] -= x_sq


def second_kernel(half, at, x, acc, n_a, n_b, out, held, sems):
    copies = started(sems, *((p, held.at[n]) for n, p in enumerate((n_a, n_b))))
    for block in range(2):
        for j in range(4):
            out[block, j] = acc[2 * half + block, j]
    for copy in copies:
        copy.wait()
    block, _ = near_place(at, 2, 0)

    @pl.when((block >= 2) == bool(half))
    def _():
        for n, r in ((0, 0), (1, 2)):
            noise = flat(held[n])
            value = cross(x[0], noise) - half_squares(noise)
            out[block - 2 * half, near_place(at, 2, r)[1]] += value[:, :128]
            out[block - 2 * half, near_place(at, 2, r + 1)[1]] += value[:, 128:]


def third_kernel(at, x, f_a, f_b, keep, give, held, sems):
    copies = started(sems, *((p, held.at[n]) for n, p in enumerate((f_a, f_b))))
    for n, copy in enumerate(copies):
        copy.wait()
        noise = flat(held[n])
        value = cross(x[1], noise) - half_squares(noise)
        for side in range(2):
            block, _ = far_place(at, 2, 2 * n + side)
            part = value[:, 128 * side : 128 * side + 128]

            @pl.when(block < 2)
            def _():
                keep[block] = part

            @pl.when(block >= 2)
            def _():
                give[block - 2] = part


def weights_of(at, weights, place, own_rows):
    rows = weights.shape[2] // 2
    to_l = at[2] if own_rows else 1 - at[2]
    here = pl.ds(pl.multiple_of(to_l * rows, rows), rows)
    parts = []
    for k, rs in ((0, range(4)), (1, range(4)), (3, range(4)), (2, (0, 1)), (2, (2, 3))):
        blocks = [place(at, k, r) for r in rs]
        parts.append(
            jnp.concatenate([weights[block[0], block[1], here] for block in blocks], axis=1)
        )
    total = 0.0
    for value in parts:
        total = total + cross(jnp.ones((16, value.shape[1]), jnp.bfloat16), value)
    return parts, total[:1]


STEP = 256


def product(parts, noise, first):
    span = slice(first, first + STEP)
    return sum(dot(w, flat(p[:, :, span])) for w, p in zip(parts, noise))


def target_1_kernel(
    least, at, came, plan, other, row_scale, p0, p1, p3, p2_a, p2_b, weights, low, high
):
    c = at[4]
    mine = sum(came[2 * n + c] for n in range(came.shape[0] // 2))
    theirs = sum(came[2 * n + 1 - c] for n in range(came.shape[0] // 2))
    for half, (values, total) in enumerate(((plan, mine), (other, theirs))):
        scale = 1.0 / jnp.maximum(total, least)
        for b in range(values.shape[0]):
            value = values[b] * row_scale[...] * scale[b : b + 1]
            weights[2 * half + b // 4, b % 4] = value.astype(weights.dtype)
    parts, total = weights_of(at, weights, far_place, True)
    mid = low.shape[0] - 16
    for first in range(0, p0.shape[-1], STEP):
        value = product(parts, (p0, p1, p3, p2_a, p2_b), first)
        low[:mid, first : first + STEP] = value[:mid].astype(low.dtype)
        high[:mid, first : first + STEP] = value[mid:].astype(high.dtype)
    for n, out in enumerate((low, high)):
        out[mid:, :] = jnp.zeros((16, out.shape[1]), out.dtype)
        out[mid:, :mid] = terms_in_rows(total[:, n * mid : n * mid + mid])


def target_2_kernel(
    place, half, at, weights, p0, p1, p3, p2_a, p2_b, message, values, row_total
):
    parts, total = weights_of(at, weights, place, False)
    mid = values.shape[0]
    kept, sent = (slice(n * mid, n * mid + mid) for n in (half, 1 - half))
    for first in range(0, p0.shape[-1], STEP):
        value = product(parts, (p0, p1, p3, p2_a, p2_b), first)
        message[:, first : first + STEP] = value[sent].astype(message.dtype)
        values[:, first : first + STEP] = value[kept]
    row_total[...] = jnp.broadcast_to(total, row_total.shape)


def target_3_kernel(at, weights, p0, p1, p3, p2_a, p2_b, values, row_total):
    parts, total = weights_of(at, weights, near_place, True)
    for first in range(0, p0.shape[-1], STEP):
        values[:, first : first + STEP] = product(parts, (p0, p1, p3, p2_a, p2_b), first)
    row_total[...] = jnp.broadcast_to(total, row_total.shape)


def add_kernel(half, at, values, row_total, came, out):
    mid = values.shape[0]
    out[:mid, :] = (values[...] + came[:mid].astype(jnp.float32)).astype(out.dtype)
    terms = came[mid:, :mid].astype(jnp.float32)
    total = [row_total[:1, :mid], row_total[:1, mid:]]
    total[half] = total[half] + terms[0:1] + terms[1:2] + terms[2:3]
    out[mid:, :] = jnp.zeros((16, out.shape[1]), out.dtype)
    out[mid:, : 2 * mid] = terms_in_rows(jnp.concatenate(total, axis=1))


def last_kernel(at, own, own_total, l_low, l_high, lh_low, lh_high, out):
    mid = own.shape[0] // 2
    terms = [m[mid:, : 2 * mid] for m in (l_high, lh_low)]
    total = 1.0 / to_rows(jnp.concatenate([terms_in_rows(own_total[:1])] + terms, axis=0))
    for n, messages in enumerate(((l_low, lh_low), (l_high, lh_high))):
        here = slice(n * mid, n * mid + mid)
        for column in range(0, own.shape[1], 128):
            span = slice(column, column + 128)
            value = own[here, span]
            for m in messages:
                value = value + m[:mid, span].astype(jnp.float32)
            out[here, span] = (value * total[here]).astype(out.dtype)


TILE = 64


def rows_1_kernel(scale, at, keep, got, far_keep, far_got, score, sent, tops, sums):
    late = lax.rem(at[1] + 2, 4)
    scales = [jnp.where(late == j, scale, 0.0) for j in range(4)]
    blocks = range(keep.shape[0])

    @pl.loop(0, keep.shape[1] // TILE)
    def _(t):
        here = pl.ds(pl.multiple_of(t * TILE, TILE), TILE)
        far = [far_keep[b, here] + far_got[b, here] for b in range(2)]
        top = None
        for b in blocks:
            value = (keep[b, here] + got[b, here]) * scale + far[b // 4] * scales[b % 4]
            score[b, here] = value
            top = value if top is None else jnp.maximum(top, value)
        tops[here] = top

    tops[...] = jnp.broadcast_to(jnp.max(tops[...], axis=1, keepdims=True), tops.shape)

    @pl.loop(0, keep.shape[1] // TILE)
    def _(t):
        here = pl.ds(pl.multiple_of(t * TILE, TILE), TILE)
        top = tops[here]
        sums[here] = sum(jnp.exp(score[b, here] - top) for b in blocks)

    log_row = first_lanes(tops[...]) + jnp.log(lane_sums(sums[...]))
    for n in range(sent.shape[0]):
        sent[n] = log_row


def columns_1_kernel(log_count, at, came, score, row_pot, sent):
    pot = -log_count - log_sum_exp([came[n] for n in range(came.shape[0])])
    row_pot[...] = to_rows(terms_in_rows(pot))
    logs = []
    for b in range(score.shape[0]):
        value = score[b] + row_pot[...]
        top = jnp.max(value, axis=0, keepdims=True)
        total = jnp.sum(jnp.exp(value - top), axis=0, keepdims=True)
        logs.append(top + jnp.log(total))
    logs = jnp.concatenate(logs)
    for n in range(sent.shape[0]):
        sent[n] = logs


def rows_2_kernel(at, came, score, row_pot, plan, sent, sums):
    pot = -log_sum_exp([came[n] for n in range(came.shape[0])])

    @pl.loop(0, score.shape[1] // TILE)
    def _(t):
        here = pl.ds(pl.multiple_of(t * TILE, TILE), TILE)
        total = 0.0
        for b in range(score.shape[0]):
            value = score[b, here] + row_pot[here] + pot[b : b + 1]
            value = jnp.exp(jnp.minimum(value, 0.0))
            plan[b, here] = value
            total = total + value
        sums[here] = total

    row_sum = lane_sums(sums[...])
    for n in range(sent.shape[0]):
        sent[n] = row_sum


def columns_2_kernel(least, at, came, plan, row_scale, sent):
    total = sum(came[n] for n in range(came.shape[0]))
    row_scale[...] = to_rows(terms_in_rows(1.0 / jnp.maximum(total, least)))
    sums = []
    for b in range(plan.shape[0]):
        sums.append(jnp.sum(plan[b] * row_scale[...], axis=0, keepdims=True))
    sums = jnp.concatenate(sums)
    for n in range(sent.shape[0]):
        sent[n] = sums


def per_device(data_rows, noise_rows):
    z, y, l, h, c = (lax.axis_index(name) for name in AXES)
    rows, part = data_rows.shape
    width = part * 4
    count = rows * 32
    eps = 0.64 / math.sqrt(width)
    log_count = math.log(count)
    piece = rows // 4

    def float32(*shape):
        return jax.ShapeDtypeStruct(shape, jnp.float32)

    def bfloat16(*shape):
        return jax.ShapeDtypeStruct(shape, jnp.bfloat16)

    at = jnp.stack([z, y, l, h, c])

    wave = lax.optimization_barrier
    mid = rows // 2
    near = lax.dynamic_slice_in_dim(noise_rows, h * mid, mid)
    far = flip(lax.dynamic_slice_in_dim(noise_rows, (1 - h) * mid, mid), "h")
    near_1, near_3 = from_y(near, 1), from_y(near, 3)
    far, data_rows = wave((far, data_rows))
    data_l = flip(data_rows, "l")
    near_2 = from_y(near_1, 1)
    far_3 = from_z(far, 3)
    near_3, far_1, data_rows = wave((near_3, from_z(far, 1), data_rows))
    data_lh = flip(data_rows, "lh")
    far_2, data_l, data_rows = wave((from_z(far_1, 1), data_l, data_rows))
    sems = pltpu.SemaphoreType.DMA((4,))

    def stacked(*blocks):
        out = [bfloat16(4, *blocks[0].shape)]
        return call(
            stack_kernel, out, 0, at, *blocks, anywhere=4, spaces=pl.ANY, scratch=[sems]
        )[0]

    def halves(next_, last):
        out = [bfloat16(2, *next_.shape[1:])] * 2
        return call(
            halves_kernel, out, 0, at, next_, last, anywhere=2, spaces=pl.ANY, scratch=[sems]
        )

    near, far = stacked(near, near_1, near_2, near_3), stacked(far, far_1, far_2, far_3)
    near_next, near_last = from_z(near, 1), from_z(near, 3)
    far_next, far_last = from_y(far, 1), from_y(far, 3)
    data_lh, data_rows = wave((data_lh, data_rows))
    data_h = flip(data_rows, "h")
    far_next, far_last, data_h = wave((far_next, far_last, data_h))
    nears, fars = (near, near_next, near_last), (far, far_next, far_last)
    low, high = halves(near_next, near_last)
    near_two = from_z(low, 1), from_z(high, 3)
    low, high = halves(far_next, far_last)
    far_two = from_y(low, 1), from_y(high, 3)

    one = 2 * 2 * rows * part * 2 * 2 * piece
    noise_shape = 4, 2 * piece, part
    scores, x_all = call(
        first_kernel,
        [float32(4, 4, 2 * rows, 2 * piece), bfloat16(2, 2 * rows, part)],
        12 * one,
        *(at, data_rows, data_l, data_h, data_lh, *nears, *fars),
        anywhere=10,
        scratch=[pltpu.VMEM((6, *noise_shape), jnp.bfloat16), pltpu.SemaphoreType.DMA((10,))],
    )
    give, keep = (
        call(
            functools.partial(second_kernel, half),
            [float32(2, 4, 2 * rows, 2 * piece)],
            100 * one,
            *(at, x_all, scores, *near_two),
            anywhere=2,
            scratch=[pltpu.VMEM((2, 2, *noise_shape[1:]), jnp.bfloat16), sems],
        )[0]
        for half in (1, 0)
    )
    far_keep, far_give = call(
        third_kernel,
        [float32(2, 2 * rows, 2 * piece)] * 2,
        2 * one,
        *(at, x_all, *far_two),
        anywhere=2,
        scratch=[pltpu.VMEM((2, 2, *noise_shape[1:]), jnp.bfloat16), sems],
    )

    blocks = (8, 2 * rows, 2 * piece)
    tall = 2 * rows, 2 * piece
    least = 0.5 / count
    row_axes, col_axes = ("l", "h", "c"), ("z", "y")
    row_sent, col_sent = float32(8, 1, 2 * rows), float32(16, 8, 2 * piece)

    def exchange(sent, axes):
        return lax.all_to_all(sent, axes, 0, 0, tiled=True)

    keep, give = keep.reshape(blocks), give.reshape(blocks)
    kernel = functools.partial(rows_1_kernel, 2.0 / (width * eps))
    score, sent = call(
        kernel,
        [float32(*blocks), row_sent],
        0,
        *(at, keep, flip(give, "c"), far_keep, flip(far_give, "c")),
        scratch=[pltpu.VMEM(tall, jnp.float32)] * 2,
    )
    kernel = functools.partial(columns_1_kernel, log_count)
    row_pot, sent = call(
        kernel, [float32(*tall), col_sent], 0, at, exchange(sent, row_axes), score
    )
    plan, sent = call(
        rows_2_kernel,
        [float32(*blocks), row_sent],
        0,
        *(at, exchange(sent, col_axes), score, row_pot),
        scratch=[pltpu.VMEM(tall, jnp.float32)],
    )
    plan_other = flip(plan, "c")
    kernel = functools.partial(columns_2_kernel, least)
    col_sent = float32(32, 8, 2 * piece)
    row_scale, sent = call(
        kernel, [float32(*tall), col_sent], 0, at, exchange(sent, row_axes), plan
    )
    near_noise, far_noise = (*nears, *near_two), (*fars, *far_two)
    message = bfloat16(mid + 16, part)
    weights, low, high = call(
        functools.partial(target_1_kernel, least),
        [bfloat16(4, 4, *blocks[1:]), message, message],
        8 * one,
        *(at, exchange(sent, ("z", "y", "c")), plan, plan_other, row_scale, *far_noise),
    )
    low, high = flip(low, "l"), flip(high, "lh")

    def other_rows(place, half, came, names):
        noise = near_noise if place is near_place else far_noise
        kernel = functools.partial(target_2_kernel, place, half)
        outs = [bfloat16(mid, part), float32(mid, part), float32(8, rows)]
        sent, *kept = call(kernel, outs, 8 * one, at, weights, *noise)
        added = call(functools.partial(add_kernel, half), [message], 0, at, *kept, came)[0]
        return flip(sent, names), flip(added, names)

    lh_high, lh_low = other_rows(far_place, 0, low, "lh")
    l_low, l_high = other_rows(near_place, 1, high, "l")
    own = call(
        target_3_kernel,
        [float32(rows, part), float32(8, rows)],
        64 * one,
        *(at, weights, *near_noise),
    )
    messages = l_low, l_high, lh_low, lh_high
    return call(last_kernel, [bfloat16(rows, part)], 0, at, *own, *messages)[0]


def solution(mesh):
    fine = Mesh(mesh.devices.reshape(SIZES), AXES)
    spec = P(("z", "y", "l"), ("h", "c"))
    return jax.shard_map(
        per_device, mesh=fine, in_specs=(spec, spec), out_specs=spec, check_vma=False
    )
```

```python
import functools
import itertools
import math

import jax
import jax.numpy as jnp
from jax import lax
from jax.experimental import pallas as pl
from jax.experimental.pallas import tpu as pltpu
from jax.sharding import Mesh, PartitionSpec as P

AXES = ("z", "y", "l", "h", "c")
SIZES = (4, 4, 2, 2, 2)


def index_of(*place):
    index = 0
    for n, a in zip(SIZES, place):
        index = index * n + a % n
    return index


def move(value, dest):
    places = itertools.product(*(range(n) for n in SIZES))
    pairs = [(index_of(*place), index_of(*dest(*place))) for place in places]
    return lax.ppermute(value, AXES, pairs)


def from_y(value, k):
    return move(value, lambda z, y, l, h, c: (z, y - k, l, h, c))


def from_z(value, k):
    return move(value, lambda z, y, l, h, c: (z - k, y, l, h, c))


def flip(value, names):
    return move(
        value,
        lambda *place: [1 - a if name in names else a for name, a in zip(AXES, place)],
    )


def cross(a, b):
    return lax.dot_general(a, b, (((1,), (1,)), ((), ())), preferred_element_type=jnp.float32)


def dot(a, b):
    return jnp.dot(a, b, preferred_element_type=jnp.float32)


def exact_terms(total):
    terms = []
    for _ in range(3):
        terms.append(total.astype(jnp.bfloat16))
        total = total - terms[-1].astype(jnp.float32)
    return terms


def flat(blocks):
    return blocks.reshape(-1, blocks.shape[-1])


def half_squares(rows):
    sums = 0.0
    for at in range(0, rows.shape[1], 128):
        wide = rows[:, at : at + 128].astype(jnp.float32)
        sums = sums + wide * wide
    ones = jnp.full((16, 128), 0.5, jnp.bfloat16)
    return sum(cross(ones, term) for term in exact_terms(sums))[:1]


def call(kernel, outs, flops, *args, anywhere=0, spaces=None, scratch=()):
    moved = sum(a.size * a.dtype.itemsize for a in (*args, *outs))
    inner = len(args) - 1 - anywhere
    return pl.pallas_call(
        kernel,
        out_shape=outs,
        in_specs=[pl.BlockSpec(memory_space=pltpu.SMEM)]
        + [pl.BlockSpec(memory_space=pltpu.VMEM)] * inner
        + [pl.BlockSpec(memory_space=pl.ANY)] * anywhere,
        out_specs=[pl.BlockSpec(memory_space=spaces or pltpu.VMEM)] * len(outs),
        scratch_shapes=scratch,
        compiler_params=pltpu.CompilerParams(vmem_limit_bytes=20 * 2**20),
        cost_estimate=pl.CostEstimate(flops=flops, bytes_accessed=moved, transcendentals=0),
    )(*args)


def started(sems, *pairs):
    copies = [pltpu.make_async_copy(a, b, sems.at[n]) for n, (a, b) in enumerate(pairs)]
    for copy in copies:
        copy.start()
    return copies


def terms_in_rows(vec):
    row = lax.broadcasted_iota(jnp.int32, (16, vec.shape[1]), 0)
    terms = jnp.zeros(row.shape, jnp.float32)
    for n, term in enumerate(exact_terms(vec)):
        terms = jnp.where(row == n, term.astype(jnp.float32), terms)
    return terms.astype(jnp.bfloat16)


def to_rows(terms):
    ones = jnp.ones((terms.shape[0], 128), jnp.bfloat16)
    return lax.dot_general(
        terms, ones, (((0,), (0,)), ((), ())), preferred_element_type=jnp.float32
    )


def lane_sums(values):
    ones = jnp.ones((16, 128), jnp.bfloat16)
    return sum(cross(ones, term) for term in exact_terms(values))[:1]


def first_lanes(values):
    lane = lax.broadcasted_iota(jnp.int32, (16, 128), 1)
    pick = jnp.where(lane == 0, 1.0, 0.0).astype(jnp.bfloat16)
    return sum(cross(pick, term) for term in exact_terms(values))[:1]


def log_sum_exp(values):
    top = functools.reduce(jnp.maximum, values)
    return top + jnp.log(sum(jnp.exp(v - top) for v in values))


def stack_kernel(at, *refs):
    *blocks, out, sems = refs
    copies = started(sems, *((block, out.at[n]) for n, block in enumerate(blocks)))
    for copy in copies:
        copy.wait()


def halves_kernel(at, next_, last, low, high, sems):
    for copy in started(sems, (next_.at[:2], low), (last.at[2:], high)):
        copy.wait()


def near_place(at, k, r):
    return lax.rem(at[0] + k - 2 * at[4] + 4, 4), lax.rem(at[1] + r, 4)


def far_place(at, k, r):
    return lax.rem(at[0] + r - 2 * at[4] + 4, 4), lax.rem(at[1] + k, 4)


def first_kernel(at, *refs):
    data, noises, (out, x, held, sems) = refs[:4], refs[4:10], refs[10:]
    rows = data[0].shape[0]
    own, other = (pl.ds(pl.multiple_of(r * rows, rows), rows) for r in (at[2], 1 - at[2]))
    places = x.at[0, own], x.at[0, other], x.at[1, own], x.at[1, other]
    copies = started(
        sems, *zip(data, places), *((noise, held.at[n]) for n, noise in enumerate(noises))
    )
    for copy in copies[:4]:
        copy.wait()
    for n, k in enumerate((0, 1, 3)):
        copies[4 + n].wait()
        for r in (0, 2):
            noise = flat(held[n, r : r + 2])
            value = cross(x[0], noise) - half_squares(noise)
            out[near_place(at, k, r)] = value[:, :128]
            out[near_place(at, k, r + 1)] = value[:, 128:]
    x_sq = 0.0
    for side in range(2):
        for span in range(0, x.shape[2], 128):
            wide = x[side, :, span : span + 128].astype(jnp.float32)
            x_sq = x_sq + wide * wide
    x_sq = jnp.broadcast_to(0.5 * jnp.sum(x_sq, axis=1, keepdims=True), x_sq.shape)
    for r in range(4):
        out[near_place(at, 2, r)] = -x_sq
    for n, k in enumerate((0, 1, 3)):
        copies[7 + n].wait()
        for r in (0, 2):
            noise = flat(held[3 + n, r : r + 2])
            value = cross(x[1], noise) - half_squares(noise)
            out[far_place(at, k, r)] += value[:, :128]
            out[far_place(at, k, r + 1)] += value[:, 128:]
    for n, k in enumerate((0, 1, 3)):
        for r in range(4):
            out[near_place(at, k, r)] -= x_sq


def second_kernel(half, at, x, acc, n_a, n_b, out, held, sems):
    copies = started(sems, *((p, held.at[n]) for n, p in enumerate((n_a, n_b))))
    for block in range(2):
        for j in range(4):
            out[block, j] = acc[2 * half + block, j]
    for copy in copies:
        copy.wait()
    block, _ = near_place(at, 2, 0)

    @pl.when((block >= 2) == bool(half))
    def _():
        for n, r in ((0, 0), (1, 2)):
            noise = flat(held[n])
            value = cross(x[0], noise) - half_squares(noise)
            out[block - 2 * half, near_place(at, 2, r)[1]] += value[:, :128]
            out[block - 2 * half, near_place(at, 2, r + 1)[1]] += value[:, 128:]


def third_kernel(at, x, f_a, f_b, keep, give, held, sems):
    copies = started(sems, *((p, held.at[n]) for n, p in enumerate((f_a, f_b))))
    for n, copy in enumerate(copies):
        copy.wait()
        noise = flat(held[n])
        value = cross(x[1], noise) - half_squares(noise)
        for side in range(2):
            block, _ = far_place(at, 2, 2 * n + side)
            part = value[:, 128 * side : 128 * side + 128]

            @pl.when(block < 2)
            def _():
                keep[block] = part

            @pl.when(block >= 2)
            def _():
                give[block - 2] = part


def weights_of(at, weights, place, own_rows):
    rows = weights.shape[2] // 2
    to_l = at[2] if own_rows else 1 - at[2]
    here = pl.ds(pl.multiple_of(to_l * rows, rows), rows)
    parts = []
    for k, rs in ((0, range(4)), (1, range(4)), (3, range(4)), (2, (0, 1)), (2, (2, 3))):
        blocks = [place(at, k, r) for r in rs]
        parts.append(
            jnp.concatenate([weights[block[0], block[1], here] for block in blocks], axis=1)
        )
    total = 0.0
    for value in parts:
        total = total + cross(jnp.ones((16, value.shape[1]), jnp.bfloat16), value)
    return parts, total[:1]


STEP = 256


def product(parts, noise, first):
    span = slice(first, first + STEP)
    return sum(dot(w, flat(p[:, :, span])) for w, p in zip(parts, noise))


def target_1_kernel(
    least, at, came, plan, other, row_scale, p0, p1, p3, p2_a, p2_b, weights, low, high
):
    c = at[4]
    mine = sum(came[2 * n + c] for n in range(came.shape[0] // 2))
    theirs = sum(came[2 * n + 1 - c] for n in range(came.shape[0] // 2))
    for half, (values, total) in enumerate(((plan, mine), (other, theirs))):
        scale = 1.0 / jnp.maximum(total, least)
        for b in range(values.shape[0]):
            value = values[b] * row_scale[...] * scale[b : b + 1]
            weights[2 * half + b // 4, b % 4] = value.astype(weights.dtype)
    parts, total = weights_of(at, weights, far_place, True)
    mid = low.shape[0] - 16
    for first in range(0, p0.shape[-1], STEP):
        value = product(parts, (p0, p1, p3, p2_a, p2_b), first)
        low[:mid, first : first + STEP] = value[:mid].astype(low.dtype)
        high[:mid, first : first + STEP] = value[mid:].astype(high.dtype)
    for n, out in enumerate((low, high)):
        out[mid:, :] = jnp.zeros((16, out.shape[1]), out.dtype)
        out[mid:, :mid] = terms_in_rows(total[:, n * mid : n * mid + mid])


def target_2_kernel(
    place, half, at, weights, p0, p1, p3, p2_a, p2_b, message, values, row_total
):
    parts, total = weights_of(at, weights, place, False)
    mid = values.shape[0]
    kept, sent = (slice(n * mid, n * mid + mid) for n in (half, 1 - half))
    for first in range(0, p0.shape[-1], STEP):
        value = product(parts, (p0, p1, p3, p2_a, p2_b), first)
        message[:, first : first + STEP] = value[sent].astype(message.dtype)
        values[:, first : first + STEP] = value[kept]
    row_total[...] = jnp.broadcast_to(total, row_total.shape)


def target_3_kernel(at, weights, p0, p1, p3, p2_a, p2_b, values, row_total):
    parts, total = weights_of(at, weights, near_place, True)
    for first in range(0, p0.shape[-1], STEP):
        values[:, first : first + STEP] = product(parts, (p0, p1, p3, p2_a, p2_b), first)
    row_total[...] = jnp.broadcast_to(total, row_total.shape)


def add_kernel(half, at, values, row_total, came, out):
    mid = values.shape[0]
    out[:mid, :] = (values[...] + came[:mid].astype(jnp.float32)).astype(out.dtype)
    terms = came[mid:, :mid].astype(jnp.float32)
    total = [row_total[:1, :mid], row_total[:1, mid:]]
    total[half] = total[half] + terms[0:1] + terms[1:2] + terms[2:3]
    out[mid:, :] = jnp.zeros((16, out.shape[1]), out.dtype)
    out[mid:, : 2 * mid] = terms_in_rows(jnp.concatenate(total, axis=1))


def last_kernel(at, own, own_total, l_low, l_high, lh_low, lh_high, out):
    mid = own.shape[0] // 2
    terms = [m[mid:, : 2 * mid] for m in (l_high, lh_low)]
    total = 1.0 / to_rows(jnp.concatenate([terms_in_rows(own_total[:1])] + terms, axis=0))
    for n, messages in enumerate(((l_low, lh_low), (l_high, lh_high))):
        here = slice(n * mid, n * mid + mid)
        for column in range(0, own.shape[1], 128):
            span = slice(column, column + 128)
            value = own[here, span]
            for m in messages:
                value = value + m[:mid, span].astype(jnp.float32)
            out[here, span] = (value * total[here]).astype(out.dtype)


TILE = 64


def rows_1_kernel(scale, at, keep, got, far_keep, far_got, score, sent, tops, sums):
    late = lax.rem(at[1] + 2, 4)
    scales = [jnp.where(late == j, scale, 0.0) for j in range(4)]
    blocks = range(keep.shape[0])

    @pl.loop(0, keep.shape[1] // TILE)
    def _(t):
        here = pl.ds(pl.multiple_of(t * TILE, TILE), TILE)
        far = [far_keep[b, here] + far_got[b, here] for b in range(2)]
        top = None
        for b in blocks:
            value = (keep[b, here] + got[b, here]) * scale + far[b // 4] * scales[b % 4]
            score[b, here] = value
            top = value if top is None else jnp.maximum(top, value)
        tops[here] = top

    tops[...] = jnp.broadcast_to(jnp.max(tops[...], axis=1, keepdims=True), tops.shape)

    @pl.loop(0, keep.shape[1] // TILE)
    def _(t):
        here = pl.ds(pl.multiple_of(t * TILE, TILE), TILE)
        top = tops[here]
        sums[here] = sum(jnp.exp(score[b, here] - top) for b in blocks)

    log_row = first_lanes(tops[...]) + jnp.log(lane_sums(sums[...]))
    for n in range(sent.shape[0]):
        sent[n] = log_row


def columns_1_kernel(log_count, at, came, score, row_pot, sent):
    pot = -log_count - log_sum_exp([came[n] for n in range(came.shape[0])])
    row_pot[...] = to_rows(terms_in_rows(pot))
    logs = []
    for b in range(score.shape[0]):
        value = score[b] + row_pot[...]
        top = jnp.max(value, axis=0, keepdims=True)
        total = jnp.sum(jnp.exp(value - top), axis=0, keepdims=True)
        logs.append(top + jnp.log(total))
    logs = jnp.concatenate(logs)
    for n in range(sent.shape[0]):
        sent[n] = logs


def rows_2_kernel(at, came, score, row_pot, plan, sent, sums):
    pot = -log_sum_exp([came[n] for n in range(came.shape[0])])

    @pl.loop(0, score.shape[1] // TILE)
    def _(t):
        here = pl.ds(pl.multiple_of(t * TILE, TILE), TILE)
        total = 0.0
        for b in range(score.shape[0]):
            value = score[b, here] + row_pot[here] + pot[b : b + 1]
            value = jnp.exp(jnp.minimum(value, 0.0))
            plan[b, here] = value
            total = total + value
        sums[here] = total

    row_sum = lane_sums(sums[...])
    for n in range(sent.shape[0]):
        sent[n] = row_sum


def columns_2_kernel(least, at, came, plan, row_scale, sent):
    total = sum(came[n] for n in range(came.shape[0]))
    row_scale[...] = to_rows(terms_in_rows(1.0 / jnp.maximum(total, least)))
    sums = []
    for b in range(plan.shape[0]):
        sums.append(jnp.sum(plan[b] * row_scale[...], axis=0, keepdims=True))
    sums = jnp.concatenate(sums)
    for n in range(sent.shape[0]):
        sent[n] = sums


def per_device(data_rows, noise_rows):
    z, y, l, h, c = (lax.axis_index(name) for name in AXES)
    rows, part = data_rows.shape
    width = part * 4
    count = rows * 32
    eps = 0.64 / math.sqrt(width)
    log_count = math.log(count)
    piece = rows // 4

    def float32(*shape):
        return jax.ShapeDtypeStruct(shape, jnp.float32)

    def bfloat16(*shape):
        return jax.ShapeDtypeStruct(shape, jnp.bfloat16)

    at = jnp.stack([z, y, l, h, c])

    wave = lax.optimization_barrier
    mid = rows // 2
    near = lax.dynamic_slice_in_dim(noise_rows, h * mid, mid)
    far = flip(lax.dynamic_slice_in_dim(noise_rows, (1 - h) * mid, mid), "h")
    near_1, near_3 = from_y(near, 1), from_y(near, 3)
    far, data_rows = wave((far, data_rows))
    data_l, data_lh = flip(data_rows, "l"), flip(data_rows, "lh")
    near_2 = from_y(near_1, 1)
    near_3, far_1, far_3 = wave((near_3, from_z(far, 1), from_z(far, 3)))
    far_2, data_l, data_lh, data_rows = wave((from_z(far_1, 1), data_l, data_lh, data_rows))
    sems = pltpu.SemaphoreType.DMA((4,))

    def stacked(*blocks):
        out = [bfloat16(4, *blocks[0].shape)]
        return call(
            stack_kernel, out, 0, at, *blocks, anywhere=4, spaces=pl.ANY, scratch=[sems]
        )[0]

    def halves(next_, last):
        out = [bfloat16(2, *next_.shape[1:])] * 2
        return call(
            halves_kernel, out, 0, at, next_, last, anywhere=2, spaces=pl.ANY, scratch=[sems]
        )

    near, far = stacked(near, near_1, near_2, near_3), stacked(far, far_1, far_2, far_3)
    near_next, near_last = from_z(near, 1), from_z(near, 3)
    far_next, far_last = from_y(far, 1), from_y(far, 3)
    data_h = flip(data_rows, "h")
    far_next, far_last, data_h = wave((far_next, far_last, data_h))
    nears, fars = (near, near_next, near_last), (far, far_next, far_last)
    low, high = halves(near_next, near_last)
    near_two = from_z(low, 1), from_z(high, 3)
    low, high = halves(far_next, far_last)
    far_two = from_y(low, 1), from_y(high, 3)

    one = 2 * 2 * rows * part * 2 * 2 * piece
    noise_shape = 4, 2 * piece, part
    scores, x_all = call(
        first_kernel,
        [float32(4, 4, 2 * rows, 2 * piece), bfloat16(2, 2 * rows, part)],
        12 * one,
        *(at, data_rows, data_l, data_h, data_lh, *nears, *fars),
        anywhere=10,
        scratch=[pltpu.VMEM((6, *noise_shape), jnp.bfloat16), pltpu.SemaphoreType.DMA((10,))],
    )
    give, keep = (
        call(
            functools.partial(second_kernel, half),
            [float32(2, 4, 2 * rows, 2 * piece)],
            100 * one,
            *(at, x_all, scores, *near_two),
            anywhere=2,
            scratch=[pltpu.VMEM((2, 2, *noise_shape[1:]), jnp.bfloat16), sems],
        )[0]
        for half in (1, 0)
    )
    far_keep, far_give = call(
        third_kernel,
        [float32(2, 2 * rows, 2 * piece)] * 2,
        2 * one,
        *(at, x_all, *far_two),
        anywhere=2,
        scratch=[pltpu.VMEM((2, 2, *noise_shape[1:]), jnp.bfloat16), sems],
    )

    blocks = (8, 2 * rows, 2 * piece)
    tall = 2 * rows, 2 * piece
    least = 0.5 / count
    row_axes, col_axes = ("l", "h", "c"), ("z", "y")
    row_sent, col_sent = float32(8, 1, 2 * rows), float32(16, 8, 2 * piece)

    def exchange(sent, axes):
        return lax.all_to_all(sent, axes, 0, 0, tiled=True)

    keep, give = keep.reshape(blocks), give.reshape(blocks)
    kernel = functools.partial(rows_1_kernel, 2.0 / (width * eps))
    score, sent = call(
        kernel,
        [float32(*blocks), row_sent],
        0,
        *(at, keep, flip(give, "c"), far_keep, flip(far_give, "c")),
        scratch=[pltpu.VMEM(tall, jnp.float32)] * 2,
    )
    kernel = functools.partial(columns_1_kernel, log_count)
    row_pot, sent = call(
        kernel, [float32(*tall), col_sent], 0, at, exchange(sent, row_axes), score
    )
    plan, sent = call(
        rows_2_kernel,
        [float32(*blocks), row_sent],
        0,
        *(at, exchange(sent, col_axes), score, row_pot),
        scratch=[pltpu.VMEM(tall, jnp.float32)],
    )
    plan_other = flip(plan, "c")
    kernel = functools.partial(columns_2_kernel, least)
    col_sent = float32(32, 8, 2 * piece)
    row_scale, sent = call(
        kernel, [float32(*tall), col_sent], 0, at, exchange(sent, row_axes), plan
    )
    near_noise, far_noise = (*nears, *near_two), (*fars, *far_two)
    message = bfloat16(mid + 16, part)
    weights, low, high = call(
        functools.partial(target_1_kernel, least),
        [bfloat16(4, 4, *blocks[1:]), message, message],
        8 * one,
        *(at, exchange(sent, ("z", "y", "c")), plan, plan_other, row_scale, *far_noise),
    )
    low, high = flip(low, "l"), flip(high, "lh")

    def other_rows(place, half, came, names):
        noise = near_noise if place is near_place else far_noise
        kernel = functools.partial(target_2_kernel, place, half)
        outs = [bfloat16(mid, part), float32(mid, part), float32(8, rows)]
        sent, *kept = call(kernel, outs, 8 * one, at, weights, *noise)
        added = call(functools.partial(add_kernel, half), [message], 0, at, *kept, came)[0]
        return flip(sent, names), flip(added, names)

    lh_high, lh_low = other_rows(far_place, 0, low, "lh")
    l_low, l_high = other_rows(near_place, 1, high, "l")
    own = call(
        target_3_kernel,
        [float32(rows, part), float32(8, rows)],
        64 * one,
        *(at, weights, *near_noise),
    )
    messages = l_low, l_high, lh_low, lh_high
    return call(last_kernel, [bfloat16(rows, part)], 0, at, *own, *messages)[0]


def solution(mesh):
    fine = Mesh(mesh.devices.reshape(SIZES), AXES)
    spec = P(("z", "y", "l"), ("h", "c"))
    return jax.shard_map(
        per_device, mesh=fine, in_specs=(spec, spec), out_specs=spec, check_vma=False
    )
```

```python
import functools
import itertools
import math

import jax
import jax.numpy as jnp
from jax import lax
from jax.experimental import pallas as pl
from jax.experimental.pallas import tpu as pltpu
from jax.sharding import Mesh, PartitionSpec as P

AXES = ("z", "y", "l", "h", "c")
SIZES = (4, 4, 2, 2, 2)


def index_of(*place):
    index = 0
    for n, a in zip(SIZES, place):
        index = index * n + a % n
    return index


def move(value, dest):
    places = itertools.product(*(range(n) for n in SIZES))
    pairs = [(index_of(*place), index_of(*dest(*place))) for place in places]
    return lax.ppermute(value, AXES, pairs)


def from_y(value, k):
    return move(value, lambda z, y, l, h, c: (z, y - k, l, h, c))


def from_z(value, k):
    return move(value, lambda z, y, l, h, c: (z - k, y, l, h, c))


def flip(value, names):
    return move(
        value,
        lambda *place: [1 - a if name in names else a for name, a in zip(AXES, place)],
    )


def cross(a, b):
    return lax.dot_general(a, b, (((1,), (1,)), ((), ())), preferred_element_type=jnp.float32)


def dot(a, b):
    return jnp.dot(a, b, preferred_element_type=jnp.float32)


def exact_terms(total):
    terms = []
    for _ in range(3):
        terms.append(total.astype(jnp.bfloat16))
        total = total - terms[-1].astype(jnp.float32)
    return terms


def flat(blocks):
    return blocks.reshape(-1, blocks.shape[-1])


def half_squares(rows):
    sums = 0.0
    for at in range(0, rows.shape[1], 128):
        wide = rows[:, at : at + 128].astype(jnp.float32)
        sums = sums + wide * wide
    ones = jnp.full((16, 128), 0.5, jnp.bfloat16)
    return sum(cross(ones, term) for term in exact_terms(sums))[:1]


def call(kernel, outs, flops, *args, anywhere=0, spaces=None, scratch=()):
    moved = sum(a.size * a.dtype.itemsize for a in (*args, *outs))
    inner = len(args) - 1 - anywhere
    return pl.pallas_call(
        kernel,
        out_shape=outs,
        in_specs=[pl.BlockSpec(memory_space=pltpu.SMEM)]
        + [pl.BlockSpec(memory_space=pltpu.VMEM)] * inner
        + [pl.BlockSpec(memory_space=pl.ANY)] * anywhere,
        out_specs=[pl.BlockSpec(memory_space=spaces or pltpu.VMEM)] * len(outs),
        scratch_shapes=scratch,
        compiler_params=pltpu.CompilerParams(vmem_limit_bytes=20 * 2**20),
        cost_estimate=pl.CostEstimate(flops=flops, bytes_accessed=moved, transcendentals=0),
    )(*args)


def started(sems, *pairs):
    copies = [pltpu.make_async_copy(a, b, sems.at[n]) for n, (a, b) in enumerate(pairs)]
    for copy in copies:
        copy.start()
    return copies


def terms_in_rows(vec):
    row = lax.broadcasted_iota(jnp.int32, (16, vec.shape[1]), 0)
    terms = jnp.zeros(row.shape, jnp.float32)
    for n, term in enumerate(exact_terms(vec)):
        terms = jnp.where(row == n, term.astype(jnp.float32), terms)
    return terms.astype(jnp.bfloat16)


def to_rows(terms):
    ones = jnp.ones((terms.shape[0], 128), jnp.bfloat16)
    return lax.dot_general(
        terms, ones, (((0,), (0,)), ((), ())), preferred_element_type=jnp.float32
    )


def lane_sums(values):
    ones = jnp.ones((16, 128), jnp.bfloat16)
    return sum(cross(ones, term) for term in exact_terms(values))[:1]


def first_lanes(values):
    lane = lax.broadcasted_iota(jnp.int32, (16, 128), 1)
    pick = jnp.where(lane == 0, 1.0, 0.0).astype(jnp.bfloat16)
    return sum(cross(pick, term) for term in exact_terms(values))[:1]


def log_sum_exp(values):
    top = functools.reduce(jnp.maximum, values)
    return top + jnp.log(sum(jnp.exp(v - top) for v in values))


def stack_kernel(at, *refs):
    *blocks, out, sems = refs
    copies = started(sems, *((block, out.at[n]) for n, block in enumerate(blocks)))
    for copy in copies:
        copy.wait()


def halves_kernel(at, next_, last, low, high, sems):
    for copy in started(sems, (next_.at[:2], low), (last.at[2:], high)):
        copy.wait()


def near_place(at, k, r):
    return lax.rem(at[0] + k - 2 * at[4] + 4, 4), lax.rem(at[1] + r, 4)


def far_place(at, k, r):
    return lax.rem(at[0] + r - 2 * at[4] + 4, 4), lax.rem(at[1] + k, 4)


def first_kernel(at, *refs):
    data, noises, (out, x, held, sems) = refs[:4], refs[4:10], refs[10:]
    rows = data[0].shape[0]
    own, other = (pl.ds(pl.multiple_of(r * rows, rows), rows) for r in (at[2], 1 - at[2]))
    places = x.at[0, own], x.at[0, other], x.at[1, own], x.at[1, other]
    copies = started(
        sems, *zip(data, places), *((noise, held.at[n]) for n, noise in enumerate(noises))
    )
    for copy in copies[:4]:
        copy.wait()
    for n, k in enumerate((0, 1, 3)):
        copies[4 + n].wait()
        for r in (0, 2):
            noise = flat(held[n, r : r + 2])
            value = cross(x[0], noise) - half_squares(noise)
            out[near_place(at, k, r)] = value[:, :128]
            out[near_place(at, k, r + 1)] = value[:, 128:]
    x_sq = 0.0
    for side in range(2):
        for span in range(0, x.shape[2], 128):
            wide = x[side, :, span : span + 128].astype(jnp.float32)
            x_sq = x_sq + wide * wide
    x_sq = jnp.broadcast_to(0.5 * jnp.sum(x_sq, axis=1, keepdims=True), x_sq.shape)
    for r in range(4):
        out[near_place(at, 2, r)] = -x_sq
    for n, k in enumerate((0, 1, 3)):
        copies[7 + n].wait()
        for r in (0, 2):
            noise = flat(held[3 + n, r : r + 2])
            value = cross(x[1], noise) - half_squares(noise)
            out[far_place(at, k, r)] += value[:, :128]
            out[far_place(at, k, r + 1)] += value[:, 128:]
    for n, k in enumerate((0, 1, 3)):
        for r in range(4):
            out[near_place(at, k, r)] -= x_sq


def second_kernel(half, at, x, acc, n_a, n_b, out, held, sems):
    copies = started(sems, *((p, held.at[n]) for n, p in enumerate((n_a, n_b))))
    for block in range(2):
        for j in range(4):
            out[block, j] = acc[2 * half + block, j]
    for copy in copies:
        copy.wait()
    block, _ = near_place(at, 2, 0)

    @pl.when((block >= 2) == bool(half))
    def _():
        for n, r in ((0, 0), (1, 2)):
            noise = flat(held[n])
            value = cross(x[0], noise) - half_squares(noise)
            out[block - 2 * half, near_place(at, 2, r)[1]] += value[:, :128]
            out[block - 2 * half, near_place(at, 2, r + 1)[1]] += value[:, 128:]


def third_kernel(at, x, f_a, f_b, keep, give, held, sems):
    copies = started(sems, *((p, held.at[n]) for n, p in enumerate((f_a, f_b))))
    for n, copy in enumerate(copies):
        copy.wait()
        noise = flat(held[n])
        value = cross(x[1], noise) - half_squares(noise)
        for side in range(2):
            block, _ = far_place(at, 2, 2 * n + side)
            part = value[:, 128 * side : 128 * side + 128]

            @pl.when(block < 2)
            def _():
                keep[block] = part

            @pl.when(block >= 2)
            def _():
                give[block - 2] = part


def weights_of(at, weights, place, own_rows):
    rows = weights.shape[2] // 2
    to_l = at[2] if own_rows else 1 - at[2]
    here = pl.ds(pl.multiple_of(to_l * rows, rows), rows)
    parts = []
    for k, rs in ((0, range(4)), (1, range(4)), (3, range(4)), (2, (0, 1)), (2, (2, 3))):
        blocks = [place(at, k, r) for r in rs]
        parts.append(
            jnp.concatenate([weights[block[0], block[1], here] for block in blocks], axis=1)
        )
    total = 0.0
    for value in parts:
        total = total + cross(jnp.ones((16, value.shape[1]), jnp.bfloat16), value)
    return parts, total[:1]


STEP = 256


def product(parts, noise, first):
    span = slice(first, first + STEP)
    return sum(dot(w, flat(p[:, :, span])) for w, p in zip(parts, noise))


def target_1_kernel(
    least, at, came, plan, other, row_scale, p0, p1, p3, p2_a, p2_b, weights, low, high
):
    c = at[4]
    mine = sum(came[2 * n + c] for n in range(came.shape[0] // 2))
    theirs = sum(came[2 * n + 1 - c] for n in range(came.shape[0] // 2))
    for half, (values, total) in enumerate(((plan, mine), (other, theirs))):
        scale = 1.0 / jnp.maximum(total, least)
        for b in range(values.shape[0]):
            value = values[b] * row_scale[...] * scale[b : b + 1]
            weights[2 * half + b // 4, b % 4] = value.astype(weights.dtype)
    parts, total = weights_of(at, weights, far_place, True)
    mid = low.shape[0] - 16
    for first in range(0, p0.shape[-1], STEP):
        value = product(parts, (p0, p1, p3, p2_a, p2_b), first)
        low[:mid, first : first + STEP] = value[:mid].astype(low.dtype)
        high[:mid, first : first + STEP] = value[mid:].astype(high.dtype)
    for n, out in enumerate((low, high)):
        out[mid:, :] = jnp.zeros((16, out.shape[1]), out.dtype)
        out[mid:, :mid] = terms_in_rows(total[:, n * mid : n * mid + mid])


def target_2_kernel(
    place, half, at, weights, p0, p1, p3, p2_a, p2_b, message, values, row_total
):
    parts, total = weights_of(at, weights, place, False)
    mid = values.shape[0]
    kept, sent = (slice(n * mid, n * mid + mid) for n in (half, 1 - half))
    for first in range(0, p0.shape[-1], STEP):
        value = product(parts, (p0, p1, p3, p2_a, p2_b), first)
        message[:, first : first + STEP] = value[sent].astype(message.dtype)
        values[:, first : first + STEP] = value[kept]
    row_total[...] = jnp.broadcast_to(total, row_total.shape)


def target_3_kernel(at, weights, p0, p1, p3, p2_a, p2_b, values, row_total):
    parts, total = weights_of(at, weights, near_place, True)
    for first in range(0, p0.shape[-1], STEP):
        values[:, first : first + STEP] = product(parts, (p0, p1, p3, p2_a, p2_b), first)
    row_total[...] = jnp.broadcast_to(total, row_total.shape)


def add_kernel(half, at, values, row_total, came, out):
    mid = values.shape[0]
    out[:mid, :] = (values[...] + came[:mid].astype(jnp.float32)).astype(out.dtype)
    terms = came[mid:, :mid].astype(jnp.float32)
    total = [row_total[:1, :mid], row_total[:1, mid:]]
    total[half] = total[half] + terms[0:1] + terms[1:2] + terms[2:3]
    out[mid:, :] = jnp.zeros((16, out.shape[1]), out.dtype)
    out[mid:, : 2 * mid] = terms_in_rows(jnp.concatenate(total, axis=1))


def early_kernel(at, own, low, high, out):
    mid = low.shape[0]
    out[:mid, :] = own[:mid] + low[...].astype(jnp.float32)
    out[mid:, :] = own[mid:] + high[...].astype(jnp.float32)


def last_kernel(at, sums, own_total, low, high, out):
    mid = sums.shape[0] // 2
    terms = [m[mid:, : 2 * mid] for m in (low, high)]
    total = 1.0 / to_rows(jnp.concatenate([terms_in_rows(own_total[:1])] + terms, axis=0))
    for n, message in enumerate((low, high)):
        here = slice(n * mid, n * mid + mid)
        for column in range(0, sums.shape[1], 128):
            span = slice(column, column + 128)
            value = sums[here, span] + message[:mid, span].astype(jnp.float32)
            out[here, span] = (value * total[here]).astype(out.dtype)


TILE = 64


def rows_1_kernel(scale, at, keep, got, far_keep, far_got, score, sent, tops, sums):
    late = lax.rem(at[1] + 2, 4)
    scales = [jnp.where(late == j, scale, 0.0) for j in range(4)]
    blocks = range(keep.shape[0])

    @pl.loop(0, keep.shape[1] // TILE)
    def _(t):
        here = pl.ds(pl.multiple_of(t * TILE, TILE), TILE)
        far = [far_keep[b, here] + far_got[b, here] for b in range(2)]
        top = None
        for b in blocks:
            value = (keep[b, here] + got[b, here]) * scale + far[b // 4] * scales[b % 4]
            score[b, here] = value
            top = value if top is None else jnp.maximum(top, value)
        tops[here] = top

    tops[...] = jnp.broadcast_to(jnp.max(tops[...], axis=1, keepdims=True), tops.shape)

    @pl.loop(0, keep.shape[1] // TILE)
    def _(t):
        here = pl.ds(pl.multiple_of(t * TILE, TILE), TILE)
        top = tops[here]
        sums[here] = sum(jnp.exp(score[b, here] - top) for b in blocks)

    log_row = first_lanes(tops[...]) + jnp.log(lane_sums(sums[...]))
    for n in range(sent.shape[0]):
        sent[n] = log_row


def columns_1_kernel(log_count, at, came, score, row_pot, sent):
    pot = -log_count - log_sum_exp([came[n] for n in range(came.shape[0])])
    row_pot[...] = to_rows(terms_in_rows(pot))
    logs = []
    for b in range(score.shape[0]):
        value = score[b] + row_pot[...]
        top = jnp.max(value, axis=0, keepdims=True)
        total = jnp.sum(jnp.exp(value - top), axis=0, keepdims=True)
        logs.append(top + jnp.log(total))
    logs = jnp.concatenate(logs)
    for n in range(sent.shape[0]):
        sent[n] = logs


def rows_2_kernel(at, came, score, row_pot, plan, sent, sums):
    pot = -log_sum_exp([came[n] for n in range(came.shape[0])])

    @pl.loop(0, score.shape[1] // TILE)
    def _(t):
        here = pl.ds(pl.multiple_of(t * TILE, TILE), TILE)
        total = 0.0
        for b in range(score.shape[0]):
            value = score[b, here] + row_pot[here] + pot[b : b + 1]
            value = jnp.exp(jnp.minimum(value, 0.0))
            plan[b, here] = value
            total = total + value
        sums[here] = total

    row_sum = lane_sums(sums[...])
    for n in range(sent.shape[0]):
        sent[n] = row_sum


def columns_2_kernel(least, at, came, plan, row_scale, sent):
    total = sum(came[n] for n in range(came.shape[0]))
    row_scale[...] = to_rows(terms_in_rows(1.0 / jnp.maximum(total, least)))
    sums = []
    for b in range(plan.shape[0]):
        sums.append(jnp.sum(plan[b] * row_scale[...], axis=0, keepdims=True))
    sums = jnp.concatenate(sums)
    for n in range(sent.shape[0]):
        sent[n] = sums


def per_device(data_rows, noise_rows):
    z, y, l, h, c = (lax.axis_index(name) for name in AXES)
    rows, part = data_rows.shape
    width = part * 4
    count = rows * 32
    eps = 0.64 / math.sqrt(width)
    log_count = math.log(count)
    piece = rows // 4

    def float32(*shape):
        return jax.ShapeDtypeStruct(shape, jnp.float32)

    def bfloat16(*shape):
        return jax.ShapeDtypeStruct(shape, jnp.bfloat16)

    at = jnp.stack([z, y, l, h, c])

    wave = lax.optimization_barrier
    mid = rows // 2
    near = lax.dynamic_slice_in_dim(noise_rows, h * mid, mid)
    far = flip(lax.dynamic_slice_in_dim(noise_rows, (1 - h) * mid, mid), "h")
    near_1, near_3 = from_y(near, 1), from_y(near, 3)
    far, data_rows = wave((far, data_rows))
    data_l, data_lh = flip(data_rows, "l"), flip(data_rows, "lh")
    near_2 = from_y(near_1, 1)
    near_3, far_1, far_3 = wave((near_3, from_z(far, 1), from_z(far, 3)))
    far_2, data_l, data_lh, data_rows = wave((from_z(far_1, 1), data_l, data_lh, data_rows))
    sems = pltpu.SemaphoreType.DMA((4,))

    def stacked(*blocks):
        out = [bfloat16(4, *blocks[0].shape)]
        return call(
            stack_kernel, out, 0, at, *blocks, anywhere=4, spaces=pl.ANY, scratch=[sems]
        )[0]

    def halves(next_, last):
        out = [bfloat16(2, *next_.shape[1:])] * 2
        return call(
            halves_kernel, out, 0, at, next_, last, anywhere=2, spaces=pl.ANY, scratch=[sems]
        )

    near, far = stacked(near, near_1, near_2, near_3), stacked(far, far_1, far_2, far_3)
    near_next, near_last = from_z(near, 1), from_z(near, 3)
    far_next, far_last = from_y(far, 1), from_y(far, 3)
    data_h = flip(data_rows, "h")
    far_next, far_last, data_h = wave((far_next, far_last, data_h))
    nears, fars = (near, near_next, near_last), (far, far_next, far_last)
    low, high = halves(near_next, near_last)
    near_two = from_z(low, 1), from_z(high, 3)
    low, high = halves(far_next, far_last)
    far_two = from_y(low, 1), from_y(high, 3)

    one = 2 * 2 * rows * part * 2 * 2 * piece
    noise_shape = 4, 2 * piece, part
    scores, x_all = call(
        first_kernel,
        [float32(4, 4, 2 * rows, 2 * piece), bfloat16(2, 2 * rows, part)],
        12 * one,
        *(at, data_rows, data_l, data_h, data_lh, *nears, *fars),
        anywhere=10,
        scratch=[pltpu.VMEM((6, *noise_shape), jnp.bfloat16), pltpu.SemaphoreType.DMA((10,))],
    )
    give, keep = (
        call(
            functools.partial(second_kernel, half),
            [float32(2, 4, 2 * rows, 2 * piece)],
            100 * one,
            *(at, x_all, scores, *near_two),
            anywhere=2,
            scratch=[pltpu.VMEM((2, 2, *noise_shape[1:]), jnp.bfloat16), sems],
        )[0]
        for half in (1, 0)
    )
    far_keep, far_give = call(
        third_kernel,
        [float32(2, 2 * rows, 2 * piece)] * 2,
        2 * one,
        *(at, x_all, *far_two),
        anywhere=2,
        scratch=[pltpu.VMEM((2, 2, *noise_shape[1:]), jnp.bfloat16), sems],
    )

    blocks = (8, 2 * rows, 2 * piece)
    tall = 2 * rows, 2 * piece
    least = 0.5 / count
    row_axes, col_axes = ("l", "h", "c"), ("z", "y")
    row_sent, col_sent = float32(8, 1, 2 * rows), float32(16, 8, 2 * piece)

    def exchange(sent, axes):
        return lax.all_to_all(sent, axes, 0, 0, tiled=True)

    keep, give = keep.reshape(blocks), give.reshape(blocks)
    kernel = functools.partial(rows_1_kernel, 2.0 / (width * eps))
    score, sent = call(
        kernel,
        [float32(*blocks), row_sent],
        0,
        *(at, keep, flip(give, "c"), far_keep, flip(far_give, "c")),
        scratch=[pltpu.VMEM(tall, jnp.float32)] * 2,
    )
    kernel = functools.partial(columns_1_kernel, log_count)
    row_pot, sent = call(
        kernel, [float32(*tall), col_sent], 0, at, exchange(sent, row_axes), score
    )
    plan, sent = call(
        rows_2_kernel,
        [float32(*blocks), row_sent],
        0,
        *(at, exchange(sent, col_axes), score, row_pot),
        scratch=[pltpu.VMEM(tall, jnp.float32)],
    )
    plan_other = flip(plan, "c")
    kernel = functools.partial(columns_2_kernel, least)
    col_sent = float32(32, 8, 2 * piece)
    row_scale, sent = call(
        kernel, [float32(*tall), col_sent], 0, at, exchange(sent, row_axes), plan
    )
    near_noise, far_noise = (*nears, *near_two), (*fars, *far_two)
    message = bfloat16(mid + 16, part)
    weights, low, high = call(
        functools.partial(target_1_kernel, least),
        [bfloat16(4, 4, *blocks[1:]), message, message],
        8 * one,
        *(at, exchange(sent, ("z", "y", "c")), plan, plan_other, row_scale, *far_noise),
    )
    low, high = flip(low, "l"), flip(high, "lh")

    def other_rows(place, half, came, names):
        noise = near_noise if place is near_place else far_noise
        kernel = functools.partial(target_2_kernel, place, half)
        outs = [bfloat16(mid, part), float32(mid, part), float32(8, rows)]
        sent, *kept = call(kernel, outs, 8 * one, at, weights, *noise)
        added = call(functools.partial(add_kernel, half), [message], 0, at, *kept, came)[0]
        return flip(sent, names), flip(added, names)

    lh_high, lh_low = other_rows(far_place, 0, low, "lh")
    l_low, l_high = other_rows(near_place, 1, high, "l")
    own, own_total = call(
        target_3_kernel,
        [float32(rows, part), float32(8, rows)],
        64 * one,
        *(at, weights, *near_noise),
    )
    (sums,) = call(early_kernel, [float32(rows, part)], 0, at, own, l_low, lh_high)
    return call(last_kernel, [bfloat16(rows, part)], 0, at, sums, own_total, lh_low, l_high)[0]


def solution(mesh):
    fine = Mesh(mesh.devices.reshape(SIZES), AXES)
    spec = P(("z", "y", "l"), ("h", "c"))
    return jax.shard_map(
        per_device, mesh=fine, in_specs=(spec, spec), out_specs=spec, check_vma=False
    )
```

```python
import functools
import itertools
import math

import jax
import jax.numpy as jnp
from jax import lax
from jax.experimental import pallas as pl
from jax.experimental.pallas import tpu as pltpu
from jax.sharding import Mesh, PartitionSpec as P

AXES = ("z", "y", "l", "h", "c")
SIZES = (4, 4, 2, 2, 2)


def index_of(*place):
    index = 0
    for n, a in zip(SIZES, place):
        index = index * n + a % n
    return index


def move(value, dest):
    places = itertools.product(*(range(n) for n in SIZES))
    pairs = [(index_of(*place), index_of(*dest(*place))) for place in places]
    return lax.ppermute(value, AXES, pairs)


def from_y(value, k):
    return move(value, lambda z, y, l, h, c: (z, y - k, l, h, c))


def from_z(value, k):
    return move(value, lambda z, y, l, h, c: (z - k, y, l, h, c))


def flip(value, names):
    return move(
        value,
        lambda *place: [1 - a if name in names else a for name, a in zip(AXES, place)],
    )


def cross(a, b):
    return lax.dot_general(a, b, (((1,), (1,)), ((), ())), preferred_element_type=jnp.float32)


def dot(a, b):
    return jnp.dot(a, b, preferred_element_type=jnp.float32)


def exact_terms(total):
    terms = []
    for _ in range(3):
        terms.append(total.astype(jnp.bfloat16))
        total = total - terms[-1].astype(jnp.float32)
    return terms


def flat(blocks):
    return blocks.reshape(-1, blocks.shape[-1])


def half_squares(rows):
    sums = 0.0
    for at in range(0, rows.shape[1], 128):
        wide = rows[:, at : at + 128].astype(jnp.float32)
        sums = sums + wide * wide
    ones = jnp.full((16, 128), 0.5, jnp.bfloat16)
    return sum(cross(ones, term) for term in exact_terms(sums))[:1]


def call(kernel, outs, flops, *args, anywhere=0, spaces=None, scratch=()):
    moved = sum(a.size * a.dtype.itemsize for a in (*args, *outs))
    inner = len(args) - 1 - anywhere
    return pl.pallas_call(
        kernel,
        out_shape=outs,
        in_specs=[pl.BlockSpec(memory_space=pltpu.SMEM)]
        + [pl.BlockSpec(memory_space=pltpu.VMEM)] * inner
        + [pl.BlockSpec(memory_space=pl.ANY)] * anywhere,
        out_specs=[pl.BlockSpec(memory_space=spaces or pltpu.VMEM)] * len(outs),
        scratch_shapes=scratch,
        compiler_params=pltpu.CompilerParams(vmem_limit_bytes=20 * 2**20),
        cost_estimate=pl.CostEstimate(flops=flops, bytes_accessed=moved, transcendentals=0),
    )(*args)


def started(sems, *pairs):
    copies = [pltpu.make_async_copy(a, b, sems.at[n]) for n, (a, b) in enumerate(pairs)]
    for copy in copies:
        copy.start()
    return copies


def terms_in_rows(vec):
    row = lax.broadcasted_iota(jnp.int32, (16, vec.shape[1]), 0)
    terms = jnp.zeros(row.shape, jnp.float32)
    for n, term in enumerate(exact_terms(vec)):
        terms = jnp.where(row == n, term.astype(jnp.float32), terms)
    return terms.astype(jnp.bfloat16)


def to_rows(terms):
    ones = jnp.ones((terms.shape[0], 128), jnp.bfloat16)
    return lax.dot_general(
        terms, ones, (((0,), (0,)), ((), ())), preferred_element_type=jnp.float32
    )


def lane_sums(values):
    ones = jnp.ones((16, 128), jnp.bfloat16)
    return sum(cross(ones, term) for term in exact_terms(values))[:1]


def first_lanes(values):
    lane = lax.broadcasted_iota(jnp.int32, (16, 128), 1)
    pick = jnp.where(lane == 0, 1.0, 0.0).astype(jnp.bfloat16)
    return sum(cross(pick, term) for term in exact_terms(values))[:1]


def log_sum_exp(values):
    top = functools.reduce(jnp.maximum, values)
    return top + jnp.log(sum(jnp.exp(v - top) for v in values))


def stack_kernel(at, *refs):
    *blocks, out, sems = refs
    copies = started(sems, *((block, out.at[n]) for n, block in enumerate(blocks)))
    for copy in copies:
        copy.wait()


def halves_kernel(at, next_, last, low, high, sems):
    for copy in started(sems, (next_.at[:2], low), (last.at[2:], high)):
        copy.wait()


def near_place(at, k, r):
    return lax.rem(at[0] + k - 2 * at[4] + 4, 4), lax.rem(at[1] + r, 4)


def far_place(at, k, r):
    return lax.rem(at[0] + r - 2 * at[4] + 4, 4), lax.rem(at[1] + k, 4)


def first_kernel(at, *refs):
    data, noises, (out, x, held, sems) = refs[:4], refs[4:10], refs[10:]
    rows = data[0].shape[0]
    own, other = (pl.ds(pl.multiple_of(r * rows, rows), rows) for r in (at[2], 1 - at[2]))
    places = x.at[0, own], x.at[0, other], x.at[1, own], x.at[1, other]
    copies = started(
        sems, *zip(data, places), *((noise, held.at[n]) for n, noise in enumerate(noises))
    )
    for copy in copies[:4]:
        copy.wait()
    for n, k in enumerate((0, 1, 3)):
        copies[4 + n].wait()
        for r in (0, 2):
            noise = flat(held[n, r : r + 2])
            value = cross(x[0], noise) - half_squares(noise)
            out[near_place(at, k, r)] = value[:, :128]
            out[near_place(at, k, r + 1)] = value[:, 128:]
    x_sq = 0.0
    for side in range(2):
        for span in range(0, x.shape[2], 128):
            wide = x[side, :, span : span + 128].astype(jnp.float32)
            x_sq = x_sq + wide * wide
    x_sq = jnp.broadcast_to(0.5 * jnp.sum(x_sq, axis=1, keepdims=True), x_sq.shape)
    for r in range(4):
        out[near_place(at, 2, r)] = -x_sq
    for n, k in enumerate((0, 1, 3)):
        copies[7 + n].wait()
        for r in (0, 2):
            noise = flat(held[3 + n, r : r + 2])
            value = cross(x[1], noise) - half_squares(noise)
            out[far_place(at, k, r)] += value[:, :128]
            out[far_place(at, k, r + 1)] += value[:, 128:]
    for n, k in enumerate((0, 1, 3)):
        for r in range(4):
            out[near_place(at, k, r)] -= x_sq


def second_kernel(half, at, x, acc, n_a, n_b, out, held, sems):
    copies = started(sems, *((p, held.at[n]) for n, p in enumerate((n_a, n_b))))
    for block in range(2):
        for j in range(4):
            out[block, j] = acc[2 * half + block, j]
    for copy in copies:
        copy.wait()
    block, _ = near_place(at, 2, 0)

    @pl.when((block >= 2) == bool(half))
    def _():
        for n, r in ((0, 0), (1, 2)):
            noise = flat(held[n])
            value = cross(x[0], noise) - half_squares(noise)
            out[block - 2 * half, near_place(at, 2, r)[1]] += value[:, :128]
            out[block - 2 * half, near_place(at, 2, r + 1)[1]] += value[:, 128:]


def third_kernel(at, x, f_a, f_b, keep, give, held, sems):
    copies = started(sems, *((p, held.at[n]) for n, p in enumerate((f_a, f_b))))
    for n, copy in enumerate(copies):
        copy.wait()
        noise = flat(held[n])
        value = cross(x[1], noise) - half_squares(noise)
        for side in range(2):
            block, _ = far_place(at, 2, 2 * n + side)
            part = value[:, 128 * side : 128 * side + 128]

            @pl.when(block < 2)
            def _():
                keep[block] = part

            @pl.when(block >= 2)
            def _():
                give[block - 2] = part


def weights_of(at, weights, place, own_rows):
    rows = weights.shape[2] // 2
    to_l = at[2] if own_rows else 1 - at[2]
    here = pl.ds(pl.multiple_of(to_l * rows, rows), rows)
    parts = []
    for k, rs in ((0, range(4)), (1, range(4)), (3, range(4)), (2, (0, 1)), (2, (2, 3))):
        blocks = [place(at, k, r) for r in rs]
        parts.append(
            jnp.concatenate([weights[block[0], block[1], here] for block in blocks], axis=1)
        )
    total = 0.0
    for value in parts:
        total = total + cross(jnp.ones((16, value.shape[1]), jnp.bfloat16), value)
    return parts, total[:1]


STEP = 256


def product(parts, noise, first):
    span = slice(first, first + STEP)
    return sum(dot(w, flat(p[:, :, span])) for w, p in zip(parts, noise))


def target_1_kernel(
    least, at, came, plan, other, row_scale, p0, p1, p3, p2_a, p2_b, weights, low, high
):
    c = at[4]
    mine = sum(came[2 * n + c] for n in range(came.shape[0] // 2))
    theirs = sum(came[2 * n + 1 - c] for n in range(came.shape[0] // 2))
    for half, (values, total) in enumerate(((plan, mine), (other, theirs))):
        scale = 1.0 / jnp.maximum(total, least)
        for b in range(values.shape[0]):
            value = values[b] * row_scale[...] * scale[b : b + 1]
            weights[2 * half + b // 4, b % 4] = value.astype(weights.dtype)
    parts, total = weights_of(at, weights, far_place, True)
    mid = low.shape[0] - 16
    for first in range(0, p0.shape[-1], STEP):
        value = product(parts, (p0, p1, p3, p2_a, p2_b), first)
        low[:mid, first : first + STEP] = value[:mid].astype(low.dtype)
        high[:mid, first : first + STEP] = value[mid:].astype(high.dtype)
    for n, out in enumerate((low, high)):
        out[mid:, :] = jnp.zeros((16, out.shape[1]), out.dtype)
        out[mid:, :mid] = terms_in_rows(total[:, n * mid : n * mid + mid])


def target_2_kernel(
    place, half, at, weights, p0, p1, p3, p2_a, p2_b, message, values, row_total
):
    parts, total = weights_of(at, weights, place, False)
    mid = values.shape[0]
    kept, sent = (slice(n * mid, n * mid + mid) for n in (half, 1 - half))
    for first in range(0, p0.shape[-1], STEP):
        value = product(parts, (p0, p1, p3, p2_a, p2_b), first)
        message[:, first : first + STEP] = value[sent].astype(message.dtype)
        values[:, first : first + STEP] = value[kept]
    row_total[...] = jnp.broadcast_to(total, row_total.shape)


def target_3_kernel(at, weights, p0, p1, p3, p2_a, p2_b, values, row_total):
    parts, total = weights_of(at, weights, near_place, True)
    for first in range(0, p0.shape[-1], STEP):
        values[:, first : first + STEP] = product(parts, (p0, p1, p3, p2_a, p2_b), first)
    row_total[...] = jnp.broadcast_to(total, row_total.shape)


def add_kernel(half, at, values, row_total, came, out):
    mid = values.shape[0]
    out[:mid, :] = (values[...] + came[:mid].astype(jnp.float32)).astype(out.dtype)
    terms = came[mid:, :mid].astype(jnp.float32)
    total = [row_total[:1, :mid], row_total[:1, mid:]]
    total[half] = total[half] + terms[0:1] + terms[1:2] + terms[2:3]
    out[mid:, :] = jnp.zeros((16, out.shape[1]), out.dtype)
    out[mid:, : 2 * mid] = terms_in_rows(jnp.concatenate(total, axis=1))


def last_kernel(at, own, own_total, l_low, l_high, lh_low, lh_high, out):
    mid = own.shape[0] // 2
    terms = [m[mid:, : 2 * mid] for m in (l_high, lh_low)]
    total = 1.0 / to_rows(jnp.concatenate([terms_in_rows(own_total[:1])] + terms, axis=0))
    for n, messages in enumerate(((l_low, lh_low), (l_high, lh_high))):
        here = slice(n * mid, n * mid + mid)
        for column in range(0, own.shape[1], 128):
            span = slice(column, column + 128)
            value = own[here, span]
            for m in messages:
                value = value + m[:mid, span].astype(jnp.float32)
            out[here, span] = (value * total[here]).astype(out.dtype)


TILE = 128


def rows_1_kernel(scale, at, keep, got, far_keep, far_got, score, sent, tops, sums):
    late = lax.rem(at[1] + 2, 4)
    scales = [jnp.where(late == j, scale, 0.0) for j in range(4)]
    blocks = range(keep.shape[0])

    @pl.loop(0, keep.shape[1] // TILE)
    def _(t):
        here = pl.ds(pl.multiple_of(t * TILE, TILE), TILE)
        far = [far_keep[b, here] + far_got[b, here] for b in range(2)]
        top = None
        for b in blocks:
            value = (keep[b, here] + got[b, here]) * scale + far[b // 4] * scales[b % 4]
            score[b, here] = value
            top = value if top is None else jnp.maximum(top, value)
        tops[here] = top

    tops[...] = jnp.broadcast_to(jnp.max(tops[...], axis=1, keepdims=True), tops.shape)

    @pl.loop(0, keep.shape[1] // TILE)
    def _(t):
        here = pl.ds(pl.multiple_of(t * TILE, TILE), TILE)
        top = tops[here]
        sums[here] = sum(jnp.exp(score[b, here] - top) for b in blocks)

    log_row = first_lanes(tops[...]) + jnp.log(lane_sums(sums[...]))
    for n in range(sent.shape[0]):
        sent[n] = log_row


def columns_1_kernel(log_count, at, came, score, row_pot, sent):
    pot = -log_count - log_sum_exp([came[n] for n in range(came.shape[0])])
    row_pot[...] = to_rows(terms_in_rows(pot))
    logs = []
    for b in range(score.shape[0]):
        value = score[b] + row_pot[...]
        top = jnp.max(value, axis=0, keepdims=True)
        total = jnp.sum(jnp.exp(value - top), axis=0, keepdims=True)
        logs.append(top + jnp.log(total))
    logs = jnp.concatenate(logs)
    for n in range(sent.shape[0]):
        sent[n] = logs


def rows_2_kernel(at, came, score, row_pot, plan, sent, sums):
    pot = -log_sum_exp([came[n] for n in range(came.shape[0])])

    @pl.loop(0, score.shape[1] // TILE)
    def _(t):
        here = pl.ds(pl.multiple_of(t * TILE, TILE), TILE)
        total = 0.0
        for b in range(score.shape[0]):
            value = score[b, here] + row_pot[here] + pot[b : b + 1]
            value = jnp.exp(jnp.minimum(value, 0.0))
            plan[b, here] = value
            total = total + value
        sums[here] = total

    row_sum = lane_sums(sums[...])
    for n in range(sent.shape[0]):
        sent[n] = row_sum


def columns_2_kernel(least, at, came, plan, row_scale, sent):
    total = sum(came[n] for n in range(came.shape[0]))
    row_scale[...] = to_rows(terms_in_rows(1.0 / jnp.maximum(total, least)))
    sums = []
    for b in range(plan.shape[0]):
        sums.append(jnp.sum(plan[b] * row_scale[...], axis=0, keepdims=True))
    sums = jnp.concatenate(sums)
    for n in range(sent.shape[0]):
        sent[n] = sums


def per_device(data_rows, noise_rows):
    z, y, l, h, c = (lax.axis_index(name) for name in AXES)
    rows, part = data_rows.shape
    width = part * 4
    count = rows * 32
    eps = 0.64 / math.sqrt(width)
    log_count = math.log(count)
    piece = rows // 4

    def float32(*shape):
        return jax.ShapeDtypeStruct(shape, jnp.float32)

    def bfloat16(*shape):
        return jax.ShapeDtypeStruct(shape, jnp.bfloat16)

    at = jnp.stack([z, y, l, h, c])

    wave = lax.optimization_barrier
    mid = rows // 2
    near = lax.dynamic_slice_in_dim(noise_rows, h * mid, mid)
    far = flip(lax.dynamic_slice_in_dim(noise_rows, (1 - h) * mid, mid), "h")
    near_1, near_3 = from_y(near, 1), from_y(near, 3)
    far, data_rows = wave((far, data_rows))
    data_l, data_lh = flip(data_rows, "l"), flip(data_rows, "lh")
    near_2 = from_y(near_1, 1)
    near_3, far_1, far_3 = wave((near_3, from_z(far, 1), from_z(far, 3)))
    far_2, data_l, data_lh, data_rows = wave((from_z(far_1, 1), data_l, data_lh, data_rows))
    sems = pltpu.SemaphoreType.DMA((4,))

    def stacked(*blocks):
        out = [bfloat16(4, *blocks[0].shape)]
        return call(
            stack_kernel, out, 0, at, *blocks, anywhere=4, spaces=pl.ANY, scratch=[sems]
        )[0]

    def halves(next_, last):
        out = [bfloat16(2, *next_.shape[1:])] * 2
        return call(
            halves_kernel, out, 0, at, next_, last, anywhere=2, spaces=pl.ANY, scratch=[sems]
        )

    near, far = stacked(near, near_1, near_2, near_3), stacked(far, far_1, far_2, far_3)
    near_next, near_last = from_z(near, 1), from_z(near, 3)
    far_next, far_last = from_y(far, 1), from_y(far, 3)
    data_h = flip(data_rows, "h")
    far_next, far_last, data_h = wave((far_next, far_last, data_h))
    nears, fars = (near, near_next, near_last), (far, far_next, far_last)
    low, high = halves(near_next, near_last)
    near_two = from_z(low, 1), from_z(high, 3)
    low, high = halves(far_next, far_last)
    far_two = from_y(low, 1), from_y(high, 3)

    one = 2 * 2 * rows * part * 2 * 2 * piece
    noise_shape = 4, 2 * piece, part
    scores, x_all = call(
        first_kernel,
        [float32(4, 4, 2 * rows, 2 * piece), bfloat16(2, 2 * rows, part)],
        12 * one,
        *(at, data_rows, data_l, data_h, data_lh, *nears, *fars),
        anywhere=10,
        scratch=[pltpu.VMEM((6, *noise_shape), jnp.bfloat16), pltpu.SemaphoreType.DMA((10,))],
    )
    give, keep = (
        call(
            functools.partial(second_kernel, half),
            [float32(2, 4, 2 * rows, 2 * piece)],
            100 * one,
            *(at, x_all, scores, *near_two),
            anywhere=2,
            scratch=[pltpu.VMEM((2, 2, *noise_shape[1:]), jnp.bfloat16), sems],
        )[0]
        for half in (1, 0)
    )
    far_keep, far_give = call(
        third_kernel,
        [float32(2, 2 * rows, 2 * piece)] * 2,
        2 * one,
        *(at, x_all, *far_two),
        anywhere=2,
        scratch=[pltpu.VMEM((2, 2, *noise_shape[1:]), jnp.bfloat16), sems],
    )

    blocks = (8, 2 * rows, 2 * piece)
    tall = 2 * rows, 2 * piece
    least = 0.5 / count
    row_axes, col_axes = ("l", "h", "c"), ("z", "y")
    row_sent, col_sent = float32(8, 1, 2 * rows), float32(16, 8, 2 * piece)

    def exchange(sent, axes):
        return lax.all_to_all(sent, axes, 0, 0, tiled=True)

    keep, give = keep.reshape(blocks), give.reshape(blocks)
    kernel = functools.partial(rows_1_kernel, 2.0 / (width * eps))
    score, sent = call(
        kernel,
        [float32(*blocks), row_sent],
        0,
        *(at, keep, flip(give, "c"), far_keep, flip(far_give, "c")),
        scratch=[pltpu.VMEM(tall, jnp.float32)] * 2,
    )
    kernel = functools.partial(columns_1_kernel, log_count)
    row_pot, sent = call(
        kernel, [float32(*tall), col_sent], 0, at, exchange(sent, row_axes), score
    )
    plan, sent = call(
        rows_2_kernel,
        [float32(*blocks), row_sent],
        0,
        *(at, exchange(sent, col_axes), score, row_pot),
        scratch=[pltpu.VMEM(tall, jnp.float32)],
    )
    plan_other = flip(plan, "c")
    kernel = functools.partial(columns_2_kernel, least)
    col_sent = float32(32, 8, 2 * piece)
    row_scale, sent = call(
        kernel, [float32(*tall), col_sent], 0, at, exchange(sent, row_axes), plan
    )
    near_noise, far_noise = (*nears, *near_two), (*fars, *far_two)
    message = bfloat16(mid + 16, part)
    weights, low, high = call(
        functools.partial(target_1_kernel, least),
        [bfloat16(4, 4, *blocks[1:]), message, message],
        8 * one,
        *(at, exchange(sent, ("z", "y", "c")), plan, plan_other, row_scale, *far_noise),
    )
    low, high = flip(low, "l"), flip(high, "lh")

    def other_rows(place, half, came, names):
        noise = near_noise if place is near_place else far_noise
        kernel = functools.partial(target_2_kernel, place, half)
        outs = [bfloat16(mid, part), float32(mid, part), float32(8, rows)]
        sent, *kept = call(kernel, outs, 8 * one, at, weights, *noise)
        added = call(functools.partial(add_kernel, half), [message], 0, at, *kept, came)[0]
        return flip(sent, names), flip(added, names)

    lh_high, lh_low = other_rows(far_place, 0, low, "lh")
    l_low, l_high = other_rows(near_place, 1, high, "l")
    own = call(
        target_3_kernel,
        [float32(rows, part), float32(8, rows)],
        64 * one,
        *(at, weights, *near_noise),
    )
    messages = l_low, l_high, lh_low, lh_high
    return call(last_kernel, [bfloat16(rows, part)], 0, at, *own, *messages)[0]


def solution(mesh):
    fine = Mesh(mesh.devices.reshape(SIZES), AXES)
    spec = P(("z", "y", "l"), ("h", "c"))
    return jax.shard_map(
        per_device, mesh=fine, in_specs=(spec, spec), out_specs=spec, check_vma=False
    )
```
